32 devices in a mesh: dp: 4 (over z), fsdp: 8 (over y, x, core).
Axes of the slice: x: 2, y: 2, z: 4, core: 2. Of those that a mesh axis runs over, the one named last changes fastest.
Arguments:
- tokens: bfloat16 [32768, 768], P(('dp', 'fsdp')), may hold values from -6 to 6
- token_ids: int32 [32768], P(('dp', 'fsdp')), may hold values from 0 to 8007
- lengths: int32 [32], P(('dp', 'fsdp')), may hold values from 1 to 1024, 20480 in all
- hash_table: int32 [8008], replicated, may hold values from 0 to 3
- w_qkv: bfloat16 [768, 2304], P(('dp', 'fsdp')), may hold values from -0.21875 to 0.21875
- w_attn_out: bfloat16 [768, 768], P(('dp', 'fsdp')), may hold values from -1.75 to 1.75
- norm_gains: bfloat16 [768, 2], P(('dp', 'fsdp')), may hold values from 0.5 to 1.5
- norm_biases: bfloat16 [768, 2], P(('dp', 'fsdp')), may hold values from -1.5 to 1.5
- w_in: bfloat16 [3072, 3072], P(('dp', 'fsdp')), may hold values from -0.21875 to 0.21875
- w_out: bfloat16 [12288, 768], P(('dp', 'fsdp')), may hold values from -0.109375 to 0.109375
- cotangent: bfloat16 [32768, 768], P(('dp', 'fsdp')), may hold values from -6 to 6
Outputs:
- layer_out: bfloat16 [32768, 768], P(('dp', 'fsdp'))
- grad_tokens: float32 [32768, 768], P(('dp', 'fsdp'))
- grad_w_qkv: float32 [768, 2304], P(('dp', 'fsdp'))
- grad_w_attn_out: float32 [768, 768], P(('dp', 'fsdp'))
- grad_norm_gains: float32 [768, 2], P(('dp', 'fsdp'))
- grad_norm_biases: float32 [768, 2], P(('dp', 'fsdp'))
- grad_w_in: float32 [3072, 3072], P(('dp', 'fsdp'))
- grad_w_out: float32 [12288, 768], P(('dp', 'fsdp'))
- expert_counts: int32 [4], replicated
The draws below stay inside these ranges and needn't reach their ends.
Inputs may be any that keep to these rules, and one draw needn't show every extreme that they name: `lengths`: every sequence has at least one used token and one sequence of each draw uses all 1024 slots.
All inputs are finite; a program needn't handle non-finite values. No bound on the sum of `lengths` on one device may be relied on, other than what follows from the above.
Results may differ from the reference program's by a relative error of at most 0.0094.
Values may be sent and summed in bfloat16 or wider, within the bound.
A program may use at most 512 MiB of HBM per device.

```python
import math
import jax
import jax.numpy as jnp
import numpy as np
from jax import lax

D = 768
HEADS = 12
HEAD_DIM = 64
FF = 3072
VOCAB = 8008
EXPERTS = 4
LEN = 1024
SEQ_DEV = 1
TOK_DEV = 1024
SEQS = 32
TOKENS = 32768


def set_ends(values, stream_key, low, largest):
    place = [jax.random.randint(jax.random.fold_in(stream_key, axis), (), 0, length) for axis, length in enumerate(values.shape)]
    longest = values.shape.index(max(values.shape))
    neighbour = place[:longest] + [(place[longest] + 1) % values.shape[longest]] + place[longest + 1:]
    return values.at[tuple(place)].set(low).at[tuple(neighbour)].set(largest)


def level_of(stream_key, shape, split, low, top_value):
    def one(dim, parts):
        draws = jax.random.uniform(jax.random.fold_in(jax.random.fold_in(stream_key, 6), dim), (parts,), jnp.float32, low / len(split), top_value / len(split))
        return jnp.repeat(jnp.exp(draws), shape[dim] // parts).reshape((-1,) + (1,) * (len(shape) - dim - 1))

    loudness = one(*split[0])
    for cut in split[1:]:
        loudness = loudness * one(*cut)
    return loudness


def cumulative_ranks(number_of, lean):
    weights = [(1 << 20) // math.isqrt(grade ** lean) + 1 for grade in range(1, number_of + 1)]
    deviation = 1 + sum(weights) // (1 << 30)
    return np.cumsum(np.array([max(1, weight // deviation) for weight in weights]))


def skewed_ids(rng, extent, number_of, skew):
    listing = cumulative_ranks(number_of, skew)
    ticket = jax.random.randint(jax.random.fold_in(rng, 1), extent, 0, int(listing[number_of - 1]))
    grade = jnp.searchsorted(jnp.asarray(listing, jnp.int32), ticket, side="right")
    return jax.random.permutation(jax.random.fold_in(rng, 2), number_of)[grade].astype(jnp.int32)


def length_profile(count, total, reach, skew):
    portions = [(1 << 20) // math.isqrt(standing ** skew) + 1 for standing in range(2, count + 1)]
    rest, given = total - reach - (count - 1), [1] * (count - 1)
    while rest > 0:
        movable = [i for i in range(count - 1) if given[i] < reach]
        whole, left = sum([portions[i] for i in movable]), rest
        for i in movable:
            more = min(reach - given[i], max(1, left * portions[i] // whole), rest)
            given[i] = given[i] + more
            rest = rest - more
    return np.array([reach] + given)


def uneven_parts(key, amount, total, reach, slope):
    if amount == 2:
        one = jax.random.randint(key, (), max(1, total - reach), min(reach, total - 1) + 1)
        return jnp.stack([one, total - one])
    sizes = jnp.asarray(length_profile(amount, total, reach, slope), jnp.int32)
    pairs = (amount - 1) // 2
    giver, sink = sizes[1:1 + 2 * pairs:2], sizes[2:2 + 2 * pairs:2]
    room = jnp.minimum(giver - 1, reach - sink)
    moved = jax.random.randint(jax.random.fold_in(key, 1), (pairs,), 0, 1 << 20) % (room + 1)
    sizes = sizes.at[1:1 + 2 * pairs:2].set(giver - moved).at[2:2 + 2 * pairs:2].set(sink + moved)
    return sizes[jax.random.permutation(jax.random.fold_in(key, 2), amount)]


def noise(rng, extent, width, limit, cuts=(), held_as=jnp.bfloat16):
    gain = level_of(rng, extent, cuts, -0.22, 0.18) if cuts else 1.0
    values = jax.random.normal(rng, extent, jnp.float32) * width * gain
    return jnp.minimum(jnp.maximum(values, -limit), limit).astype(held_as)


def setup_inputs(seed: int = 0) -> dict:
    seeds = jax.random.split(jax.random.key(seed), 12)
    return {
        "tokens": noise(seeds[0], (TOKENS, D), 1.0, 6.0, ((0, 32),)),
        "token_ids": set_ends(skewed_ids(seeds[1], (TOKENS,), VOCAB, 2), jax.random.fold_in(seeds[1], 3), 0, VOCAB - 1).astype(jnp.int32),
        "lengths": uneven_parts(seeds[2], SEQS, SEQS * LEN * 5 // 8, LEN, 0).astype(jnp.int32),
        "hash_table": set_ends(jax.random.randint(seeds[3], (VOCAB,), 0, EXPERTS), jax.random.fold_in(seeds[3], 1), 0, EXPERTS - 1).astype(jnp.int32),
        "w_qkv": noise(seeds[4], (D, 3 * D), D ** -0.5, 0.21875, ((0, 32),)),
        "w_attn_out": noise(seeds[5], (D, D), (D // 64) ** -0.5, 1.75, ((0, 32),)),
        "norm_gains": jnp.clip(1.0 + 0.1 * jax.random.normal(seeds[6], (D, 2), jnp.float32), 0.5, 1.5).astype(jnp.bfloat16),
        "norm_biases": noise(seeds[7], (D, 2), 0.3, 1.5, ((0, 32),)),
        "w_in": noise(seeds[8], (EXPERTS * D, FF), D ** -0.5, 0.21875, ((0, 32),)),
        "w_out": noise(seeds[9], (EXPERTS * FF, D), FF ** -0.5, 0.109375, ((0, 32),)),
        "cotangent": noise(seeds[10], (TOKENS, D), 1.0, 6.0, ((0, 32),)),
    }


@jax.custom_vjp
def low(v):
    return lax.optimization_barrier(v.astype(jnp.bfloat16)).astype(jnp.float32)

@jax.custom_vjp
def low_back(v):
    return v

def low_keep(v):
    return (low(v), None)

def low_pass(kept, grad):
    return (grad,)

def back_keep(v):
    return (v, None)

def back_low(kept, grad):
    return (low(grad),)
low.defvjp(low_keep, low_pass)
low_back.defvjp(back_keep, back_low)
HIGH = lax.Precision.HIGHEST
EPSILON = 1e-05
NEGATIVE = -1e+30

def layer_norm(values, gain_col, bias_col):
    average = lax.optimization_barrier(jnp.mean(values, axis=-1, keepdims=True))
    centred = values - average
    spread = lax.optimization_barrier(jnp.mean(centred * centred, axis=-1, keepdims=True))
    return centred * lax.rsqrt(spread + EPSILON) * gain_col + bias_col

def attend_one(queries, keys, values, length):
    scores = jnp.einsum('qhd,khd->hqk', queries, keys, precision=HIGH) * HEAD_DIM ** (-0.5)
    scores = low_back(scores)
    places = jnp.arange(LEN, dtype=jnp.int32)
    allowed = (places[None, :] <= places[:, None]) & (places[None, :] < length)
    scores = jnp.where(allowed[None], scores, NEGATIVE)
    probs = low(jax.nn.softmax(scores, axis=-1))
    mixed = jnp.einsum('hqk,khd->qhd', probs, values, precision=HIGH)
    return low(low_back(mixed.reshape(LEN, D)))

def layer_block(rows_in, expert_ids, seq_lengths, w_qkv, w_attn_out, gains, biases, w_in, w_out):
    normed = low(layer_norm(rows_in, gains[:, 0], biases[:, 0]))
    qkv = low(low_back(jnp.dot(normed, w_qkv, precision=HIGH)))
    packed = qkv.reshape(SEQ_DEV, LEN, 3, HEADS, HEAD_DIM)
    mixed = jax.vmap(attend_one)(packed[:, :, 0], packed[:, :, 1], packed[:, :, 2], seq_lengths)
    mixed = mixed.reshape(TOK_DEV, D)
    branch = low_back(jnp.dot(mixed, w_attn_out, precision=HIGH))
    hidden = rows_in + branch
    normed_two = low(layer_norm(hidden, gains[:, 1], biases[:, 1]))
    ordering = jnp.argsort(expert_ids, stable=True).astype(jnp.int32)
    inverse = jnp.argsort(ordering).astype(jnp.int32)
    group_sizes = lax.optimization_barrier(jnp.sum((expert_ids[:, None] == jnp.arange(EXPERTS + 1, dtype=jnp.int32)[None, :]).astype(jnp.int32), axis=0)).astype(jnp.int32)
    inner = jnp.concatenate([w_in.reshape(EXPERTS, D, FF), jnp.zeros((1, D, FF), w_in.dtype)], axis=0)
    outer = jnp.concatenate([w_out.reshape(EXPERTS, FF, D), jnp.zeros((1, FF, D), w_out.dtype)], axis=0)
    pre = low_back(lax.ragged_dot(normed_two[ordering], inner, group_sizes, precision=HIGH))
    activated = low(jax.nn.gelu(pre))
    expert_out = low_back(lax.ragged_dot(activated, outer, group_sizes, precision=HIGH))
    return hidden + expert_out[inverse]

def reference(tokens, token_ids, lengths, hash_table, w_qkv, w_attn_out, norm_gains, norm_biases, w_in, w_out, cotangent):
    groups = TOKENS // TOK_DEV
    places = jnp.arange(TOKENS, dtype=jnp.int32) % LEN
    seq_of_slot = jnp.repeat(lengths, LEN, total_repeat_length=TOKENS)
    used = places < seq_of_slot
    expert_ids = jnp.where(used, hash_table[token_ids], EXPERTS).astype(jnp.int32)
    expert_counts = lax.optimization_barrier(jnp.sum((expert_ids[:, None] == jnp.arange(EXPERTS, dtype=jnp.int32)[None, :]).astype(jnp.int32), axis=0)).astype(jnp.int32)

    def forward(rows_all, wq, wo, gains, biases, wi, wu):

        def scan_step(running, pieces):
            rows_in, ids_here, lens_here = pieces
            return (running, jax.checkpoint(layer_block)(rows_in, ids_here, lens_here, wq, wo, gains, biases, wi, wu))
        _, stacked = lax.scan(scan_step, jnp.zeros((), jnp.float32), (rows_all.reshape(groups, TOK_DEV, D), expert_ids.reshape(groups, TOK_DEV), lengths.reshape(groups, SEQ_DEV)))
        return stacked.reshape(TOKENS, D)
    floats = (tokens.astype(jnp.float32), w_qkv.astype(jnp.float32), w_attn_out.astype(jnp.float32), norm_gains.astype(jnp.float32), norm_biases.astype(jnp.float32), w_in.astype(jnp.float32), w_out.astype(jnp.float32))
    result, pullback = jax.vjp(forward, *floats)
    grads = pullback(cotangent.astype(jnp.float32))
    return (result.astype(jnp.bfloat16), grads[0], grads[1], grads[2], grads[3], grads[4], grads[5], grads[6], expert_counts)
```

```python
import jax
import jax.numpy as jnp
from jax import lax
from jax.experimental import pallas as pl
from jax.experimental.pallas import tpu as pltpu
from jax.sharding import PartitionSpec as P

D = 768
HEADS = 12
HEAD_DIM = 64
EXPERTS = 4
BLOCK = 128


EPSILON = 1e-05
NEGATIVE = -1e30


def layer_stats(values):
    average = jnp.mean(values, axis=-1, keepdims=True)
    centred = values - average
    scaled = lax.rsqrt(jnp.mean(centred * centred, axis=-1, keepdims=True) + EPSILON)
    return (centred * scaled, scaled)


def norm_backward(grad_normed, normal, scaled, gain_col):
    grad_scaled = grad_normed * gain_col
    first_mean = jnp.mean(grad_scaled, axis=-1, keepdims=True)
    second_mean = jnp.mean(grad_scaled * normal, axis=-1, keepdims=True)
    return scaled * (grad_scaled - first_mean - normal * second_mean)


def head_groups(heads):
    group_width = 4
    return [(start, start + group_width) for start in range(0, heads, group_width)]


def allowed_keys(length, seq_len):
    places = jnp.arange(seq_len, dtype=jnp.int32)
    return (places[None, :] <= places[:, None]) & (places[None, :] < length)


def masked_scores(query_part, key_part, allowed):
    scale = query_part.shape[-1] ** (-0.5)
    raw = (
        jnp.einsum("qhd,khd->hqk", query_part, key_part, preferred_element_type=jnp.float32) * scale
    )
    return jnp.where(allowed[None], raw, NEGATIVE)


def attention_forward(entry):
    queries, keys, values, length = entry
    allowed = allowed_keys(length, queries.shape[0])
    mixed_parts = []
    total_parts = []
    for start, finish in head_groups(queries.shape[1]):
        scores = masked_scores(queries[:, start:finish], keys[:, start:finish], allowed)
        highest = jnp.max(scores, axis=-1, keepdims=True)
        totals = highest + jnp.log(jnp.sum(jnp.exp(scores - highest), axis=-1, keepdims=True))
        weights = jnp.exp(scores - totals).astype(jnp.bfloat16)
        mixed_parts.append(
            jnp.einsum(
                "hqk,khd->qhd", weights, values[:, start:finish], preferred_element_type=jnp.float32
            ).astype(jnp.bfloat16)
        )
        total_parts.append(totals[..., 0])
    return (jnp.concatenate(mixed_parts, axis=1), jnp.concatenate(total_parts, axis=0))


def attention_backward(entry):
    queries, keys, values, totals, grad_mixed, length = entry
    allowed = allowed_keys(length, queries.shape[0])
    scale = queries.shape[-1] ** (-0.5)
    query_parts, key_parts, value_parts = ([], [], [])
    for start, finish in head_groups(queries.shape[1]):
        scores = masked_scores(queries[:, start:finish], keys[:, start:finish], allowed)
        weights = jnp.exp(scores - totals[start:finish][..., None])
        grad_weights = jnp.einsum(
            "qhd,khd->hqk",
            grad_mixed[:, start:finish],
            values[:, start:finish],
            preferred_element_type=jnp.float32,
        )
        inner_sum = jnp.sum(grad_weights * weights, axis=-1, keepdims=True)
        grad_scores = (weights * (grad_weights - inner_sum)).astype(jnp.bfloat16)
        value_parts.append(
            jnp.einsum(
                "hqk,qhd->khd",
                weights.astype(jnp.bfloat16),
                grad_mixed[:, start:finish],
                preferred_element_type=jnp.float32,
            )
        )
        query_parts.append(
            jnp.einsum(
                "hqk,khd->qhd",
                grad_scores,
                keys[:, start:finish],
                preferred_element_type=jnp.float32,
            )
            * scale
        )
        key_parts.append(
            jnp.einsum(
                "hqk,qhd->khd",
                grad_scores,
                queries[:, start:finish],
                preferred_element_type=jnp.float32,
            )
            * scale
        )
    return (
        jnp.concatenate(query_parts, axis=1),
        jnp.concatenate(key_parts, axis=1),
        jnp.concatenate(value_parts, axis=1),
    )


def segment_table(group_ends, total_rows, block_rows):
    block_count = total_rows // block_rows
    block_starts = jnp.arange(block_count, dtype=jnp.int32) * block_rows
    points = jnp.sort(jnp.concatenate([block_starts, group_ends]))
    finishes = jnp.concatenate([points[1:], jnp.full((1,), total_rows, jnp.int32)])
    blocks = jnp.minimum(points // block_rows, block_count - 1)
    owners = jnp.sum((group_ends[None, :] <= points[:, None]).astype(jnp.int32), axis=1)
    active = (finishes > points) & (owners < group_ends.shape[0])
    owners = jnp.minimum(owners, group_ends.shape[0] - 1)
    return (points, finishes, blocks, owners, active)


def expert_forward(sorted_rows, inner_all, outer_all, table, block_rows):
    model_width = sorted_rows.shape[1]
    hidden_width = inner_all.shape[1]

    def visit(state, entry):
        start, finish, block_id, owner, live = entry

        def compute(inner_state):
            pre_all, result_all = inner_state
            base = block_id * block_rows
            rows_here = lax.dynamic_slice_in_dim(sorted_rows, base, block_rows, 0)
            inner = lax.dynamic_slice_in_dim(inner_all, owner * model_width, model_width, 0)
            outer = lax.dynamic_slice_in_dim(outer_all, owner * hidden_width, hidden_width, 0)
            places = base + jnp.arange(block_rows, dtype=jnp.int32)
            inside = ((places >= start) & (places < finish))[:, None]
            pre = jnp.dot(rows_here, inner, preferred_element_type=jnp.float32)
            result = jnp.dot(
                jax.nn.gelu(pre).astype(jnp.bfloat16), outer, preferred_element_type=jnp.float32
            )
            old_pre = lax.dynamic_slice_in_dim(pre_all, base, block_rows, 0)
            old_result = lax.dynamic_slice_in_dim(result_all, base, block_rows, 0)
            pre_all = lax.dynamic_update_slice_in_dim(
                pre_all, jnp.where(inside, pre, old_pre), base, 0
            )
            result_all = lax.dynamic_update_slice_in_dim(
                result_all, jnp.where(inside, result, old_result), base, 0
            )
            return (pre_all, result_all)

        return (lax.cond(live, compute, lambda same: same, state), None)

    start_state = (
        jnp.zeros((sorted_rows.shape[0], hidden_width), jnp.float32),
        jnp.zeros((sorted_rows.shape[0], model_width), jnp.float32),
    )
    final_state, _ = lax.scan(visit, start_state, table)
    return final_state


def expert_backward(sorted_rows, pre_all, grad_sorted, inner_all, outer_all, table, block_rows):
    model_width = sorted_rows.shape[1]
    hidden_width = inner_all.shape[1]

    def visit(state, entry):
        start, finish, block_id, owner, live = entry

        def compute(inner_state):
            grad_rows, grad_inner, grad_outer = inner_state
            base = block_id * block_rows
            rows_here = lax.dynamic_slice_in_dim(sorted_rows, base, block_rows, 0)
            pre = lax.dynamic_slice_in_dim(pre_all, base, block_rows, 0)
            inner = lax.dynamic_slice_in_dim(inner_all, owner * model_width, model_width, 0)
            outer = lax.dynamic_slice_in_dim(outer_all, owner * hidden_width, hidden_width, 0)
            places = base + jnp.arange(block_rows, dtype=jnp.int32)
            inside = ((places >= start) & (places < finish))[:, None]
            grad_block = jnp.where(
                inside,
                lax.dynamic_slice_in_dim(grad_sorted, base, block_rows, 0),
                jnp.zeros((), jnp.bfloat16),
            )
            activated, gelu_pull = jax.vjp(jax.nn.gelu, pre)
            outer_piece = jnp.einsum(
                "tf,td->fd",
                activated.astype(jnp.bfloat16),
                grad_block,
                preferred_element_type=jnp.float32,
            )
            grad_act = jnp.einsum(
                "td,fd->tf", grad_block, outer, preferred_element_type=jnp.float32
            )
            grad_pre = gelu_pull(grad_act)[0].astype(jnp.bfloat16)
            inner_piece = jnp.einsum(
                "td,tf->df", rows_here, grad_pre, preferred_element_type=jnp.float32
            )
            rows_piece = jnp.einsum(
                "tf,df->td", grad_pre, inner, preferred_element_type=jnp.float32
            )
            old_rows = lax.dynamic_slice_in_dim(grad_rows, base, block_rows, 0)
            grad_rows = lax.dynamic_update_slice_in_dim(grad_rows, old_rows + rows_piece, base, 0)
            old_inner = lax.dynamic_slice_in_dim(grad_inner, owner * model_width, model_width, 0)
            grad_inner = lax.dynamic_update_slice_in_dim(
                grad_inner, old_inner + inner_piece, owner * model_width, 0
            )
            old_outer = lax.dynamic_slice_in_dim(grad_outer, owner * hidden_width, hidden_width, 0)
            grad_outer = lax.dynamic_update_slice_in_dim(
                grad_outer, old_outer + outer_piece, owner * hidden_width, 0
            )
            return (grad_rows, grad_inner, grad_outer)

        return (lax.cond(live, compute, lambda same: same, state), None)

    start_state = (
        jnp.zeros(sorted_rows.shape, jnp.float32),
        jnp.zeros(inner_all.shape, jnp.float32),
        jnp.zeros(outer_all.shape, jnp.float32),
    )
    final_state, _ = lax.scan(visit, start_state, table)
    return final_state


def body(
    tokens,
    token_ids,
    lengths,
    hash_table,
    w_qkv,
    w_attn_out,
    norm_gains,
    norm_biases,
    w_in,
    w_out,
    cotangent,
):
    rows_count = tokens.shape[0]
    seq_count = lengths.shape[0]
    seq_len = rows_count // seq_count
    model_width = D
    expert_total = EXPERTS
    qkv_full, proj_full, gains_full, biases_full = (
        lax.all_gather(w_qkv, ("dp", "fsdp"), axis=0, tiled=True),
        lax.all_gather(w_attn_out, ("dp", "fsdp"), axis=0, tiled=True),
        lax.all_gather(norm_gains, ("dp", "fsdp"), axis=0, tiled=True),
        lax.all_gather(norm_biases, ("dp", "fsdp"), axis=0, tiled=True),
    )
    gains_f = gains_full.astype(jnp.float32)
    biases_f = biases_full.astype(jnp.float32)
    inputs = tokens.astype(jnp.float32)
    normal_one, scaled_one = layer_stats(inputs)
    first_in = (normal_one * gains_f[:, 0] + biases_f[:, 0]).astype(jnp.bfloat16)
    qkv_low = jnp.dot(first_in, qkv_full, preferred_element_type=jnp.float32).astype(jnp.bfloat16)
    packed = qkv_low.reshape(seq_count, seq_len, 3, HEADS, HEAD_DIM)
    queries = packed[:, :, 0]
    keys = packed[:, :, 1]
    values = packed[:, :, 2]
    mixed, totals = lax.map(attention_forward, (queries, keys, values, lengths))
    mixed_flat = mixed.reshape(rows_count, model_width)
    hidden = inputs + jnp.dot(mixed_flat, proj_full, preferred_element_type=jnp.float32)
    normal_two, scaled_two = layer_stats(hidden)
    second_in = (normal_two * gains_f[:, 1] + biases_f[:, 1]).astype(jnp.bfloat16)
    places = jnp.arange(rows_count, dtype=jnp.int32) % seq_len
    used = places < jnp.repeat(lengths, seq_len, total_repeat_length=rows_count)
    expert_ids = jnp.where(used, hash_table[token_ids], expert_total)
    matches = (expert_ids[:, None] == jnp.arange(expert_total, dtype=jnp.int32)[None, :]).astype(
        jnp.int32
    )
    local_counts = jnp.sum(matches, axis=0)
    expert_counts = lax.psum(local_counts, ("dp", "fsdp"))
    ordering = jnp.argsort(expert_ids, stable=True)
    inverse = (
        jnp.zeros((rows_count,), jnp.int32)
        .at[ordering]
        .set(jnp.arange(rows_count, dtype=jnp.int32))
    )
    group_ends = jnp.cumsum(local_counts)
    table = segment_table(group_ends, rows_count, BLOCK)
    inner_all, outer_all = (
        lax.all_gather(w_in, ("dp", "fsdp"), axis=0, tiled=True),
        lax.all_gather(w_out, ("dp", "fsdp"), axis=0, tiled=True),
    )
    sorted_rows = second_in[ordering]
    pre_all, result_sorted = expert_forward(sorted_rows, inner_all, outer_all, table, BLOCK)
    layer_out = (hidden + result_sorted[inverse]).astype(jnp.bfloat16)
    grad_out = cotangent.astype(jnp.float32)
    grad_sorted = cotangent[ordering]
    inner_back, outer_back = (
        lax.all_gather(w_in, ("dp", "fsdp"), axis=0, tiled=True),
        lax.all_gather(w_out, ("dp", "fsdp"), axis=0, tiled=True),
    )
    grad_rows_sorted, grad_inner, grad_outer = expert_backward(
        sorted_rows, pre_all, grad_sorted, inner_back, outer_back, table, BLOCK
    )
    grad_w_in, grad_w_out = (
        lax.psum_scatter(grad_inner, ("dp", "fsdp"), scatter_dimension=0, tiled=True),
        lax.psum_scatter(grad_outer, ("dp", "fsdp"), scatter_dimension=0, tiled=True),
    )
    grad_second = grad_rows_sorted[inverse]
    gain_two = jnp.sum(grad_second * normal_two, axis=0)
    bias_two = jnp.sum(grad_second, axis=0)
    grad_hidden = grad_out + norm_backward(grad_second, normal_two, scaled_two, gains_f[:, 1])
    grad_branch = grad_hidden.astype(jnp.bfloat16)
    qkv_back, proj_back = (
        lax.all_gather(w_qkv, ("dp", "fsdp"), axis=0, tiled=True),
        lax.all_gather(w_attn_out, ("dp", "fsdp"), axis=0, tiled=True),
    )
    grad_proj = jnp.einsum("td,te->de", mixed_flat, grad_branch, preferred_element_type=jnp.float32)
    grad_mixed = jnp.einsum(
        "te,de->td", grad_branch, proj_back, preferred_element_type=jnp.float32
    ).astype(jnp.bfloat16)
    grad_mixed = grad_mixed.reshape(seq_count, seq_len, HEADS, HEAD_DIM)
    grad_queries, grad_keys, grad_values = lax.map(
        attention_backward, (queries, keys, values, totals, grad_mixed, lengths)
    )
    grad_qkv = (
        jnp.stack([grad_queries, grad_keys, grad_values], axis=2)
        .reshape(rows_count, 3 * model_width)
        .astype(jnp.bfloat16)
    )
    grad_qkv_w = jnp.einsum("td,te->de", first_in, grad_qkv, preferred_element_type=jnp.float32)
    grad_first = jnp.einsum("te,de->td", grad_qkv, qkv_back, preferred_element_type=jnp.float32)
    gain_one = jnp.sum(grad_first * normal_one, axis=0)
    bias_one = jnp.sum(grad_first, axis=0)
    grad_tokens = grad_hidden + norm_backward(grad_first, normal_one, scaled_one, gains_f[:, 0])
    grad_gains = jnp.stack([gain_one, gain_two], axis=1)
    grad_biases = jnp.stack([bias_one, bias_two], axis=1)
    grad_w_qkv, grad_w_attn_out, grad_norm_gains, grad_norm_biases = (
        lax.psum_scatter(grad_qkv_w, ("dp", "fsdp"), scatter_dimension=0, tiled=True),
        lax.psum_scatter(grad_proj, ("dp", "fsdp"), scatter_dimension=0, tiled=True),
        lax.psum_scatter(grad_gains, ("dp", "fsdp"), scatter_dimension=0, tiled=True),
        lax.psum_scatter(grad_biases, ("dp", "fsdp"), scatter_dimension=0, tiled=True),
    )
    return (
        layer_out,
        grad_tokens,
        grad_w_qkv,
        grad_w_attn_out,
        grad_norm_gains,
        grad_norm_biases,
        grad_w_in,
        grad_w_out,
        expert_counts,
    )


LOG2E = 1.4426950408889634
ROWS = 256
GROUP = 16
MIB = 1024 * 1024
NT = (((1,), (1,)), ((), ()))
NN = (((1,), (0,)), ((), ()))
ROOT = 0.7978845608028654
CUBIC = 0.044715


def mul(a, b, dims=NN):
    return lax.dot_general(a, b, dims, preferred_element_type=jnp.float32)


def iota(shape, dim):
    return lax.broadcasted_iota(jnp.int32, shape, dim)


def padded_rows(slots):
    return slots + EXPERTS * GROUP


def three_parts(v):
    first = v.astype(jnp.bfloat16)
    rest = v - first.astype(jnp.float32)
    second = rest.astype(jnp.bfloat16)
    third = (rest - second.astype(jnp.float32)).astype(jnp.bfloat16)
    return first, second, third


def own_lanes(lane, half):
    return (lane < HEAD_DIM) if half == 0 else (lane >= HEAD_DIM)


def extra_lane(half):
    return HEAD_DIM if half == 0 else 0


def routing(ids, table, length, perm_ref):
    slots = ids.shape[1]
    chosen = (iota((table.shape[1], slots), 0) == (ids >> 7)).astype(jnp.bfloat16)
    rows = mul(table, chosen)
    expert = jnp.sum(
        jnp.where(iota(rows.shape, 0) == (ids & 127), rows, 0.0), axis=0, keepdims=True
    ).astype(jnp.int32)
    used = iota((1, slots), 1) < length
    member = (iota((8, slots), 0) == expert) & used
    member_f = jnp.where(member, 1.0, 0.0)
    perm_ref[0:slots, :] = (iota((slots, slots), 0) <= iota((slots, slots), 1)).astype(jnp.bfloat16)
    rank = mul(member_f.astype(jnp.bfloat16), perm_ref[0:slots, :])
    counts = rank[:, slots - 1 : slots]
    groups = jnp.floor((counts + (GROUP - 1)) * (1.0 / GROUP))
    row8 = iota((8, 1), 0)
    start = jnp.zeros((8, 1), jnp.float32)
    for e in range(EXPERTS - 1):
        start = start + jnp.where(row8 > e, groups[e : e + 1, :], 0.0)
    place = jnp.sum(member_f * (rank - 1.0 + start * GROUP), axis=0, keepdims=True)
    place = jnp.where(used, place, -1.0)
    return place, counts, groups


def front_kernel(
    len_ref, x_ref, ids_ref, table_ref, g_ref, wa_ref, norms_ref,
    qkv_ref, mixed_ref, aug_ref, hidden_ref, xs_ref, gs_ref, pos_ref, counts_ref,
    perm_ref, normed_ref, qa_ref, ka_ref, va_ref,
):
    slots, width = x_ref.shape
    heads = width // HEAD_DIM
    rp = padded_rows(slots)
    length = len_ref[0]

    place, counts, groups = routing(ids_ref[...], table_ref[...], length, perm_ref)
    pos_ref[...] = jnp.broadcast_to(place, (128, slots)).T
    counts_ref[...] = jnp.broadcast_to(counts, (8, 128)).astype(jnp.int32)
    place_i = place.astype(jnp.int32)
    step = rp // 4

    @pl.loop(0, 4)
    def _(i):
        base = i * step
        perm_ref[pl.ds(base, step), :] = (
            iota((step, slots), 0) + base == place_i
        ).astype(jnp.bfloat16)
        gs_ref[pl.ds(base, step), :] = mul(perm_ref[pl.ds(base, step), :], g_ref[...]).astype(jnp.bfloat16)

    tail = jnp.broadcast_to(jnp.concatenate([groups, groups], axis=0), (GROUP, width)).astype(jnp.bfloat16)
    xs_ref[rp : rp + GROUP, :] = tail
    gs_ref[rp : rp + GROUP, :] = tail

    @pl.loop(0, slots // ROWS)
    def _(i):
        rows = pl.ds(i * ROWS, ROWS)
        normal, _ = layer_stats(x_ref[rows, :].astype(jnp.float32))
        normed = (normal * norms_ref[0:1, :] + norms_ref[2:3, :]).astype(jnp.bfloat16)
        for c in range(3):
            cols = slice(c * width, (c + 1) * width)
            qkv_ref[rows, cols] = mul(normed, wa_ref[:, cols]).astype(jnp.bfloat16)

    lane = iota((slots, 128), 1)
    key_bias = jnp.where(iota((slots, 128), 0) < length, 0.0, NEGATIVE).astype(jnp.bfloat16)
    causal = iota((ROWS, ROWS), 1) <= iota((ROWS, ROWS), 0)
    lane_b = iota((ROWS, 128), 1)

    @pl.loop(0, heads // 2)
    def _(p):
        cols = pl.ds(p * 128, 128)
        q = qkv_ref[:, cols].astype(jnp.float32) * (HEAD_DIM ** -0.5 * LOG2E)
        q_hi = q.astype(jnp.bfloat16)
        q_lo = (q - q_hi.astype(jnp.float32)).astype(jnp.bfloat16)
        k = qkv_ref[:, pl.ds(width + p * 128, 128)]
        v = qkv_ref[:, pl.ds(2 * width + p * 128, 128)]
        zero = jnp.zeros_like(q_hi)
        one = jnp.ones_like(q_hi)
        sides = []
        for half in range(2):
            own = own_lanes(lane, half)
            extra = extra_lane(half)
            qa_ref[half, :, 0:128] = jnp.where(own, q_hi, zero)
            qa_ref[half, :, 128:256] = jnp.where(own, q_lo, jnp.where(lane == extra, one, zero))
            ka_ref[half, :, 0:128] = k
            ka_ref[half, :, 128:256] = jnp.where(own, k, jnp.where(lane == extra, key_bias, zero))
            va_ref[half, :, :] = jnp.where(own, v, one)
        for i in range(slots // ROWS):
            rows = slice(i * ROWS, (i + 1) * ROWS)
            keys = (i + 1) * ROWS
            outs = []
            for half in range(2):
                s = mul(qa_ref[half, rows, :], ka_ref[half, 0:keys, :], NT)
                diag = jnp.where(causal, s[:, i * ROWS :], NEGATIVE)
                s = diag if i == 0 else jnp.concatenate([s[:, : i * ROWS], diag], axis=1)
                top = jnp.max(s, axis=1, keepdims=True)
                probs = jnp.exp2(s - top).astype(jnp.bfloat16)
                out = mul(probs, va_ref[half, 0:keys, :])
                total = pltpu.roll(out, HEAD_DIM, 1)
                outs.append(out / total)
                minus = -(top + jnp.log2(out))
                a, b, c = three_parts(minus)
                extra = extra_lane(half)
                seen = qa_ref[half, rows, 128:256]
                seen = jnp.where(lane_b == extra + 1, a, seen)
                seen = jnp.where(lane_b == extra + 2, b, seen)
                seen = jnp.where(lane_b == extra + 3, c, seen)
                aug_ref[2 * p + half, rows, :] = seen
            mixed_ref[rows, cols] = jnp.where(lane_b < HEAD_DIM, outs[0], outs[1]).astype(jnp.bfloat16)

    @pl.loop(0, slots // ROWS)
    def _(i):
        rows = pl.ds(i * ROWS, ROWS)
        hidden = x_ref[rows, :].astype(jnp.float32) + mul(mixed_ref[rows, :], wa_ref[:, 3 * width :])
        hidden_ref[rows, :] = hidden
        normal, _ = layer_stats(hidden)
        normed_ref[rows, :] = (normal * norms_ref[1:2, :] + norms_ref[3:4, :]).astype(jnp.bfloat16)

    @pl.loop(0, 4)
    def _(i):
        rows = pl.ds(i * step, step)
        xs_ref[rows, :] = mul(perm_ref[rows, :], normed_ref[...]).astype(jnp.bfloat16)


def front(length, x, ids, table, g, wa, norms):
    slots, width = x.shape
    rp = padded_rows(slots)
    bf = jnp.bfloat16
    whole = pl.BlockSpec(memory_space=pltpu.VMEM)
    return pl.pallas_call(
        front_kernel,
        out_shape=(
            jax.ShapeDtypeStruct((slots, 3 * width), bf),
            jax.ShapeDtypeStruct((slots, width), bf),
            jax.ShapeDtypeStruct((HEADS, slots, 128), bf),
            jax.ShapeDtypeStruct((slots, width), jnp.float32),
            jax.ShapeDtypeStruct((rp + GROUP, width), bf),
            jax.ShapeDtypeStruct((rp + GROUP, width), bf),
            jax.ShapeDtypeStruct((slots, 128), jnp.float32),
            jax.ShapeDtypeStruct((8, 128), jnp.int32),
        ),
        in_specs=[pl.BlockSpec(memory_space=pltpu.SMEM)] + [whole] * 6,
        out_specs=tuple([whole] * 8),
        scratch_shapes=[
            pltpu.VMEM((rp, slots), bf),
            pltpu.VMEM((slots, width), bf),
            pltpu.VMEM((2, slots, 256), bf),
            pltpu.VMEM((2, slots, 256), bf),
            pltpu.VMEM((2, slots, 128), bf),
        ],
        compiler_params=pltpu.CompilerParams(vmem_limit_bytes=56 * MIB),
        name="front",
    )(length, x, ids, table, g, wa, norms)


CHUNK = 32


def experts_kernel(
    n_ref, x_ref, g_ref, w1_ref, w2_ref,
    o_ref, dx_ref, gw1_ref, gw2_ref,
    xb, gb, ob, db, acc1, acc2, blank, sem_in, sem_out, sem_zero,
):
    sources, groups, _, width = x_ref.shape
    groups = groups - 1
    hidden = w2_ref.shape[1]
    rows = CHUNK * GROUP

    blank[...] = jnp.zeros_like(blank)
    xb[...] = jnp.zeros_like(xb)
    gw1_ref[...] = jnp.zeros_like(gw1_ref)
    gw2_ref[...] = jnp.zeros_like(gw2_ref)

    totals = []
    for e in range(EXPERTS):
        totals.append(lax.fori_loop(0, sources, lambda s, t, e=e: t + n_ref[s * EXPERTS + e], 0))
    first = [0]
    for e in range(EXPERTS):
        first.append(first[-1] + (totals[e] + (CHUNK - 1)) // CHUNK)
    chunks = first[EXPERTS]

    def pick(values, e):
        out = values[0]
        for i in range(1, EXPERTS):
            out = jnp.where(e == i, values[i], out)
        return out

    def locate(c):
        e = jnp.int32(0)
        for i in range(1, EXPERTS):
            e = e + jnp.where(c >= first[i], 1, 0)
        begin = (c - pick(first, e)) * CHUNK
        return e, begin, jnp.minimum(begin + CHUNK, pick(totals, e))

    def pieces(c, act):
        e, begin, end = locate(c)

        def visit(s, base):
            n = n_ref[s * EXPERTS + e]
            low = jnp.maximum(base, begin)
            size = jnp.minimum(base + n, end) - low
            skip = jnp.int32(0)
            for i in range(EXPERTS - 1):
                skip = skip + jnp.where(e > i, n_ref[s * EXPERTS + i], 0)

            @pl.when(size > 0)
            def _():
                act(s, skip + low - base, low - begin, size)

            return base + n

        lax.fori_loop(0, sources, visit, jnp.int32(0))

    def load(c, slot):
        def act(s, at, to, size):
            for k, (src, dst) in enumerate(((x_ref, xb), (g_ref, gb))):
                pltpu.make_async_copy(
                    src.at[s, pl.ds(at, size)], dst.at[slot, pl.ds(to, size)], sem_in.at[k, slot]
                ).start()

        pieces(c, act)

    def store(c, slot):
        def act(s, at, to, size):
            for k, (src, dst) in enumerate(((ob, o_ref), (db, dx_ref))):
                pltpu.make_async_copy(
                    src.at[slot, pl.ds(to, size)], dst.at[s, pl.ds(at, size)], sem_out.at[k, slot]
                ).start()

        pieces(c, act)

    def settle(c, slot, bufs, sems):
        _, begin, end = locate(c)
        for k, buf in enumerate(bufs):
            part = buf.at[slot, pl.ds(0, end - begin)]
            pltpu.make_async_copy(part, part, sems.at[k, slot]).wait()

    def used_groups(s):
        t = n_ref[s * EXPERTS]
        for e in range(1, EXPERTS):
            t = t + n_ref[s * EXPERTS + e]
        return t

    def rest(s, act):
        t = used_groups(s)

        @pl.when(groups - t > 0)
        def _():
            for k, dst in enumerate((o_ref, dx_ref)):
                act(
                    pltpu.make_async_copy(
                        blank.at[pl.ds(0, groups - t)], dst.at[s, pl.ds(t, groups - t)], sem_zero.at[k, s]
                    )
                )

    @pl.loop(0, sources)
    def _(s):
        rest(s, lambda copy: copy.start())

    @pl.when(chunks > 0)
    def _():
        load(0, 0)

    @pl.loop(0, chunks)
    def _(c):
        slot = c % 2
        e, begin, end = locate(c)

        @pl.when(c + 1 < chunks)
        def _():
            load(c + 1, 1 - slot)

        settle(c, slot, (xb, gb), sem_in)

        @pl.when(c >= 2)
        def _():
            settle(c - 2, slot, (ob, db), sem_out)

        x = xb[slot].reshape(rows, width)
        g = gb[slot].reshape(rows, width)
        g = jnp.where(iota((rows, width), 0) < (end - begin) * GROUP, g, jnp.zeros_like(g))
        w1 = w1_ref[e]
        w2 = w2_ref[e]
        pre = mul(x, w1)
        square = pre * pre
        t = jnp.tanh(ROOT * pre * (1.0 + CUBIC * square))
        act = (0.5 * pre * (1.0 + t)).astype(jnp.bfloat16)
        slope = 0.5 * (1.0 + t) + 0.5 * pre * (1.0 - t * t) * (ROOT * (1.0 + 3.0 * CUBIC * square))
        grad_pre = (slope * mul(g, w2, NT)).astype(jnp.bfloat16)
        ob[slot] = mul(act, w2).astype(jnp.bfloat16).reshape(CHUNK, GROUP, width)
        db[slot] = mul(grad_pre, w1, NT).astype(jnp.bfloat16).reshape(CHUNK, GROUP, width)
        store(c, slot)
        add1 = mul(grad_pre.T, x)
        add2 = mul(act.T, g)

        @pl.when(begin == 0)
        def _():
            acc1[...] = add1
            acc2[...] = add2

        @pl.when(begin > 0)
        def _():
            acc1[...] += add1
            acc2[...] += add2

        @pl.when(end == pick(totals, e))
        def _():
            gw1_ref[e] = acc1[...].astype(gw1_ref.dtype)
            gw2_ref[e] = acc2[...].astype(gw2_ref.dtype)

    @pl.when(chunks >= 2)
    def _():
        settle(chunks - 2, chunks % 2, (ob, db), sem_out)

    @pl.when(chunks >= 1)
    def _():
        settle(chunks - 1, (chunks - 1) % 2, (ob, db), sem_out)

    @pl.loop(0, sources)
    def _(s):
        rest(s, lambda copy: copy.wait())


def experts(n16, xs, gs, w1, w2):
    sources, groups, _, width = xs.shape
    hidden = w2.shape[1]
    bf = jnp.bfloat16
    whole = pl.BlockSpec(memory_space=pltpu.VMEM)
    far = pl.BlockSpec(memory_space=pl.ANY)
    out_rows = jax.ShapeDtypeStruct((sources, groups - 1, GROUP, width), bf)
    return pl.pallas_call(
        experts_kernel,
        out_shape=(
            out_rows, out_rows,
            jax.ShapeDtypeStruct((EXPERTS, hidden, width), bf),
            jax.ShapeDtypeStruct((EXPERTS, hidden, width), bf),
        ),
        in_specs=[pl.BlockSpec(memory_space=pltpu.SMEM), far, far, whole, whole],
        out_specs=(far, far, whole, whole),
        scratch_shapes=[pltpu.VMEM((2, CHUNK, GROUP, width), bf)] * 4
        + [pltpu.VMEM((hidden, width), jnp.float32)] * 2
        + [pltpu.VMEM((groups - 1, GROUP, width), bf)]
        + [pltpu.SemaphoreType.DMA((2, 2)), pltpu.SemaphoreType.DMA((2, 2)), pltpu.SemaphoreType.DMA((2, sources))],
        compiler_params=pltpu.CompilerParams(vmem_limit_bytes=56 * MIB),
        name="experts",
    )(n16, xs, gs, w1, w2)


def back_kernel(
    len_ref, x_ref, g_ref, hidden_ref, qkv_ref, mixed_ref, aug_ref, pos_ref, dxs_ref, os_ref, wa_ref, norms_ref,
    out_ref, gx_ref, gwa_ref, gn_ref,
    branch_ref, gmix_ref, gqkv_ref, tr_ref, qa_ref, ka_ref, va_ref, oa_ref, dv_ref, dk_ref, dq_ref,
):
    slots, width = x_ref.shape
    heads = width // HEAD_DIM
    rp = dxs_ref.shape[0]
    length = len_ref[0]
    scale = HEAD_DIM ** -0.5
    gn_ref[...] = jnp.zeros_like(gn_ref)

    @pl.loop(0, slots // ROWS)
    def _(i):
        rows = pl.ds(i * ROWS, ROWS)
        place = pos_ref[rows, 0:1].astype(jnp.int32)
        pick = (iota((ROWS, rp), 1) == place).astype(jnp.bfloat16)
        hidden = hidden_ref[rows, :]
        out_ref[rows, :] = (hidden + mul(pick, os_ref[...])).astype(jnp.bfloat16)
        grad = mul(pick, dxs_ref[...])
        normal, scaled = layer_stats(hidden)
        gn_ref[1:2, :] += jnp.sum(grad * normal, axis=0, keepdims=True)
        gn_ref[3:4, :] += jnp.sum(grad, axis=0, keepdims=True)
        grad_hidden = g_ref[rows, :].astype(jnp.float32) + norm_backward(grad, normal, scaled, norms_ref[1:2, :])
        gx_ref[rows, :] = grad_hidden
        branch = grad_hidden.astype(jnp.bfloat16)
        branch_ref[rows, :] = branch
        gmix_ref[rows, :] = mul(branch, wa_ref[:, 3 * width :], NT).astype(jnp.bfloat16)

    tr_ref[...] = mixed_ref[...].T
    tile = width // 3

    @pl.loop(0, 3)
    def _(i):
        rows = pl.ds(i * tile, tile)
        gwa_ref[rows, 3 * width :] = mul(tr_ref[rows, :], branch_ref[...]).astype(gwa_ref.dtype)

    lane = iota((slots, 128), 1)
    key_bias = jnp.where(iota((slots, 128), 0) < length, 0.0, NEGATIVE).astype(jnp.bfloat16)
    causal = iota((ROWS, ROWS), 0) <= iota((ROWS, ROWS), 1)

    @pl.loop(0, heads // 2)
    def _(p):
        cols = pl.ds(p * 128, 128)
        q = qkv_ref[:, cols]
        q_hi = (q.astype(jnp.float32) * (scale * LOG2E)).astype(jnp.bfloat16)
        k = qkv_ref[:, pl.ds(width + p * 128, 128)]
        v = qkv_ref[:, pl.ds(2 * width + p * 128, 128)]
        do = gmix_ref[:, cols]
        prod = do.astype(jnp.float32) * mixed_ref[:, cols].astype(jnp.float32)
        k_t = k.T
        zero = jnp.zeros_like(q)
        one = jnp.ones_like(q)
        for half in range(2):
            own = own_lanes(lane, half)
            extra = extra_lane(half)
            parts = (lane > extra) & (lane <= extra + 3)
            qa_ref[half, :, 0:128] = jnp.where(own, q_hi, zero)
            qa_ref[half, :, 128:256] = aug_ref[2 * p + half]
            ka_ref[half, :, 0:128] = k
            ka_ref[half, :, 128:256] = jnp.where(
                own, k, jnp.where(lane == extra, key_bias, jnp.where(parts, one, zero))
            )
            va_ref[half, :, :] = jnp.where(own, v, jnp.where(parts, one, zero))
            minus = -jnp.sum(jnp.where(own, prod, 0.0), axis=1, keepdims=True)
            a, b, c = three_parts(jnp.broadcast_to(minus, (slots, 128)))
            oa_ref[half, :, :] = jnp.where(
                own, do,
                jnp.where(lane == extra + 1, a, jnp.where(lane == extra + 2, b, jnp.where(lane == extra + 3, c, zero))),
            )
        for half in range(2):
            k_own = k_t[half * HEAD_DIM : (half + 1) * HEAD_DIM, :]
            heads_rows = slice(half * HEAD_DIM, (half + 1) * HEAD_DIM)
            for j in range(slots // ROWS):
                keys = slice(j * ROWS, (j + 1) * ROWS)
                late = slice(j * ROWS, slots)
                s = mul(ka_ref[half, keys, :], qa_ref[half, late, :], NT)
                diag = jnp.where(causal, s[:, :ROWS], NEGATIVE)
                s = diag if j == slots // ROWS - 1 else jnp.concatenate([diag, s[:, ROWS:]], axis=1)
                probs = jnp.exp2(s)
                dp = mul(va_ref[half, keys, :], oa_ref[half, late, :], NT)
                ds = (probs * dp).astype(jnp.bfloat16)
                probs = probs.astype(jnp.bfloat16)
                dv_ref[half, keys, :] = mul(probs, gmix_ref[late, cols])
                dk_ref[half, keys, :] = mul(ds, qkv_ref[late, cols])
                dq = mul(k_own[:, keys], ds)
                if j == 0:
                    dq_ref[heads_rows, late] = dq
                else:
                    dq_ref[heads_rows, late] += dq
        first = lane < HEAD_DIM
        gqkv_ref[:, cols] = (dq_ref[...].T * scale).astype(jnp.bfloat16)
        gqkv_ref[:, pl.ds(width + p * 128, 128)] = (jnp.where(first, dk_ref[0], dk_ref[1]) * scale).astype(jnp.bfloat16)
        gqkv_ref[:, pl.ds(2 * width + p * 128, 128)] = jnp.where(first, dv_ref[0], dv_ref[1]).astype(jnp.bfloat16)

    @pl.loop(0, slots // ROWS)
    def _(i):
        rows = pl.ds(i * ROWS, ROWS)
        normal, scaled = layer_stats(x_ref[rows, :].astype(jnp.float32))
        branch_ref[rows, :] = (normal * norms_ref[0:1, :] + norms_ref[2:3, :]).astype(jnp.bfloat16)
        grad = mul(gqkv_ref[rows, :], wa_ref[:, : 3 * width], NT)
        gn_ref[0:1, :] += jnp.sum(grad * normal, axis=0, keepdims=True)
        gn_ref[2:3, :] += jnp.sum(grad, axis=0, keepdims=True)
        gx_ref[rows, :] += norm_backward(grad, normal, scaled, norms_ref[0:1, :])

    tr_ref[...] = branch_ref[...].T

    @pl.loop(0, 3)
    def _(i):
        rows = pl.ds(i * tile, tile)
        for c in range(3):
            cols = slice(c * width, (c + 1) * width)
            gwa_ref[rows, cols] = mul(tr_ref[rows, :], gqkv_ref[:, cols]).astype(gwa_ref.dtype)


def back(length, x, g, hidden, qkv, mixed, aug, pos, dxs, os, wa, norms):
    slots, width = x.shape
    bf = jnp.bfloat16
    f32 = jnp.float32
    whole = pl.BlockSpec(memory_space=pltpu.VMEM)
    return pl.pallas_call(
        back_kernel,
        out_shape=(
            jax.ShapeDtypeStruct((slots, width), bf),
            jax.ShapeDtypeStruct((slots, width), f32),
            jax.ShapeDtypeStruct((width, 4 * width), bf),
            jax.ShapeDtypeStruct((8, width), f32),
        ),
        in_specs=[pl.BlockSpec(memory_space=pltpu.SMEM)] + [whole] * 11,
        out_specs=tuple([whole] * 4),
        scratch_shapes=[
            pltpu.VMEM((slots, width), bf),
            pltpu.VMEM((slots, width), bf),
            pltpu.VMEM((slots, 3 * width), bf),
            pltpu.VMEM((width, slots), bf),
            pltpu.VMEM((2, slots, 256), bf),
            pltpu.VMEM((2, slots, 256), bf),
            pltpu.VMEM((2, slots, 128), bf),
            pltpu.VMEM((2, slots, 128), bf),
            pltpu.VMEM((2, slots, 128), f32),
            pltpu.VMEM((2, slots, 128), f32),
            pltpu.VMEM((128, slots), f32),
        ],
        compiler_params=pltpu.CompilerParams(vmem_limit_bytes=60 * MIB),
        name="back",
    )(length, x, g, hidden, qkv, mixed, aug, pos, dxs, os, wa, norms)


def plane_body(
    tokens, token_ids, lengths, hash_table, w_qkv, w_attn_out, norm_gains, norm_biases, w_in, w_out, cotangent
):
    slots, width = tokens.shape
    bf = jnp.bfloat16
    both = ("dp", "fsdp")
    plane = lax.axis_size("fsdp")
    part = w_in.shape[1] // plane
    rp = padded_rows(slots)

    norm_cols = jnp.concatenate([norm_gains, norm_biases], axis=1)
    wa_local = jnp.concatenate([w_qkv, w_attn_out, jnp.pad(norm_cols, ((0, 0), (0, 124)))], axis=1)
    wa = lax.all_gather(wa_local, both, axis=0, tiled=True)
    norms = jnp.pad(wa[:, 4 * width : 4 * width + 4].astype(jnp.float32).T, ((0, 4), (0, 0)))
    wa = wa[:, : 4 * width]
    w1 = lax.all_to_all(w_in, "fsdp", split_axis=1, concat_axis=0, tiled=True)
    w1 = lax.all_gather(w1, "dp", axis=0, tiled=True).reshape(EXPERTS, width, part)
    w2 = lax.all_gather(w_out, "dp", axis=0, tiled=True).reshape(EXPERTS, part, width)

    table = jnp.pad(hash_table, (0, (-hash_table.shape[0]) % 8192)).reshape(64, 128).T.astype(bf)
    qkv, mixed, aug, hidden, xs, gs, pos, counts = front(
        lengths, tokens, token_ids.reshape(1, slots), table, cotangent, wa, norms
    )
    expert_counts = lax.psum(counts[:EXPERTS, 0], both)
    xs_all = lax.all_gather(xs, "fsdp", axis=0, tiled=True).reshape(plane, rp // GROUP + 1, GROUP, width)
    gs_all = lax.all_gather(gs, "fsdp", axis=0, tiled=True).reshape(plane, rp // GROUP + 1, GROUP, width)
    n16 = xs_all[:, rp // GROUP, :EXPERTS, 0].astype(jnp.int32).reshape(-1)
    o_part, dx_part, gw1, gw2 = experts(n16, xs_all, gs_all, w1, w2)
    os = lax.psum_scatter(o_part.reshape(plane * rp, width), "fsdp", scatter_dimension=0, tiled=True)
    dxs = lax.psum_scatter(dx_part.reshape(plane * rp, width), "fsdp", scatter_dimension=0, tiled=True)
    gw1 = lax.psum_scatter(gw1.reshape(EXPERTS * part, width), "dp", scatter_dimension=0, tiled=True)
    gw2 = lax.psum_scatter(gw2.reshape(EXPERTS * part, width), "dp", scatter_dimension=0, tiled=True)
    gw1 = lax.all_to_all(gw1, "fsdp", split_axis=1, concat_axis=0, tiled=True)
    out, gx, gwa, gn = back(lengths, tokens, cotangent, hidden, qkv, mixed, aug, pos, dxs, os, wa, norms)
    gwa = lax.psum_scatter(gwa, both, scatter_dimension=0, tiled=True).astype(jnp.float32)
    gn = lax.psum_scatter(gn[:4].T, both, scatter_dimension=0, tiled=True)
    return (
        out, gx, gwa[:, : 3 * width], gwa[:, 3 * width :], gn[:, 0:2], gn[:, 2:4],
        gw1.T.astype(jnp.float32), gw2.astype(jnp.float32), expert_counts,
    )


def solution(mesh):
    placed = (
        P(("dp", "fsdp"), None),
        P(("dp", "fsdp")),
        P(("dp", "fsdp")),
        P(),
        P(("dp", "fsdp"), None),
        P(("dp", "fsdp"), None),
        P(("dp", "fsdp"), None),
        P(("dp", "fsdp"), None),
        P(("dp", "fsdp"), None),
        P(("dp", "fsdp"), None),
        P(("dp", "fsdp"), None),
    )
    by_plane = mesh.shape["dp"] == EXPERTS and mesh.shape["fsdp"] == 8
    return jax.shard_map(
        plane_body if by_plane else body,
        mesh=mesh,
        in_specs=placed,
        out_specs=(
            P(("dp", "fsdp"), None),
            P(("dp", "fsdp"), None),
            P(("dp", "fsdp"), None),
            P(("dp", "fsdp"), None),
            P(("dp", "fsdp"), None),
            P(("dp", "fsdp"), None),
            P(("dp", "fsdp"), None),
            P(("dp", "fsdp"), None),
            P(),
        ),
        check_vma=False,
    )
```

```python
import functools

import jax
import jax.numpy as jnp
from jax import lax
from jax.experimental import pallas as pl
from jax.experimental.pallas import tpu as pltpu
from jax.sharding import PartitionSpec as P

D = 768
HEADS = 12
HEAD_DIM = 64
EXPERTS = 4
BLOCK = 128


EPSILON = 1e-05
NEGATIVE = -1e30


def layer_stats(values):
    average = jnp.mean(values, axis=-1, keepdims=True)
    centred = values - average
    scaled = lax.rsqrt(jnp.mean(centred * centred, axis=-1, keepdims=True) + EPSILON)
    return (centred * scaled, scaled)


def norm_backward(grad_normed, normal, scaled, gain_col):
    grad_scaled = grad_normed * gain_col
    first_mean = jnp.mean(grad_scaled, axis=-1, keepdims=True)
    second_mean = jnp.mean(grad_scaled * normal, axis=-1, keepdims=True)
    return scaled * (grad_scaled - first_mean - normal * second_mean)


def head_groups(heads):
    group_width = 4
    return [(start, start + group_width) for start in range(0, heads, group_width)]


def allowed_keys(length, seq_len):
    places = jnp.arange(seq_len, dtype=jnp.int32)
    return (places[None, :] <= places[:, None]) & (places[None, :] < length)


def masked_scores(query_part, key_part, allowed):
    scale = query_part.shape[-1] ** (-0.5)
    raw = (
        jnp.einsum("qhd,khd->hqk", query_part, key_part, preferred_element_type=jnp.float32) * scale
    )
    return jnp.where(allowed[None], raw, NEGATIVE)


def attention_forward(entry):
    queries, keys, values, length = entry
    allowed = allowed_keys(length, queries.shape[0])
    mixed_parts = []
    total_parts = []
    for start, finish in head_groups(queries.shape[1]):
        scores = masked_scores(queries[:, start:finish], keys[:, start:finish], allowed)
        highest = jnp.max(scores, axis=-1, keepdims=True)
        totals = highest + jnp.log(jnp.sum(jnp.exp(scores - highest), axis=-1, keepdims=True))
        weights = jnp.exp(scores - totals).astype(jnp.bfloat16)
        mixed_parts.append(
            jnp.einsum(
                "hqk,khd->qhd", weights, values[:, start:finish], preferred_element_type=jnp.float32
            ).astype(jnp.bfloat16)
        )
        total_parts.append(totals[..., 0])
    return (jnp.concatenate(mixed_parts, axis=1), jnp.concatenate(total_parts, axis=0))


def attention_backward(entry):
    queries, keys, values, totals, grad_mixed, length = entry
    allowed = allowed_keys(length, queries.shape[0])
    scale = queries.shape[-1] ** (-0.5)
    query_parts, key_parts, value_parts = ([], [], [])
    for start, finish in head_groups(queries.shape[1]):
        scores = masked_scores(queries[:, start:finish], keys[:, start:finish], allowed)
        weights = jnp.exp(scores - totals[start:finish][..., None])
        grad_weights = jnp.einsum(
            "qhd,khd->hqk",
            grad_mixed[:, start:finish],
            values[:, start:finish],
            preferred_element_type=jnp.float32,
        )
        inner_sum = jnp.sum(grad_weights * weights, axis=-1, keepdims=True)
        grad_scores = (weights * (grad_weights - inner_sum)).astype(jnp.bfloat16)
        value_parts.append(
            jnp.einsum(
                "hqk,qhd->khd",
                weights.astype(jnp.bfloat16),
                grad_mixed[:, start:finish],
                preferred_element_type=jnp.float32,
            )
        )
        query_parts.append(
            jnp.einsum(
                "hqk,khd->qhd",
                grad_scores,
                keys[:, start:finish],
                preferred_element_type=jnp.float32,
            )
            * scale
        )
        key_parts.append(
            jnp.einsum(
                "hqk,qhd->khd",
                grad_scores,
                queries[:, start:finish],
                preferred_element_type=jnp.float32,
            )
            * scale
        )
    return (
        jnp.concatenate(query_parts, axis=1),
        jnp.concatenate(key_parts, axis=1),
        jnp.concatenate(value_parts, axis=1),
    )


def segment_table(group_ends, total_rows, block_rows):
    block_count = total_rows // block_rows
    block_starts = jnp.arange(block_count, dtype=jnp.int32) * block_rows
    points = jnp.sort(jnp.concatenate([block_starts, group_ends]))
    finishes = jnp.concatenate([points[1:], jnp.full((1,), total_rows, jnp.int32)])
    blocks = jnp.minimum(points // block_rows, block_count - 1)
    owners = jnp.sum((group_ends[None, :] <= points[:, None]).astype(jnp.int32), axis=1)
    active = (finishes > points) & (owners < group_ends.shape[0])
    owners = jnp.minimum(owners, group_ends.shape[0] - 1)
    return (points, finishes, blocks, owners, active)


def expert_forward(sorted_rows, inner_all, outer_all, table, block_rows):
    model_width = sorted_rows.shape[1]
    hidden_width = inner_all.shape[1]

    def visit(state, entry):
        start, finish, block_id, owner, live = entry

        def compute(inner_state):
            pre_all, result_all = inner_state
            base = block_id * block_rows
            rows_here = lax.dynamic_slice_in_dim(sorted_rows, base, block_rows, 0)
            inner = lax.dynamic_slice_in_dim(inner_all, owner * model_width, model_width, 0)
            outer = lax.dynamic_slice_in_dim(outer_all, owner * hidden_width, hidden_width, 0)
            places = base + jnp.arange(block_rows, dtype=jnp.int32)
            inside = ((places >= start) & (places < finish))[:, None]
            pre = jnp.dot(rows_here, inner, preferred_element_type=jnp.float32)
            result = jnp.dot(
                jax.nn.gelu(pre).astype(jnp.bfloat16), outer, preferred_element_type=jnp.float32
            )
            old_pre = lax.dynamic_slice_in_dim(pre_all, base, block_rows, 0)
            old_result = lax.dynamic_slice_in_dim(result_all, base, block_rows, 0)
            pre_all = lax.dynamic_update_slice_in_dim(
                pre_all, jnp.where(inside, pre, old_pre), base, 0
            )
            result_all = lax.dynamic_update_slice_in_dim(
                result_all, jnp.where(inside, result, old_result), base, 0
            )
            return (pre_all, result_all)

        return (lax.cond(live, compute, lambda same: same, state), None)

    start_state = (
        jnp.zeros((sorted_rows.shape[0], hidden_width), jnp.float32),
        jnp.zeros((sorted_rows.shape[0], model_width), jnp.float32),
    )
    final_state, _ = lax.scan(visit, start_state, table)
    return final_state


def expert_backward(sorted_rows, pre_all, grad_sorted, inner_all, outer_all, table, block_rows):
    model_width = sorted_rows.shape[1]
    hidden_width = inner_all.shape[1]

    def visit(state, entry):
        start, finish, block_id, owner, live = entry

        def compute(inner_state):
            grad_rows, grad_inner, grad_outer = inner_state
            base = block_id * block_rows
            rows_here = lax.dynamic_slice_in_dim(sorted_rows, base, block_rows, 0)
            pre = lax.dynamic_slice_in_dim(pre_all, base, block_rows, 0)
            inner = lax.dynamic_slice_in_dim(inner_all, owner * model_width, model_width, 0)
            outer = lax.dynamic_slice_in_dim(outer_all, owner * hidden_width, hidden_width, 0)
            places = base + jnp.arange(block_rows, dtype=jnp.int32)
            inside = ((places >= start) & (places < finish))[:, None]
            grad_block = jnp.where(
                inside,
                lax.dynamic_slice_in_dim(grad_sorted, base, block_rows, 0),
                jnp.zeros((), jnp.bfloat16),
            )
            activated, gelu_pull = jax.vjp(jax.nn.gelu, pre)
            outer_piece = jnp.einsum(
                "tf,td->fd",
                activated.astype(jnp.bfloat16),
                grad_block,
                preferred_element_type=jnp.float32,
            )
            grad_act = jnp.einsum(
                "td,fd->tf", grad_block, outer, preferred_element_type=jnp.float32
            )
            grad_pre = gelu_pull(grad_act)[0].astype(jnp.bfloat16)
            inner_piece = jnp.einsum(
                "td,tf->df", rows_here, grad_pre, preferred_element_type=jnp.float32
            )
            rows_piece = jnp.einsum(
                "tf,df->td", grad_pre, inner, preferred_element_type=jnp.float32
            )
            old_rows = lax.dynamic_slice_in_dim(grad_rows, base, block_rows, 0)
            grad_rows = lax.dynamic_update_slice_in_dim(grad_rows, old_rows + rows_piece, base, 0)
            old_inner = lax.dynamic_slice_in_dim(grad_inner, owner * model_width, model_width, 0)
            grad_inner = lax.dynamic_update_slice_in_dim(
                grad_inner, old_inner + inner_piece, owner * model_width, 0
            )
            old_outer = lax.dynamic_slice_in_dim(grad_outer, owner * hidden_width, hidden_width, 0)
            grad_outer = lax.dynamic_update_slice_in_dim(
                grad_outer, old_outer + outer_piece, owner * hidden_width, 0
            )
            return (grad_rows, grad_inner, grad_outer)

        return (lax.cond(live, compute, lambda same: same, state), None)

    start_state = (
        jnp.zeros(sorted_rows.shape, jnp.float32),
        jnp.zeros(inner_all.shape, jnp.float32),
        jnp.zeros(outer_all.shape, jnp.float32),
    )
    final_state, _ = lax.scan(visit, start_state, table)
    return final_state


def body(
    tokens,
    token_ids,
    lengths,
    hash_table,
    w_qkv,
    w_attn_out,
    norm_gains,
    norm_biases,
    w_in,
    w_out,
    cotangent,
):
    rows_count = tokens.shape[0]
    seq_count = lengths.shape[0]
    seq_len = rows_count // seq_count
    model_width = D
    expert_total = EXPERTS
    qkv_full, proj_full, gains_full, biases_full = (
        lax.all_gather(w_qkv, ("dp", "fsdp"), axis=0, tiled=True),
        lax.all_gather(w_attn_out, ("dp", "fsdp"), axis=0, tiled=True),
        lax.all_gather(norm_gains, ("dp", "fsdp"), axis=0, tiled=True),
        lax.all_gather(norm_biases, ("dp", "fsdp"), axis=0, tiled=True),
    )
    gains_f = gains_full.astype(jnp.float32)
    biases_f = biases_full.astype(jnp.float32)
    inputs = tokens.astype(jnp.float32)
    normal_one, scaled_one = layer_stats(inputs)
    first_in = (normal_one * gains_f[:, 0] + biases_f[:, 0]).astype(jnp.bfloat16)
    qkv_low = jnp.dot(first_in, qkv_full, preferred_element_type=jnp.float32).astype(jnp.bfloat16)
    packed = qkv_low.reshape(seq_count, seq_len, 3, HEADS, HEAD_DIM)
    queries = packed[:, :, 0]
    keys = packed[:, :, 1]
    values = packed[:, :, 2]
    mixed, totals = lax.map(attention_forward, (queries, keys, values, lengths))
    mixed_flat = mixed.reshape(rows_count, model_width)
    hidden = inputs + jnp.dot(mixed_flat, proj_full, preferred_element_type=jnp.float32)
    normal_two, scaled_two = layer_stats(hidden)
    second_in = (normal_two * gains_f[:, 1] + biases_f[:, 1]).astype(jnp.bfloat16)
    places = jnp.arange(rows_count, dtype=jnp.int32) % seq_len
    used = places < jnp.repeat(lengths, seq_len, total_repeat_length=rows_count)
    expert_ids = jnp.where(used, hash_table[token_ids], expert_total)
    matches = (expert_ids[:, None] == jnp.arange(expert_total, dtype=jnp.int32)[None, :]).astype(
        jnp.int32
    )
    local_counts = jnp.sum(matches, axis=0)
    expert_counts = lax.psum(local_counts, ("dp", "fsdp"))
    ordering = jnp.argsort(expert_ids, stable=True)
    inverse = (
        jnp.zeros((rows_count,), jnp.int32)
        .at[ordering]
        .set(jnp.arange(rows_count, dtype=jnp.int32))
    )
    group_ends = jnp.cumsum(local_counts)
    table = segment_table(group_ends, rows_count, BLOCK)
    inner_all, outer_all = (
        lax.all_gather(w_in, ("dp", "fsdp"), axis=0, tiled=True),
        lax.all_gather(w_out, ("dp", "fsdp"), axis=0, tiled=True),
    )
    sorted_rows = second_in[ordering]
    pre_all, result_sorted = expert_forward(sorted_rows, inner_all, outer_all, table, BLOCK)
    layer_out = (hidden + result_sorted[inverse]).astype(jnp.bfloat16)
    grad_out = cotangent.astype(jnp.float32)
    grad_sorted = cotangent[ordering]
    inner_back, outer_back = (
        lax.all_gather(w_in, ("dp", "fsdp"), axis=0, tiled=True),
        lax.all_gather(w_out, ("dp", "fsdp"), axis=0, tiled=True),
    )
    grad_rows_sorted, grad_inner, grad_outer = expert_backward(
        sorted_rows, pre_all, grad_sorted, inner_back, outer_back, table, BLOCK
    )
    grad_w_in, grad_w_out = (
        lax.psum_scatter(grad_inner, ("dp", "fsdp"), scatter_dimension=0, tiled=True),
        lax.psum_scatter(grad_outer, ("dp", "fsdp"), scatter_dimension=0, tiled=True),
    )
    grad_second = grad_rows_sorted[inverse]
    gain_two = jnp.sum(grad_second * normal_two, axis=0)
    bias_two = jnp.sum(grad_second, axis=0)
    grad_hidden = grad_out + norm_backward(grad_second, normal_two, scaled_two, gains_f[:, 1])
    grad_branch = grad_hidden.astype(jnp.bfloat16)
    qkv_back, proj_back = (
        lax.all_gather(w_qkv, ("dp", "fsdp"), axis=0, tiled=True),
        lax.all_gather(w_attn_out, ("dp", "fsdp"), axis=0, tiled=True),
    )
    grad_proj = jnp.einsum("td,te->de", mixed_flat, grad_branch, preferred_element_type=jnp.float32)
    grad_mixed = jnp.einsum(
        "te,de->td", grad_branch, proj_back, preferred_element_type=jnp.float32
    ).astype(jnp.bfloat16)
    grad_mixed = grad_mixed.reshape(seq_count, seq_len, HEADS, HEAD_DIM)
    grad_queries, grad_keys, grad_values = lax.map(
        attention_backward, (queries, keys, values, totals, grad_mixed, lengths)
    )
    grad_qkv = (
        jnp.stack([grad_queries, grad_keys, grad_values], axis=2)
        .reshape(rows_count, 3 * model_width)
        .astype(jnp.bfloat16)
    )
    grad_qkv_w = jnp.einsum("td,te->de", first_in, grad_qkv, preferred_element_type=jnp.float32)
    grad_first = jnp.einsum("te,de->td", grad_qkv, qkv_back, preferred_element_type=jnp.float32)
    gain_one = jnp.sum(grad_first * normal_one, axis=0)
    bias_one = jnp.sum(grad_first, axis=0)
    grad_tokens = grad_hidden + norm_backward(grad_first, normal_one, scaled_one, gains_f[:, 0])
    grad_gains = jnp.stack([gain_one, gain_two], axis=1)
    grad_biases = jnp.stack([bias_one, bias_two], axis=1)
    grad_w_qkv, grad_w_attn_out, grad_norm_gains, grad_norm_biases = (
        lax.psum_scatter(grad_qkv_w, ("dp", "fsdp"), scatter_dimension=0, tiled=True),
        lax.psum_scatter(grad_proj, ("dp", "fsdp"), scatter_dimension=0, tiled=True),
        lax.psum_scatter(grad_gains, ("dp", "fsdp"), scatter_dimension=0, tiled=True),
        lax.psum_scatter(grad_biases, ("dp", "fsdp"), scatter_dimension=0, tiled=True),
    )
    return (
        layer_out,
        grad_tokens,
        grad_w_qkv,
        grad_w_attn_out,
        grad_norm_gains,
        grad_norm_biases,
        grad_w_in,
        grad_w_out,
        expert_counts,
    )


LOG2E = 1.4426950408889634
ROWS = 256
GROUP = 16
MIB = 1024 * 1024
NT = (((1,), (1,)), ((), ()))
NN = (((1,), (0,)), ((), ()))
ROOT = 0.7978845608028654
CUBIC = 0.044715


def mul(a, b, dims=NN):
    return lax.dot_general(a, b, dims, preferred_element_type=jnp.float32)


def iota(shape, dim):
    return lax.broadcasted_iota(jnp.int32, shape, dim)


def padded_rows(slots):
    return slots + EXPERTS * GROUP


def three_parts(v):
    first = v.astype(jnp.bfloat16)
    rest = v - first.astype(jnp.float32)
    second = rest.astype(jnp.bfloat16)
    third = (rest - second.astype(jnp.float32)).astype(jnp.bfloat16)
    return first, second, third


def own_lanes(lane, half):
    return (lane < HEAD_DIM) if half == 0 else (lane >= HEAD_DIM)


def extra_lane(half):
    return HEAD_DIM if half == 0 else 0


def routing(ids, table, length, perm_ref):
    slots = ids.shape[1]
    chosen = (iota((table.shape[1], slots), 0) == (ids >> 7)).astype(jnp.bfloat16)
    rows = mul(table, chosen)
    expert = jnp.sum(
        jnp.where(iota(rows.shape, 0) == (ids & 127), rows, 0.0), axis=0, keepdims=True
    ).astype(jnp.int32)
    used = iota((1, slots), 1) < length
    member = (iota((8, slots), 0) == expert) & used
    member_f = jnp.where(member, 1.0, 0.0)
    perm_ref[0:slots, :] = (iota((slots, slots), 0) <= iota((slots, slots), 1)).astype(jnp.bfloat16)
    rank = mul(member_f.astype(jnp.bfloat16), perm_ref[0:slots, :])
    counts = rank[:, slots - 1 : slots]
    groups = jnp.floor((counts + (GROUP - 1)) * (1.0 / GROUP))
    row8 = iota((8, 1), 0)
    start = jnp.zeros((8, 1), jnp.float32)
    for e in range(EXPERTS - 1):
        start = start + jnp.where(row8 > e, groups[e : e + 1, :], 0.0)
    place = jnp.sum(member_f * (rank - 1.0 + start * GROUP), axis=0, keepdims=True)
    place = jnp.where(used, place, -1.0)
    return place, counts, groups


MESH = pl.DeviceIdType.MESH
HALF = 1664
WIDE = 2 * HALF


class Place:
    def __init__(self):
        self.z = lax.axis_index("dp")
        f = lax.axis_index("fsdp")
        self.y = f // 4
        self.x = (f // 2) % 2
        self.c = f % 2

    def at(self, z=None, y=None, x=None, c=None):
        z = self.z if z is None else z
        y = self.y if y is None else y
        x = self.x if x is None else x
        c = self.c if c is None else c
        return (z, 4 * y + 2 * x + c)

    def greet(self, peers):
        barrier = pltpu.get_barrier_semaphore()
        for peer in peers:
            pl.semaphore_signal(barrier, inc=1, device_id=peer, device_id_type=MESH)
        pl.semaphore_wait(barrier, len(peers))


def push(src, dst, send, recv, peer):
    return pltpu.make_async_remote_copy(
        src_ref=src, dst_ref=dst, send_sem=send, recv_sem=recv, device_id=peer, device_id_type=MESH
    )


def front_kernel(
    len_ref, x_ref, ids_ref, table_ref, g_ref, local_ref, win_ref, wout_ref,
    qkv_ref, mixed_ref, aug_ref, hidden_ref, xs_ref, gs_ref, w_ref, wa_ref, norms_ref, pos_ref, counts_ref,
    perm_ref, normed_ref, qa_ref, ka_ref, va_ref, tokx_ref, tokg_ref, sib_ref,
    sem0, sz, rz, sy, ry, sx, rx, sd, rd, ss, rs,
    tok_local, tok_send, tok_recv,
    lane_local, lane_send, lane_recv, up_send, down_send, line_recv, y_send, y_recv,
):
    slots, width = x_ref.shape
    heads = width // HEAD_DIM
    rp = padded_rows(slots)
    length = len_ref[0]
    me = Place()
    z, y, x, c = me.z, me.y, me.x, me.c
    depth = 4
    sibling, beside, across = me.at(c=1 - c), me.at(x=1 - x), me.at(y=1 - y)
    me.greet([sibling, beside, across, me.at(x=1 - x, c=1 - c)] + [me.at(z=z ^ k) for k in range(1, depth)])

    first = push(local_ref, sib_ref, sem0.at[0], sem0.at[1], sibling)
    first.start()

    def block(zz, yy, xx):
        rows = pl.ds(pl.multiple_of(48 * (4 * zz + 2 * yy + xx), 48), 48)
        return wa_ref.at[rows, pl.ds(pl.multiple_of(c * HALF, 128), HALF)]

    def share(zz, yy, xx, send, recv, peer):
        ref = block(zz, yy, xx)
        return push(ref, ref, send, recv, peer)

    def z_copy(k, source):
        return share(source, y, x, sz.at[k - 1], rz.at[source], me.at(z=z ^ k))

    def y_copy(zz, source_y):
        return share(zz, source_y, x, sy.at[zz], ry.at[zz], across)

    def x_copy(zz, source_x):
        return share(zz, y, source_x, sx.at[zz], rx.at[zz], beside)

    def d_copy_x(zz, yy, xx):
        return share(zz, yy, xx, sd.at[zz], rd.at[zz], beside)

    def d_copy_y(zz, yy, xx):
        return share(zz, yy, xx, sd.at[zz], rd.at[zz], across)

    def s_copy(zz, side):
        ref = wa_ref.at[pl.ds(pl.multiple_of(192 * zz, 192), 192), pl.ds(pl.multiple_of(side * HALF, 128), HALF)]
        return push(ref, ref, ss.at[zz], rs.at[zz], sibling)

    part = wout_ref.shape[0]
    rows_in = win_ref.shape[0]
    lanes = [(1 - x, c), (x, 1 - c), (1 - x, 1 - c)]

    def lane_cols(b, xx, cc):
        return win_ref.at[:, pl.ds(pl.multiple_of(part * (4 * b + 2 * xx + cc), 128), part)]

    def lane_home(b, xx, cc):
        return w_ref.at[0, z, y, pl.ds(pl.multiple_of(rows_in * (2 * xx + cc), rows_in), rows_in), pl.ds(b * part, part)]

    def lane_copy(i, b, arrive):
        xx, cc = lanes[i]
        home = lane_home(b, xx, cc) if arrive else lane_home(b, x, c)
        return push(lane_cols(b, xx, cc), home, lane_send.at[i, b], lane_recv.at[i, b], me.at(x=xx, c=cc))

    def lane_own(b):
        return pltpu.make_async_copy(lane_cols(b, x, c), lane_home(b, x, c), lane_local.at[b])

    own_out = pltpu.make_async_copy(wout_ref, w_ref.at[1, z, y], lane_local.at[2])

    def shard(k, zz, yy):
        return w_ref.at[k, zz, yy]

    def up_copy(k, zz):
        return push(shard(k, zz, y), shard(k, zz, y), up_send.at[k, zz], line_recv.at[k, zz], me.at(z=jnp.minimum(z + 1, depth - 1)))

    def down_copy(k, zz):
        return push(shard(k, zz, y), shard(k, zz, y), down_send.at[k, zz], line_recv.at[k, zz], me.at(z=jnp.maximum(z - 1, 0)))

    def over_copy(k, zz, yy):
        return push(shard(k, zz, yy), shard(k, zz, yy), y_send.at[k, zz], y_recv.at[k, zz], across)

    def spread(k):
        @pl.when(z < depth - 1)
        def _():
            up_copy(k, z).start()

        @pl.when(z > 0)
        def _():
            down_copy(k, z).start()

        over_copy(k, z, y).start()

    def relay(k, s):
        @pl.when(z >= s)
        def _():
            up_copy(k, z - s).wait_recv()

            @pl.when(z < depth - 1)
            def _():
                up_copy(k, z - s).start()

            over_copy(k, z - s, y).start()

        @pl.when(z + s < depth)
        def _():
            down_copy(k, z + s).wait_recv()

            @pl.when(z > 0)
            def _():
                down_copy(k, z + s).start()

            over_copy(k, z + s, y).start()

    def weights_start():
        for i in range(3):
            for b in range(2):
                lane_copy(i, b, False).start()
        spread(1)

    def weights_lane():
        for i in range(3):
            for b in range(2):
                lane_copy(i, b, True).wait_recv()
        for b in range(2):
            lane_own(b).wait()
        spread(0)

    ticks = [weights_lane] + [functools.partial(relay, k, s) for s in range(1, depth) for k in (1, 0)]

    def weights_end():
        for k in (1, 0):
            for zz in range(depth):
                over_copy(k, zz, 1 - y).wait()
                for copy, stop in ((up_copy, depth - 1), (down_copy, 0)):
                    inside = (zz <= z) if stop else (zz >= z)

                    @pl.when(inside & (z != stop))
                    def _():
                        copy(k, zz).wait_send()

        for i in range(3):
            for b in range(2):
                lane_copy(i, b, False).wait_send()

    mine = 2 * x + c

    def tok_copies(k, scratch, far_ref):
        own = pltpu.make_async_copy(scratch, far_ref.at[mine], tok_local.at[k])
        near = push(scratch, far_ref.at[mine], tok_send.at[k, 0], tok_recv.at[k, 0], sibling)
        far = push(scratch, far_ref.at[mine], tok_send.at[k, 1], tok_recv.at[k, 1], beside)
        slot = far_ref.at[2 * (1 - x) + c]
        onward = push(slot, slot, tok_send.at[k, 2], tok_recv.at[k, 2], sibling)
        return own, near, far, onward

    x_copies = tok_copies(0, tokx_ref, xs_ref)
    g_copies = tok_copies(1, tokg_ref, gs_ref)

    first.wait_recv()
    zero_core = c == 0
    own_cols = pl.ds(pl.multiple_of(c * HALF, 128), HALF)
    local = local_ref[0:24, own_cols]
    other = sib_ref[0:24, own_cols]
    own_rows = pl.ds(pl.multiple_of(48 * (4 * z + 2 * y + x), 48), 48)
    wa_ref[own_rows, own_cols] = jnp.concatenate(
        [jnp.where(zero_core, local, other), jnp.where(zero_core, other, local)], axis=0
    )
    for k in range(1, depth):
        z_copy(k, z).start()
    y_copy(z, y).start()
    x_copy(z, x).start()
    for b in range(2):
        lane_own(b).start()
    own_out.start()

    place, counts, groups = routing(ids_ref[...], table_ref[...], length, perm_ref)
    place_i = place.astype(jnp.int32)
    pos_ref[...] = jnp.broadcast_to(place, (128, slots)).T
    counts_ref[...] = jnp.broadcast_to(counts, (8, 128)).astype(jnp.int32)

    for k in range(1, depth):
        zz = z ^ k
        z_copy(k, zz).wait_recv()
        y_copy(zz, y).start()
        x_copy(zz, x).start()

    step = rp // 4

    @pl.loop(0, 4)
    def _(i):
        base = i * step
        perm_ref[pl.ds(base, step), :] = (
            iota((step, slots), 0) + base == place_i
        ).astype(jnp.bfloat16)

    for k in range(depth):
        zz = z ^ k
        y_copy(zz, 1 - y).wait_recv()
        x_copy(zz, 1 - x).wait_recv()

        @pl.when(zz % 2 == 0)
        def _():
            d_copy_x(zz, 1 - y, x).start()

        @pl.when(zz % 2 == 1)
        def _():
            d_copy_y(zz, y, 1 - x).start()

    own_out.wait()
    weights_start()

    @pl.loop(0, 4)
    def _(i):
        rows = pl.ds(i * step, step)
        tokg_ref[rows, :] = mul(perm_ref[rows, :], g_ref[...]).astype(jnp.bfloat16)

    tail = jnp.broadcast_to(jnp.concatenate([groups, groups], axis=0), (GROUP, width)).astype(jnp.bfloat16)
    tokx_ref[rp : rp + GROUP, :] = tail
    tokg_ref[rp : rp + GROUP, :] = tail

    for k in range(depth):
        zz = z ^ k
        d_copy_x(zz, 1 - y, 1 - x).wait_recv()
        s_copy(zz, c).start()
    for k in range(depth):
        s_copy(z ^ k, 1 - c).wait_recv()
    for copy in g_copies[:3]:
        copy.start()

    cols_t = wa_ref[:, 2 * width : 2 * width + 128].astype(jnp.float32).T
    norms_ref[...] = cols_t[0:8, :]

    @pl.loop(0, slots // ROWS)
    def _(i):
        rows = pl.ds(i * ROWS, ROWS)
        normal, _ = layer_stats(x_ref[rows, :].astype(jnp.float32))
        normed = (normal * norms_ref[0:1, :] + norms_ref[2:3, :]).astype(jnp.bfloat16)
        for part_i, start in enumerate((0, width, HALF)):
            cols = slice(part_i * width, (part_i + 1) * width)
            qkv_ref[rows, cols] = mul(normed, wa_ref[:, start : start + width]).astype(jnp.bfloat16)

    lane = iota((slots, 128), 1)
    key_bias = jnp.where(iota((slots, 128), 0) < length, 0.0, NEGATIVE).astype(jnp.bfloat16)
    causal = iota((ROWS, ROWS), 1) <= iota((ROWS, ROWS), 0)
    lane_b = iota((ROWS, 128), 1)
    pairs = heads // 2
    slots_for = [[] for _ in range(pairs)]
    for i, tick in enumerate(ticks[:pairs]):
        slots_for[i].append(tick)

    @pl.loop(0, pairs)
    def _(p):
        cols = pl.ds(p * 128, 128)
        q = qkv_ref[:, cols].astype(jnp.float32) * (HEAD_DIM ** -0.5 * LOG2E)
        q_hi = q.astype(jnp.bfloat16)
        q_lo = (q - q_hi.astype(jnp.float32)).astype(jnp.bfloat16)
        k = qkv_ref[:, pl.ds(width + p * 128, 128)]
        v = qkv_ref[:, pl.ds(2 * width + p * 128, 128)]
        zero = jnp.zeros_like(q_hi)
        one = jnp.ones_like(q_hi)
        for half in range(2):
            own = own_lanes(lane, half)
            extra = extra_lane(half)
            qa_ref[half, :, 0:128] = jnp.where(own, q_hi, zero)
            qa_ref[half, :, 128:256] = jnp.where(own, q_lo, jnp.where(lane == extra, one, zero))
            ka_ref[half, :, 0:128] = k
            ka_ref[half, :, 128:256] = jnp.where(own, k, jnp.where(lane == extra, key_bias, zero))
            va_ref[half, :, :] = jnp.where(own, v, one)
        for i in range(slots // ROWS):
            rows = slice(i * ROWS, (i + 1) * ROWS)
            keys = (i + 1) * ROWS
            outs = []
            for half in range(2):
                s = mul(qa_ref[half, rows, :], ka_ref[half, 0:keys, :], NT)
                diag = jnp.where(causal, s[:, i * ROWS :], NEGATIVE)
                s = diag if i == 0 else jnp.concatenate([s[:, : i * ROWS], diag], axis=1)
                top = jnp.max(s, axis=1, keepdims=True)
                probs = jnp.exp2(s - top).astype(jnp.bfloat16)
                out = mul(probs, va_ref[half, 0:keys, :])
                total = pltpu.roll(out, HEAD_DIM, 1)
                outs.append(out / total)
                minus = -(top + jnp.log2(out))
                a, b, d = three_parts(minus)
                extra = extra_lane(half)
                seen = qa_ref[half, rows, 128:256]
                seen = jnp.where(lane_b == extra + 1, a, seen)
                seen = jnp.where(lane_b == extra + 2, b, seen)
                seen = jnp.where(lane_b == extra + 3, d, seen)
                aug_ref[2 * p + half, rows, :] = seen
            mixed_ref[rows, cols] = jnp.where(lane_b < HEAD_DIM, outs[0], outs[1]).astype(jnp.bfloat16)
        for i in range(pairs):
            @pl.when(p == i)
            def _():
                for tick in slots_for[i]:
                    tick()

    @pl.loop(0, slots // ROWS)
    def _(i):
        rows = pl.ds(i * ROWS, ROWS)
        hidden = x_ref[rows, :].astype(jnp.float32) + mul(mixed_ref[rows, :], wa_ref[:, HALF + width : HALF + 2 * width])
        hidden_ref[rows, :] = hidden
        normal, _ = layer_stats(hidden)
        normed_ref[rows, :] = (normal * norms_ref[1:2, :] + norms_ref[3:4, :]).astype(jnp.bfloat16)

    @pl.loop(0, 4)
    def _(i):
        rows = pl.ds(i * step, step)
        tokx_ref[rows, :] = mul(perm_ref[rows, :], normed_ref[...]).astype(jnp.bfloat16)

    for copy in x_copies[:3]:
        copy.start()
    g_copies[2].wait_recv()
    g_copies[3].start()
    for tick in ticks[pairs:]:
        tick()
    x_copies[2].wait_recv()
    x_copies[3].start()
    weights_end()
    for own, near, far, onward in (x_copies, g_copies):
        own.wait()
        near.wait()
        far.wait_send()
        onward.wait()
    first.wait_send()
    for k in range(1, depth):
        z_copy(k, z).wait_send()
    for zz in range(depth):
        y_copy(zz, y).wait_send()
        x_copy(zz, x).wait_send()
        d_copy_x(zz, y, x).wait_send()
        s_copy(zz, c).wait_send()


def front(length, x, ids, table, g, local, w_in, w_out):
    slots, width = x.shape
    rp = padded_rows(slots)
    part = w_out.shape[0]
    bf = jnp.bfloat16
    f32 = jnp.float32
    whole = pl.BlockSpec(memory_space=pltpu.VMEM)
    far = pl.BlockSpec(memory_space=pl.ANY)
    dma = pltpu.SemaphoreType.DMA
    return pl.pallas_call(
        front_kernel,
        out_shape=(
            jax.ShapeDtypeStruct((slots, 3 * width), bf),
            jax.ShapeDtypeStruct((slots, width), bf),
            jax.ShapeDtypeStruct((HEADS, slots, 128), bf),
            jax.ShapeDtypeStruct((slots, width), f32),
            jax.ShapeDtypeStruct((4, rp + GROUP, width), bf),
            jax.ShapeDtypeStruct((4, rp + GROUP, width), bf),
            jax.ShapeDtypeStruct((2, EXPERTS, 2, part, width), bf),
            jax.ShapeDtypeStruct((width, WIDE), bf),
            jax.ShapeDtypeStruct((8, width), f32),
            jax.ShapeDtypeStruct((slots, 128), f32),
            jax.ShapeDtypeStruct((8, 128), jnp.int32),
        ),
        in_specs=[pl.BlockSpec(memory_space=pltpu.SMEM)] + [whole] * 5 + [far] * 2,
        out_specs=(whole, whole, whole, whole, far, far, far, whole, whole, whole, whole),
        scratch_shapes=[
            pltpu.VMEM((rp, slots), bf),
            pltpu.VMEM((slots, width), bf),
            pltpu.VMEM((2, slots, 256), bf),
            pltpu.VMEM((2, slots, 256), bf),
            pltpu.VMEM((2, slots, 128), bf),
            pltpu.VMEM((rp + GROUP, width), bf),
            pltpu.VMEM((rp + GROUP, width), bf),
            pltpu.VMEM((32, WIDE), bf),
            dma((2,)), dma((3,)), dma((4,)), dma((4,)), dma((4,)), dma((4,)), dma((4,)), dma((4,)), dma((4,)),
            dma((4,)), dma((4,)),
            dma((2,)), dma((2, 3)), dma((2, 3)),
            dma((3,)), dma((3, 2)), dma((3, 2)), dma((2, 4)), dma((2, 4)), dma((2, 4)), dma((2, 4)), dma((2, 4)),
        ],
        compiler_params=pltpu.CompilerParams(vmem_limit_bytes=56 * MIB, collective_id=0, has_side_effects=True),
        name="front",
    )(length, x, ids, table, g, local, w_in, w_out)


CHUNK = 32


def experts_kernel(
    n_ref, x_ref, g_ref, w1_ref, w2_ref,
    o_ref, dx_ref, gw1_ref, gw2_ref,
    xb, gb, ob, db, acc1, acc2, blank, sem_in, sem_out, sem_zero,
):
    sources, groups, _, width = x_ref.shape
    groups = groups - 1
    hidden = w2_ref.shape[1]
    rows = CHUNK * GROUP

    blank[...] = jnp.zeros_like(blank)
    xb[...] = jnp.zeros_like(xb)
    gw1_ref[...] = jnp.zeros_like(gw1_ref)
    gw2_ref[...] = jnp.zeros_like(gw2_ref)

    totals = []
    for e in range(EXPERTS):
        totals.append(lax.fori_loop(0, sources, lambda s, t, e=e: t + n_ref[s * EXPERTS + e], 0))
    first = [0]
    for e in range(EXPERTS):
        first.append(first[-1] + (totals[e] + (CHUNK - 1)) // CHUNK)
    chunks = first[EXPERTS]

    def pick(values, e):
        out = values[0]
        for i in range(1, EXPERTS):
            out = jnp.where(e == i, values[i], out)
        return out

    def locate(c):
        e = jnp.int32(0)
        for i in range(1, EXPERTS):
            e = e + jnp.where(c >= first[i], 1, 0)
        begin = (c - pick(first, e)) * CHUNK
        return e, begin, jnp.minimum(begin + CHUNK, pick(totals, e))

    def pieces(c, act):
        e, begin, end = locate(c)

        def visit(s, base):
            n = n_ref[s * EXPERTS + e]
            low = jnp.maximum(base, begin)
            size = jnp.minimum(base + n, end) - low
            skip = jnp.int32(0)
            for i in range(EXPERTS - 1):
                skip = skip + jnp.where(e > i, n_ref[s * EXPERTS + i], 0)

            @pl.when(size > 0)
            def _():
                act(s, skip + low - base, low - begin, size)

            return base + n

        lax.fori_loop(0, sources, visit, jnp.int32(0))

    def load(c, slot):
        def act(s, at, to, size):
            for k, (src, dst) in enumerate(((x_ref, xb), (g_ref, gb))):
                pltpu.make_async_copy(
                    src.at[s, pl.ds(at, size)], dst.at[slot, pl.ds(to, size)], sem_in.at[k, slot]
                ).start()

        pieces(c, act)

    def store(c, slot):
        def act(s, at, to, size):
            for k, (src, dst) in enumerate(((ob, o_ref), (db, dx_ref))):
                pltpu.make_async_copy(
                    src.at[slot, pl.ds(to, size)], dst.at[s, pl.ds(at, size)], sem_out.at[k, slot]
                ).start()

        pieces(c, act)

    def settle(c, slot, bufs, sems):
        _, begin, end = locate(c)
        for k, buf in enumerate(bufs):
            part = buf.at[slot, pl.ds(0, end - begin)]
            pltpu.make_async_copy(part, part, sems.at[k, slot]).wait()

    def used_groups(s):
        t = n_ref[s * EXPERTS]
        for e in range(1, EXPERTS):
            t = t + n_ref[s * EXPERTS + e]
        return t

    def rest(s, act):
        t = used_groups(s)

        @pl.when(groups - t > 0)
        def _():
            for k, dst in enumerate((o_ref, dx_ref)):
                act(
                    pltpu.make_async_copy(
                        blank.at[pl.ds(0, groups - t)], dst.at[s, pl.ds(t, groups - t)], sem_zero.at[k, s]
                    )
                )

    @pl.loop(0, sources)
    def _(s):
        rest(s, lambda copy: copy.start())

    @pl.when(chunks > 0)
    def _():
        load(0, 0)

    @pl.loop(0, chunks)
    def _(c):
        slot = c % 2
        e, begin, end = locate(c)

        @pl.when(c + 1 < chunks)
        def _():
            load(c + 1, 1 - slot)

        settle(c, slot, (xb, gb), sem_in)

        @pl.when(c >= 2)
        def _():
            settle(c - 2, slot, (ob, db), sem_out)

        x = xb[slot].reshape(rows, width)
        g = gb[slot].reshape(rows, width)
        g = jnp.where(iota((rows, width), 0) < (end - begin) * GROUP, g, jnp.zeros_like(g))
        w1 = w1_ref[e]
        w2 = w2_ref[e]
        pre = mul(x, w1)
        square = pre * pre
        t = jnp.tanh(ROOT * pre * (1.0 + CUBIC * square))
        act = (0.5 * pre * (1.0 + t)).astype(jnp.bfloat16)
        slope = 0.5 * (1.0 + t) + 0.5 * pre * (1.0 - t * t) * (ROOT * (1.0 + 3.0 * CUBIC * square))
        grad_pre = (slope * mul(g, w2, NT)).astype(jnp.bfloat16)
        ob[slot] = mul(act, w2).astype(jnp.bfloat16).reshape(CHUNK, GROUP, width)
        db[slot] = mul(grad_pre, w1, NT).astype(jnp.bfloat16).reshape(CHUNK, GROUP, width)
        store(c, slot)
        add1 = mul(x.T, grad_pre)
        add2 = mul(act.T, g)

        @pl.when(begin == 0)
        def _():
            acc1[...] = add1
            acc2[...] = add2

        @pl.when(begin > 0)
        def _():
            acc1[...] += add1
            acc2[...] += add2

        @pl.when(end == pick(totals, e))
        def _():
            gw1_ref[e] = acc1[...].astype(gw1_ref.dtype)
            gw2_ref[e] = acc2[...].astype(gw2_ref.dtype)

    @pl.when(chunks >= 2)
    def _():
        settle(chunks - 2, chunks % 2, (ob, db), sem_out)

    @pl.when(chunks >= 1)
    def _():
        settle(chunks - 1, (chunks - 1) % 2, (ob, db), sem_out)

    @pl.loop(0, sources)
    def _(s):
        rest(s, lambda copy: copy.wait())


def experts(n16, xs, gs, w1, w2):
    sources, groups, _, width = xs.shape
    hidden = w2.shape[1]
    bf = jnp.bfloat16
    whole = pl.BlockSpec(memory_space=pltpu.VMEM)
    far = pl.BlockSpec(memory_space=pl.ANY)
    out_rows = jax.ShapeDtypeStruct((sources, groups - 1, GROUP, width), bf)
    return pl.pallas_call(
        experts_kernel,
        out_shape=(
            out_rows, out_rows,
            jax.ShapeDtypeStruct((EXPERTS, width, hidden), bf),
            jax.ShapeDtypeStruct((EXPERTS, hidden, width), bf),
        ),
        in_specs=[pl.BlockSpec(memory_space=pltpu.SMEM), far, far, whole, whole],
        out_specs=(far, far, whole, whole),
        scratch_shapes=[pltpu.VMEM((2, CHUNK, GROUP, width), bf)] * 4
        + [pltpu.VMEM((width, hidden), jnp.float32), pltpu.VMEM((hidden, width), jnp.float32)]
        + [pltpu.VMEM((groups - 1, GROUP, width), bf)]
        + [pltpu.SemaphoreType.DMA((2, 2)), pltpu.SemaphoreType.DMA((2, 2)), pltpu.SemaphoreType.DMA((2, sources))],
        compiler_params=pltpu.CompilerParams(vmem_limit_bytes=56 * MIB),
        name="experts",
    )(n16, xs, gs, w1, w2)


def back_kernel(
    len_ref, x_ref, g_ref, hidden_ref, qkv_ref, mixed_ref, aug_ref, pos_ref, dxs_ref, os_ref, wa_ref, norms_ref,
    out_ref, gx_ref, gwa_ref, gn_ref,
    branch_ref, gmix_ref, gqkv_ref, tr_ref, qa_ref, ka_ref, va_ref, oa_ref, dv_ref, dk_ref, dq_ref,
):
    slots, width = x_ref.shape
    heads = width // HEAD_DIM
    rp = dxs_ref.shape[0]
    length = len_ref[0]
    scale = HEAD_DIM ** -0.5
    gn_ref[...] = jnp.zeros_like(gn_ref)

    @pl.loop(0, slots // ROWS)
    def _(i):
        rows = pl.ds(i * ROWS, ROWS)
        place = pos_ref[rows, 0:1].astype(jnp.int32)
        pick = (iota((ROWS, rp), 1) == place).astype(jnp.bfloat16)
        hidden = hidden_ref[rows, :]
        out_ref[rows, :] = (hidden + mul(pick, os_ref[...])).astype(jnp.bfloat16)
        grad = mul(pick, dxs_ref[...])
        normal, scaled = layer_stats(hidden)
        gn_ref[1:2, :] += jnp.sum(grad * normal, axis=0, keepdims=True)
        gn_ref[3:4, :] += jnp.sum(grad, axis=0, keepdims=True)
        grad_hidden = g_ref[rows, :].astype(jnp.float32) + norm_backward(grad, normal, scaled, norms_ref[1:2, :])
        gx_ref[rows, :] = grad_hidden
        branch = grad_hidden.astype(jnp.bfloat16)
        branch_ref[rows, :] = branch
        gmix_ref[rows, :] = mul(branch, wa_ref[:, HALF + width : HALF + 2 * width], NT).astype(jnp.bfloat16)

    tr_ref[...] = mixed_ref[...].T
    tile = width // 3

    @pl.loop(0, 3)
    def _(i):
        rows = pl.ds(i * tile, tile)
        gwa_ref[rows, 3 * width :] = mul(tr_ref[rows, :], branch_ref[...]).astype(gwa_ref.dtype)

    lane = iota((slots, 128), 1)
    key_bias = jnp.where(iota((slots, 128), 0) < length, 0.0, NEGATIVE).astype(jnp.bfloat16)
    causal = iota((ROWS, ROWS), 0) <= iota((ROWS, ROWS), 1)

    @pl.loop(0, heads // 2)
    def _(p):
        cols = pl.ds(p * 128, 128)
        q = qkv_ref[:, cols]
        q_hi = (q.astype(jnp.float32) * (scale * LOG2E)).astype(jnp.bfloat16)
        k = qkv_ref[:, pl.ds(width + p * 128, 128)]
        v = qkv_ref[:, pl.ds(2 * width + p * 128, 128)]
        do = gmix_ref[:, cols]
        prod = do.astype(jnp.float32) * mixed_ref[:, cols].astype(jnp.float32)
        k_t = k.T
        zero = jnp.zeros_like(q)
        one = jnp.ones_like(q)
        for half in range(2):
            own = own_lanes(lane, half)
            extra = extra_lane(half)
            parts = (lane > extra) & (lane <= extra + 3)
            qa_ref[half, :, 0:128] = jnp.where(own, q_hi, zero)
            qa_ref[half, :, 128:256] = aug_ref[2 * p + half]
            ka_ref[half, :, 0:128] = k
            ka_ref[half, :, 128:256] = jnp.where(
                own, k, jnp.where(lane == extra, key_bias, jnp.where(parts, one, zero))
            )
            va_ref[half, :, :] = jnp.where(own, v, jnp.where(parts, one, zero))
            minus = -jnp.sum(jnp.where(own, prod, 0.0), axis=1, keepdims=True)
            a, b, c = three_parts(jnp.broadcast_to(minus, (slots, 128)))
            oa_ref[half, :, :] = jnp.where(
                own, do,
                jnp.where(lane == extra + 1, a, jnp.where(lane == extra + 2, b, jnp.where(lane == extra + 3, c, zero))),
            )
        for half in range(2):
            k_own = k_t[half * HEAD_DIM : (half + 1) * HEAD_DIM, :]
            heads_rows = slice(half * HEAD_DIM, (half + 1) * HEAD_DIM)
            for j in range(slots // ROWS):
                keys = slice(j * ROWS, (j + 1) * ROWS)
                late = slice(j * ROWS, slots)
                s = mul(ka_ref[half, keys, :], qa_ref[half, late, :], NT)
                diag = jnp.where(causal, s[:, :ROWS], NEGATIVE)
                s = diag if j == slots // ROWS - 1 else jnp.concatenate([diag, s[:, ROWS:]], axis=1)
                probs = jnp.exp2(s)
                dp = mul(va_ref[half, keys, :], oa_ref[half, late, :], NT)
                ds = (probs * dp).astype(jnp.bfloat16)
                probs = probs.astype(jnp.bfloat16)
                dv_ref[half, keys, :] = mul(probs, gmix_ref[late, cols])
                dk_ref[half, keys, :] = mul(ds, qkv_ref[late, cols])
                dq = mul(k_own[:, keys], ds)
                if j == 0:
                    dq_ref[heads_rows, late] = dq
                else:
                    dq_ref[heads_rows, late] += dq
        first = lane < HEAD_DIM
        gqkv_ref[:, cols] = (dq_ref[...].T * scale).astype(jnp.bfloat16)
        gqkv_ref[:, pl.ds(width + p * 128, 128)] = (jnp.where(first, dk_ref[0], dk_ref[1]) * scale).astype(jnp.bfloat16)
        gqkv_ref[:, pl.ds(2 * width + p * 128, 128)] = jnp.where(first, dv_ref[0], dv_ref[1]).astype(jnp.bfloat16)

    @pl.loop(0, slots // ROWS)
    def _(i):
        rows = pl.ds(i * ROWS, ROWS)
        normal, scaled = layer_stats(x_ref[rows, :].astype(jnp.float32))
        branch_ref[rows, :] = (normal * norms_ref[0:1, :] + norms_ref[2:3, :]).astype(jnp.bfloat16)
        grad = mul(gqkv_ref[rows, : 2 * width], wa_ref[:, : 2 * width], NT) + mul(
            gqkv_ref[rows, 2 * width :], wa_ref[:, HALF : HALF + width], NT
        )
        gn_ref[0:1, :] += jnp.sum(grad * normal, axis=0, keepdims=True)
        gn_ref[2:3, :] += jnp.sum(grad, axis=0, keepdims=True)
        gx_ref[rows, :] += norm_backward(grad, normal, scaled, norms_ref[0:1, :])

    tr_ref[...] = branch_ref[...].T

    @pl.loop(0, 3)
    def _(i):
        rows = pl.ds(i * tile, tile)
        for c in range(3):
            cols = slice(c * width, (c + 1) * width)
            gwa_ref[rows, cols] = mul(tr_ref[rows, :], gqkv_ref[:, cols]).astype(gwa_ref.dtype)


def back(length, x, g, hidden, qkv, mixed, aug, pos, dxs, os, wa, norms):
    slots, width = x.shape
    bf = jnp.bfloat16
    f32 = jnp.float32
    whole = pl.BlockSpec(memory_space=pltpu.VMEM)
    return pl.pallas_call(
        back_kernel,
        out_shape=(
            jax.ShapeDtypeStruct((slots, width), bf),
            jax.ShapeDtypeStruct((slots, width), f32),
            jax.ShapeDtypeStruct((width, 4 * width), bf),
            jax.ShapeDtypeStruct((8, width), f32),
        ),
        in_specs=[pl.BlockSpec(memory_space=pltpu.SMEM)] + [whole] * 11,
        out_specs=tuple([whole] * 4),
        scratch_shapes=[
            pltpu.VMEM((slots, width), bf),
            pltpu.VMEM((slots, width), bf),
            pltpu.VMEM((slots, 3 * width), bf),
            pltpu.VMEM((width, slots), bf),
            pltpu.VMEM((2, slots, 256), bf),
            pltpu.VMEM((2, slots, 256), bf),
            pltpu.VMEM((2, slots, 128), bf),
            pltpu.VMEM((2, slots, 128), bf),
            pltpu.VMEM((2, slots, 128), f32),
            pltpu.VMEM((2, slots, 128), f32),
            pltpu.VMEM((128, slots), f32),
        ],
        compiler_params=pltpu.CompilerParams(vmem_limit_bytes=60 * MIB),
        name="back",
    )(length, x, g, hidden, qkv, mixed, aug, pos, dxs, os, wa, norms)


def plane_body(
    tokens, token_ids, lengths, hash_table, w_qkv, w_attn_out, norm_gains, norm_biases, w_in, w_out, cotangent
):
    slots, width = tokens.shape
    bf = jnp.bfloat16
    both = ("dp", "fsdp")
    rp = padded_rows(slots)
    part = w_out.shape[0]

    norm_cols = jnp.concatenate([norm_gains, norm_biases], axis=1)
    local = jnp.concatenate(
        [w_qkv[:, : 2 * width], jnp.pad(norm_cols, ((0, 0), (0, 124))), w_qkv[:, 2 * width :], w_attn_out], axis=1
    )
    local = jnp.pad(local, ((0, 32 - local.shape[0]), (0, WIDE - local.shape[1])))
    table = jnp.pad(hash_table, (0, (-hash_table.shape[0]) % 8192)).reshape(64, 128).T.astype(bf)
    qkv, mixed, aug, hidden, xs, gs, w, wa, norms, pos, counts = front(
        lengths, tokens, token_ids.reshape(1, slots), table, cotangent, local, w_in, w_out
    )
    expert_counts = lax.psum(counts[:EXPERTS, 0], both)
    xs = xs.reshape(4, rp // GROUP + 1, GROUP, width)
    gs = gs.reshape(4, rp // GROUP + 1, GROUP, width)
    n16 = xs[:, rp // GROUP, :EXPERTS, 0].astype(jnp.int32).reshape(-1)
    w1 = w[0].reshape(EXPERTS, width, 2 * part)
    w2 = w[1].reshape(EXPERTS, 2 * part, width)
    o_part, dx_part, gw1, gw2 = experts(n16, xs, gs, w1, w2)
    near = [[0, 1, 2, 3], [4, 5, 6, 7]]
    over = [[0, 4], [1, 5], [2, 6], [3, 7]]
    sum_near = lambda v: lax.psum_scatter(v, "fsdp", scatter_dimension=0, tiled=True, axis_index_groups=near)
    os = sum_near(o_part.reshape(4 * rp, width))
    dxs = sum_near(dx_part.reshape(4 * rp, width))

    def sum_owners(v):
        v = lax.psum_scatter(v.reshape(EXPERTS * 2 * part, width), "dp", scatter_dimension=0, tiled=True)
        return lax.psum_scatter(v, "fsdp", scatter_dimension=0, tiled=True, axis_index_groups=over)

    gw1 = sum_owners(gw1)
    gw2 = sum_owners(gw2)
    gw1 = lax.all_to_all(
        gw1.reshape(4, part // 4, 2 * part), "fsdp", split_axis=0, concat_axis=0, tiled=True, axis_index_groups=near
    )
    gw1 = gw1.reshape(4, part // 4, 2, part).transpose(1, 2, 0, 3).reshape(part // 4, 8 * part)
    out, gx, gwa, gn = back(lengths, tokens, cotangent, hidden, qkv, mixed, aug, pos, dxs, os, wa, norms)
    gwa = lax.psum_scatter(gwa, both, scatter_dimension=0, tiled=True).astype(jnp.float32)
    gn = lax.psum_scatter(gn[:4].T, both, scatter_dimension=0, tiled=True)
    return (
        out, gx, gwa[:, : 3 * width], gwa[:, 3 * width :], gn[:, 0:2], gn[:, 2:4],
        gw1.astype(jnp.float32), gw2.astype(jnp.float32), expert_counts,
    )


def solution(mesh):
    placed = (
        P(("dp", "fsdp"), None),
        P(("dp", "fsdp")),
        P(("dp", "fsdp")),
        P(),
        P(("dp", "fsdp"), None),
        P(("dp", "fsdp"), None),
        P(("dp", "fsdp"), None),
        P(("dp", "fsdp"), None),
        P(("dp", "fsdp"), None),
        P(("dp", "fsdp"), None),
        P(("dp", "fsdp"), None),
    )
    by_plane = mesh.shape["dp"] == EXPERTS and mesh.shape["fsdp"] == 8
    return jax.shard_map(
        plane_body if by_plane else body,
        mesh=mesh,
        in_specs=placed,
        out_specs=(
            P(("dp", "fsdp"), None),
            P(("dp", "fsdp"), None),
            P(("dp", "fsdp"), None),
            P(("dp", "fsdp"), None),
            P(("dp", "fsdp"), None),
            P(("dp", "fsdp"), None),
            P(("dp", "fsdp"), None),
            P(("dp", "fsdp"), None),
            P(),
        ),
        check_vma=False,
    )
```

```python
import functools

import jax
import jax.numpy as jnp
from jax import lax
from jax.experimental import pallas as pl
from jax.experimental.pallas import tpu as pltpu
from jax.sharding import PartitionSpec as P

D = 768
HEADS = 12
HEAD_DIM = 64
EXPERTS = 4
BLOCK = 128


EPSILON = 1e-05
NEGATIVE = -1e30


def layer_stats(values):
    average = jnp.mean(values, axis=-1, keepdims=True)
    centred = values - average
    scaled = lax.rsqrt(jnp.mean(centred * centred, axis=-1, keepdims=True) + EPSILON)
    return (centred * scaled, scaled)


def norm_backward(grad_normed, normal, scaled, gain_col):
    grad_scaled = grad_normed * gain_col
    first_mean = jnp.mean(grad_scaled, axis=-1, keepdims=True)
    second_mean = jnp.mean(grad_scaled * normal, axis=-1, keepdims=True)
    return scaled * (grad_scaled - first_mean - normal * second_mean)


def head_groups(heads):
    group_width = 4
    return [(start, start + group_width) for start in range(0, heads, group_width)]


def allowed_keys(length, seq_len):
    places = jnp.arange(seq_len, dtype=jnp.int32)
    return (places[None, :] <= places[:, None]) & (places[None, :] < length)


def masked_scores(query_part, key_part, allowed):
    scale = query_part.shape[-1] ** (-0.5)
    raw = (
        jnp.einsum("qhd,khd->hqk", query_part, key_part, preferred_element_type=jnp.float32) * scale
    )
    return jnp.where(allowed[None], raw, NEGATIVE)


def attention_forward(entry):
    queries, keys, values, length = entry
    allowed = allowed_keys(length, queries.shape[0])
    mixed_parts = []
    total_parts = []
    for start, finish in head_groups(queries.shape[1]):
        scores = masked_scores(queries[:, start:finish], keys[:, start:finish], allowed)
        highest = jnp.max(scores, axis=-1, keepdims=True)
        totals = highest + jnp.log(jnp.sum(jnp.exp(scores - highest), axis=-1, keepdims=True))
        weights = jnp.exp(scores - totals).astype(jnp.bfloat16)
        mixed_parts.append(
            jnp.einsum(
                "hqk,khd->qhd", weights, values[:, start:finish], preferred_element_type=jnp.float32
            ).astype(jnp.bfloat16)
        )
        total_parts.append(totals[..., 0])
    return (jnp.concatenate(mixed_parts, axis=1), jnp.concatenate(total_parts, axis=0))


def attention_backward(entry):
    queries, keys, values, totals, grad_mixed, length = entry
    allowed = allowed_keys(length, queries.shape[0])
    scale = queries.shape[-1] ** (-0.5)
    query_parts, key_parts, value_parts = ([], [], [])
    for start, finish in head_groups(queries.shape[1]):
        scores = masked_scores(queries[:, start:finish], keys[:, start:finish], allowed)
        weights = jnp.exp(scores - totals[start:finish][..., None])
        grad_weights = jnp.einsum(
            "qhd,khd->hqk",
            grad_mixed[:, start:finish],
            values[:, start:finish],
            preferred_element_type=jnp.float32,
        )
        inner_sum = jnp.sum(grad_weights * weights, axis=-1, keepdims=True)
        grad_scores = (weights * (grad_weights - inner_sum)).astype(jnp.bfloat16)
        value_parts.append(
            jnp.einsum(
                "hqk,qhd->khd",
                weights.astype(jnp.bfloat16),
                grad_mixed[:, start:finish],
                preferred_element_type=jnp.float32,
            )
        )
        query_parts.append(
            jnp.einsum(
                "hqk,khd->qhd",
                grad_scores,
                keys[:, start:finish],
                preferred_element_type=jnp.float32,
            )
            * scale
        )
        key_parts.append(
            jnp.einsum(
                "hqk,qhd->khd",
                grad_scores,
                queries[:, start:finish],
                preferred_element_type=jnp.float32,
            )
            * scale
        )
    return (
        jnp.concatenate(query_parts, axis=1),
        jnp.concatenate(key_parts, axis=1),
        jnp.concatenate(value_parts, axis=1),
    )


def segment_table(group_ends, total_rows, block_rows):
    block_count = total_rows // block_rows
    block_starts = jnp.arange(block_count, dtype=jnp.int32) * block_rows
    points = jnp.sort(jnp.concatenate([block_starts, group_ends]))
    finishes = jnp.concatenate([points[1:], jnp.full((1,), total_rows, jnp.int32)])
    blocks = jnp.minimum(points // block_rows, block_count - 1)
    owners = jnp.sum((group_ends[None, :] <= points[:, None]).astype(jnp.int32), axis=1)
    active = (finishes > points) & (owners < group_ends.shape[0])
    owners = jnp.minimum(owners, group_ends.shape[0] - 1)
    return (points, finishes, blocks, owners, active)


def expert_forward(sorted_rows, inner_all, outer_all, table, block_rows):
    model_width = sorted_rows.shape[1]
    hidden_width = inner_all.shape[1]

    def visit(state, entry):
        start, finish, block_id, owner, live = entry

        def compute(inner_state):
            pre_all, result_all = inner_state
            base = block_id * block_rows
            rows_here = lax.dynamic_slice_in_dim(sorted_rows, base, block_rows, 0)
            inner = lax.dynamic_slice_in_dim(inner_all, owner * model_width, model_width, 0)
            outer = lax.dynamic_slice_in_dim(outer_all, owner * hidden_width, hidden_width, 0)
            places = base + jnp.arange(block_rows, dtype=jnp.int32)
            inside = ((places >= start) & (places < finish))[:, None]
            pre = jnp.dot(rows_here, inner, preferred_element_type=jnp.float32)
            result = jnp.dot(
                jax.nn.gelu(pre).astype(jnp.bfloat16), outer, preferred_element_type=jnp.float32
            )
            old_pre = lax.dynamic_slice_in_dim(pre_all, base, block_rows, 0)
            old_result = lax.dynamic_slice_in_dim(result_all, base, block_rows, 0)
            pre_all = lax.dynamic_update_slice_in_dim(
                pre_all, jnp.where(inside, pre, old_pre), base, 0
            )
            result_all = lax.dynamic_update_slice_in_dim(
                result_all, jnp.where(inside, result, old_result), base, 0
            )
            return (pre_all, result_all)

        return (lax.cond(live, compute, lambda same: same, state), None)

    start_state = (
        jnp.zeros((sorted_rows.shape[0], hidden_width), jnp.float32),
        jnp.zeros((sorted_rows.shape[0], model_width), jnp.float32),
    )
    final_state, _ = lax.scan(visit, start_state, table)
    return final_state


def expert_backward(sorted_rows, pre_all, grad_sorted, inner_all, outer_all, table, block_rows):
    model_width = sorted_rows.shape[1]
    hidden_width = inner_all.shape[1]

    def visit(state, entry):
        start, finish, block_id, owner, live = entry

        def compute(inner_state):
            grad_rows, grad_inner, grad_outer = inner_state
            base = block_id * block_rows
            rows_here = lax.dynamic_slice_in_dim(sorted_rows, base, block_rows, 0)
            pre = lax.dynamic_slice_in_dim(pre_all, base, block_rows, 0)
            inner = lax.dynamic_slice_in_dim(inner_all, owner * model_width, model_width, 0)
            outer = lax.dynamic_slice_in_dim(outer_all, owner * hidden_width, hidden_width, 0)
            places = base + jnp.arange(block_rows, dtype=jnp.int32)
            inside = ((places >= start) & (places < finish))[:, None]
            grad_block = jnp.where(
                inside,
                lax.dynamic_slice_in_dim(grad_sorted, base, block_rows, 0),
                jnp.zeros((), jnp.bfloat16),
            )
            activated, gelu_pull = jax.vjp(jax.nn.gelu, pre)
            outer_piece = jnp.einsum(
                "tf,td->fd",
                activated.astype(jnp.bfloat16),
                grad_block,
                preferred_element_type=jnp.float32,
            )
            grad_act = jnp.einsum(
                "td,fd->tf", grad_block, outer, preferred_element_type=jnp.float32
            )
            grad_pre = gelu_pull(grad_act)[0].astype(jnp.bfloat16)
            inner_piece = jnp.einsum(
                "td,tf->df", rows_here, grad_pre, preferred_element_type=jnp.float32
            )
            rows_piece = jnp.einsum(
                "tf,df->td", grad_pre, inner, preferred_element_type=jnp.float32
            )
            old_rows = lax.dynamic_slice_in_dim(grad_rows, base, block_rows, 0)
            grad_rows = lax.dynamic_update_slice_in_dim(grad_rows, old_rows + rows_piece, base, 0)
            old_inner = lax.dynamic_slice_in_dim(grad_inner, owner * model_width, model_width, 0)
            grad_inner = lax.dynamic_update_slice_in_dim(
                grad_inner, old_inner + inner_piece, owner * model_width, 0
            )
            old_outer = lax.dynamic_slice_in_dim(grad_outer, owner * hidden_width, hidden_width, 0)
            grad_outer = lax.dynamic_update_slice_in_dim(
                grad_outer, old_outer + outer_piece, owner * hidden_width, 0
            )
            return (grad_rows, grad_inner, grad_outer)

        return (lax.cond(live, compute, lambda same: same, state), None)

    start_state = (
        jnp.zeros(sorted_rows.shape, jnp.float32),
        jnp.zeros(inner_all.shape, jnp.float32),
        jnp.zeros(outer_all.shape, jnp.float32),
    )
    final_state, _ = lax.scan(visit, start_state, table)
    return final_state


def body(
    tokens,
    token_ids,
    lengths,
    hash_table,
    w_qkv,
    w_attn_out,
    norm_gains,
    norm_biases,
    w_in,
    w_out,
    cotangent,
):
    rows_count = tokens.shape[0]
    seq_count = lengths.shape[0]
    seq_len = rows_count // seq_count
    model_width = D
    expert_total = EXPERTS
    qkv_full, proj_full, gains_full, biases_full = (
        lax.all_gather(w_qkv, ("dp", "fsdp"), axis=0, tiled=True),
        lax.all_gather(w_attn_out, ("dp", "fsdp"), axis=0, tiled=True),
        lax.all_gather(norm_gains, ("dp", "fsdp"), axis=0, tiled=True),
        lax.all_gather(norm_biases, ("dp", "fsdp"), axis=0, tiled=True),
    )
    gains_f = gains_full.astype(jnp.float32)
    biases_f = biases_full.astype(jnp.float32)
    inputs = tokens.astype(jnp.float32)
    normal_one, scaled_one = layer_stats(inputs)
    first_in = (normal_one * gains_f[:, 0] + biases_f[:, 0]).astype(jnp.bfloat16)
    qkv_low = jnp.dot(first_in, qkv_full, preferred_element_type=jnp.float32).astype(jnp.bfloat16)
    packed = qkv_low.reshape(seq_count, seq_len, 3, HEADS, HEAD_DIM)
    queries = packed[:, :, 0]
    keys = packed[:, :, 1]
    values = packed[:, :, 2]
    mixed, totals = lax.map(attention_forward, (queries, keys, values, lengths))
    mixed_flat = mixed.reshape(rows_count, model_width)
    hidden = inputs + jnp.dot(mixed_flat, proj_full, preferred_element_type=jnp.float32)
    normal_two, scaled_two = layer_stats(hidden)
    second_in = (normal_two * gains_f[:, 1] + biases_f[:, 1]).astype(jnp.bfloat16)
    places = jnp.arange(rows_count, dtype=jnp.int32) % seq_len
    used = places < jnp.repeat(lengths, seq_len, total_repeat_length=rows_count)
    expert_ids = jnp.where(used, hash_table[token_ids], expert_total)
    matches = (expert_ids[:, None] == jnp.arange(expert_total, dtype=jnp.int32)[None, :]).astype(
        jnp.int32
    )
    local_counts = jnp.sum(matches, axis=0)
    expert_counts = lax.psum(local_counts, ("dp", "fsdp"))
    ordering = jnp.argsort(expert_ids, stable=True)
    inverse = (
        jnp.zeros((rows_count,), jnp.int32)
        .at[ordering]
        .set(jnp.arange(rows_count, dtype=jnp.int32))
    )
    group_ends = jnp.cumsum(local_counts)
    table = segment_table(group_ends, rows_count, BLOCK)
    inner_all, outer_all = (
        lax.all_gather(w_in, ("dp", "fsdp"), axis=0, tiled=True),
        lax.all_gather(w_out, ("dp", "fsdp"), axis=0, tiled=True),
    )
    sorted_rows = second_in[ordering]
    pre_all, result_sorted = expert_forward(sorted_rows, inner_all, outer_all, table, BLOCK)
    layer_out = (hidden + result_sorted[inverse]).astype(jnp.bfloat16)
    grad_out = cotangent.astype(jnp.float32)
    grad_sorted = cotangent[ordering]
    inner_back, outer_back = (
        lax.all_gather(w_in, ("dp", "fsdp"), axis=0, tiled=True),
        lax.all_gather(w_out, ("dp", "fsdp"), axis=0, tiled=True),
    )
    grad_rows_sorted, grad_inner, grad_outer = expert_backward(
        sorted_rows, pre_all, grad_sorted, inner_back, outer_back, table, BLOCK
    )
    grad_w_in, grad_w_out = (
        lax.psum_scatter(grad_inner, ("dp", "fsdp"), scatter_dimension=0, tiled=True),
        lax.psum_scatter(grad_outer, ("dp", "fsdp"), scatter_dimension=0, tiled=True),
    )
    grad_second = grad_rows_sorted[inverse]
    gain_two = jnp.sum(grad_second * normal_two, axis=0)
    bias_two = jnp.sum(grad_second, axis=0)
    grad_hidden = grad_out + norm_backward(grad_second, normal_two, scaled_two, gains_f[:, 1])
    grad_branch = grad_hidden.astype(jnp.bfloat16)
    qkv_back, proj_back = (
        lax.all_gather(w_qkv, ("dp", "fsdp"), axis=0, tiled=True),
        lax.all_gather(w_attn_out, ("dp", "fsdp"), axis=0, tiled=True),
    )
    grad_proj = jnp.einsum("td,te->de", mixed_flat, grad_branch, preferred_element_type=jnp.float32)
    grad_mixed = jnp.einsum(
        "te,de->td", grad_branch, proj_back, preferred_element_type=jnp.float32
    ).astype(jnp.bfloat16)
    grad_mixed = grad_mixed.reshape(seq_count, seq_len, HEADS, HEAD_DIM)
    grad_queries, grad_keys, grad_values = lax.map(
        attention_backward, (queries, keys, values, totals, grad_mixed, lengths)
    )
    grad_qkv = (
        jnp.stack([grad_queries, grad_keys, grad_values], axis=2)
        .reshape(rows_count, 3 * model_width)
        .astype(jnp.bfloat16)
    )
    grad_qkv_w = jnp.einsum("td,te->de", first_in, grad_qkv, preferred_element_type=jnp.float32)
    grad_first = jnp.einsum("te,de->td", grad_qkv, qkv_back, preferred_element_type=jnp.float32)
    gain_one = jnp.sum(grad_first * normal_one, axis=0)
    bias_one = jnp.sum(grad_first, axis=0)
    grad_tokens = grad_hidden + norm_backward(grad_first, normal_one, scaled_one, gains_f[:, 0])
    grad_gains = jnp.stack([gain_one, gain_two], axis=1)
    grad_biases = jnp.stack([bias_one, bias_two], axis=1)
    grad_w_qkv, grad_w_attn_out, grad_norm_gains, grad_norm_biases = (
        lax.psum_scatter(grad_qkv_w, ("dp", "fsdp"), scatter_dimension=0, tiled=True),
        lax.psum_scatter(grad_proj, ("dp", "fsdp"), scatter_dimension=0, tiled=True),
        lax.psum_scatter(grad_gains, ("dp", "fsdp"), scatter_dimension=0, tiled=True),
        lax.psum_scatter(grad_biases, ("dp", "fsdp"), scatter_dimension=0, tiled=True),
    )
    return (
        layer_out,
        grad_tokens,
        grad_w_qkv,
        grad_w_attn_out,
        grad_norm_gains,
        grad_norm_biases,
        grad_w_in,
        grad_w_out,
        expert_counts,
    )


LOG2E = 1.4426950408889634
ROWS = 256
GROUP = 16
MIB = 1024 * 1024
NT = (((1,), (1,)), ((), ()))
NN = (((1,), (0,)), ((), ()))
ROOT = 0.7978845608028654
CUBIC = 0.044715


def mul(a, b, dims=NN):
    return lax.dot_general(a, b, dims, preferred_element_type=jnp.float32)


def iota(shape, dim):
    return lax.broadcasted_iota(jnp.int32, shape, dim)


def padded_rows(slots):
    return slots + EXPERTS * GROUP


def three_parts(v):
    first = v.astype(jnp.bfloat16)
    rest = v - first.astype(jnp.float32)
    second = rest.astype(jnp.bfloat16)
    third = (rest - second.astype(jnp.float32)).astype(jnp.bfloat16)
    return first, second, third


def own_lanes(lane, half):
    return (lane < HEAD_DIM) if half == 0 else (lane >= HEAD_DIM)


def extra_lane(half):
    return HEAD_DIM if half == 0 else 0


def routing(ids, table, length, perm_ref):
    slots = ids.shape[1]
    chosen = (iota((table.shape[1], slots), 0) == (ids >> 7)).astype(jnp.bfloat16)
    rows = mul(table, chosen)
    expert = jnp.sum(
        jnp.where(iota(rows.shape, 0) == (ids & 127), rows, 0.0), axis=0, keepdims=True
    ).astype(jnp.int32)
    used = iota((1, slots), 1) < length
    member = (iota((8, slots), 0) == expert) & used
    member_f = jnp.where(member, 1.0, 0.0)
    perm_ref[0:slots, :] = (iota((slots, slots), 0) <= iota((slots, slots), 1)).astype(jnp.bfloat16)
    rank = mul(member_f.astype(jnp.bfloat16), perm_ref[0:slots, :])
    counts = rank[:, slots - 1 : slots]
    groups = jnp.floor((counts + (GROUP - 1)) * (1.0 / GROUP))
    row8 = iota((8, 1), 0)
    start = jnp.zeros((8, 1), jnp.float32)
    for e in range(EXPERTS - 1):
        start = start + jnp.where(row8 > e, groups[e : e + 1, :], 0.0)
    place = jnp.sum(member_f * (rank - 1.0 + start * GROUP), axis=0, keepdims=True)
    place = jnp.where(used, place, -1.0)
    return place, counts, groups


MESH = pl.DeviceIdType.MESH
HALF = 1664
WIDE = 2 * HALF


class Place:
    def __init__(self):
        self.z = lax.axis_index("dp")
        f = lax.axis_index("fsdp")
        self.y = f // 4
        self.x = (f // 2) % 2
        self.c = f % 2

    def at(self, z=None, y=None, x=None, c=None):
        z = self.z if z is None else z
        y = self.y if y is None else y
        x = self.x if x is None else x
        c = self.c if c is None else c
        return (z, 4 * y + 2 * x + c)

    def greet(self, peers):
        barrier = pltpu.get_barrier_semaphore()
        for peer in peers:
            pl.semaphore_signal(barrier, inc=1, device_id=peer, device_id_type=MESH)
        pl.semaphore_wait(barrier, len(peers))


def push(src, dst, send, recv, peer):
    return pltpu.make_async_remote_copy(
        src_ref=src, dst_ref=dst, send_sem=send, recv_sem=recv, device_id=peer, device_id_type=MESH
    )


def front_kernel(
    len_ref, x_ref, ids_ref, table_ref, g_ref, local_ref, win_ref, wout_ref,
    qkv_ref, mixed_ref, aug_ref, hidden_ref, xs_ref, gs_ref, w_ref, wa_ref, norms_ref, pos_ref, counts_ref,
    perm_ref, normed_ref, qa_ref, ka_ref, va_ref, tokx_ref, tokg_ref, sib_ref,
    sem0, sz, rz, sy, ry, sx, rx, sd, rd, ss, rs,
    tok_local, tok_send, tok_recv,
    lane_local, lane_send, lane_recv, up_send, down_send, line_recv, y_send, y_recv,
):
    slots, width = x_ref.shape
    heads = width // HEAD_DIM
    rp = padded_rows(slots)
    length = len_ref[0]
    me = Place()
    z, y, x, c = me.z, me.y, me.x, me.c
    depth = 4
    sibling, beside, across = me.at(c=1 - c), me.at(x=1 - x), me.at(y=1 - y)
    me.greet([sibling, beside, across, me.at(x=1 - x, c=1 - c)] + [me.at(z=z ^ k) for k in range(1, depth)])

    first = push(local_ref, sib_ref, sem0.at[0], sem0.at[1], sibling)
    first.start()

    def block(zz, yy, xx):
        rows = pl.ds(pl.multiple_of(48 * (4 * zz + 2 * yy + xx), 48), 48)
        return wa_ref.at[rows, pl.ds(pl.multiple_of(c * HALF, 128), HALF)]

    def share(zz, yy, xx, send, recv, peer):
        ref = block(zz, yy, xx)
        return push(ref, ref, send, recv, peer)

    def z_copy(k, source):
        return share(source, y, x, sz.at[k - 1], rz.at[source], me.at(z=z ^ k))

    def y_copy(zz, source_y):
        return share(zz, source_y, x, sy.at[zz], ry.at[zz], across)

    def x_copy(zz, source_x):
        return share(zz, y, source_x, sx.at[zz], rx.at[zz], beside)

    def d_copy_x(zz, yy, xx):
        return share(zz, yy, xx, sd.at[zz], rd.at[zz], beside)

    def d_copy_y(zz, yy, xx):
        return share(zz, yy, xx, sd.at[zz], rd.at[zz], across)

    def s_copy(zz, side):
        ref = wa_ref.at[pl.ds(pl.multiple_of(192 * zz, 192), 192), pl.ds(pl.multiple_of(side * HALF, 128), HALF)]
        return push(ref, ref, ss.at[zz], rs.at[zz], sibling)

    part = wout_ref.shape[0]
    rows_in = win_ref.shape[0]
    lanes = [(1 - x, c), (x, 1 - c), (1 - x, 1 - c)]

    def lane_cols(b, xx, cc):
        return win_ref.at[:, pl.ds(pl.multiple_of(part * (4 * b + 2 * xx + cc), 128), part)]

    def lane_home(b, xx, cc):
        return w_ref.at[0, z, y, pl.ds(pl.multiple_of(rows_in * (2 * xx + cc), rows_in), rows_in), pl.ds(b * part, part)]

    def lane_copy(i, b, arrive):
        xx, cc = lanes[i]
        home = lane_home(b, xx, cc) if arrive else lane_home(b, x, c)
        return push(lane_cols(b, xx, cc), home, lane_send.at[i, b], lane_recv.at[i, b], me.at(x=xx, c=cc))

    def lane_own(b):
        return pltpu.make_async_copy(lane_cols(b, x, c), lane_home(b, x, c), lane_local.at[b])

    own_out = pltpu.make_async_copy(wout_ref, w_ref.at[1, z, y], lane_local.at[2])

    def shard(k, zz, yy):
        return w_ref.at[k, zz, yy]

    def up_copy(k, zz):
        return push(shard(k, zz, y), shard(k, zz, y), up_send.at[k, zz], line_recv.at[k, zz], me.at(z=jnp.minimum(z + 1, depth - 1)))

    def down_copy(k, zz):
        return push(shard(k, zz, y), shard(k, zz, y), down_send.at[k, zz], line_recv.at[k, zz], me.at(z=jnp.maximum(z - 1, 0)))

    def over_copy(k, zz, yy):
        return push(shard(k, zz, yy), shard(k, zz, yy), y_send.at[k, zz], y_recv.at[k, zz], across)

    def spread(k):
        @pl.when(z < depth - 1)
        def _():
            up_copy(k, z).start()

        @pl.when(z > 0)
        def _():
            down_copy(k, z).start()

        over_copy(k, z, y).start()

    def relay(k, s):
        @pl.when(z >= s)
        def _():
            up_copy(k, z - s).wait_recv()

            @pl.when(z < depth - 1)
            def _():
                up_copy(k, z - s).start()

            over_copy(k, z - s, y).start()

        @pl.when(z + s < depth)
        def _():
            down_copy(k, z + s).wait_recv()

            @pl.when(z > 0)
            def _():
                down_copy(k, z + s).start()

            over_copy(k, z + s, y).start()

    def weights_start():
        for i in range(3):
            for b in range(2):
                lane_copy(i, b, False).start()
        spread(1)

    def weights_lane():
        for i in range(3):
            for b in range(2):
                lane_copy(i, b, True).wait_recv()
        for b in range(2):
            lane_own(b).wait()
        spread(0)

    ticks = [weights_lane] + [functools.partial(relay, k, s) for s in range(1, depth) for k in (1, 0)]

    def weights_end():
        for k in (1, 0):
            for zz in range(depth):
                over_copy(k, zz, 1 - y).wait()
                for copy, stop in ((up_copy, depth - 1), (down_copy, 0)):
                    inside = (zz <= z) if stop else (zz >= z)

                    @pl.when(inside & (z != stop))
                    def _():
                        copy(k, zz).wait_send()

        for i in range(3):
            for b in range(2):
                lane_copy(i, b, False).wait_send()

    mine = 2 * x + c

    def tok_copies(k, scratch, far_ref):
        own = pltpu.make_async_copy(scratch, far_ref.at[mine], tok_local.at[k])
        near = push(scratch, far_ref.at[mine], tok_send.at[k, 0], tok_recv.at[k, 0], sibling)
        far = push(scratch, far_ref.at[mine], tok_send.at[k, 1], tok_recv.at[k, 1], beside)
        slot = far_ref.at[2 * (1 - x) + c]
        onward = push(slot, slot, tok_send.at[k, 2], tok_recv.at[k, 2], sibling)
        return own, near, far, onward

    x_copies = tok_copies(0, tokx_ref, xs_ref)
    g_copies = tok_copies(1, tokg_ref, gs_ref)

    first.wait_recv()
    zero_core = c == 0
    own_cols = pl.ds(pl.multiple_of(c * HALF, 128), HALF)
    local = local_ref[0:24, own_cols]
    other = sib_ref[0:24, own_cols]
    own_rows = pl.ds(pl.multiple_of(48 * (4 * z + 2 * y + x), 48), 48)
    wa_ref[own_rows, own_cols] = jnp.concatenate(
        [jnp.where(zero_core, local, other), jnp.where(zero_core, other, local)], axis=0
    )
    for k in range(1, depth):
        z_copy(k, z).start()
    y_copy(z, y).start()
    x_copy(z, x).start()
    for b in range(2):
        lane_own(b).start()
    own_out.start()

    place, counts, groups = routing(ids_ref[...], table_ref[...], length, perm_ref)
    place_i = place.astype(jnp.int32)
    pos_ref[...] = jnp.broadcast_to(place, (128, slots)).T
    counts_ref[...] = jnp.broadcast_to(counts, (8, 128)).astype(jnp.int32)

    for k in range(1, depth):
        zz = z ^ k
        z_copy(k, zz).wait_recv()
        y_copy(zz, y).start()
        x_copy(zz, x).start()

    step = rp // 4

    @pl.loop(0, 4)
    def _(i):
        base = i * step
        perm_ref[pl.ds(base, step), :] = (
            iota((step, slots), 0) + base == place_i
        ).astype(jnp.bfloat16)

    for k in range(depth):
        zz = z ^ k
        y_copy(zz, 1 - y).wait_recv()
        x_copy(zz, 1 - x).wait_recv()

        @pl.when(zz % 2 == 0)
        def _():
            d_copy_x(zz, 1 - y, x).start()

        @pl.when(zz % 2 == 1)
        def _():
            d_copy_y(zz, y, 1 - x).start()

    own_out.wait()
    weights_start()

    @pl.loop(0, 4)
    def _(i):
        rows = pl.ds(i * step, step)
        tokg_ref[rows, :] = mul(perm_ref[rows, :], g_ref[...]).astype(jnp.bfloat16)

    tail = jnp.broadcast_to(jnp.concatenate([groups, groups], axis=0), (GROUP, width)).astype(jnp.bfloat16)
    tokx_ref[rp : rp + GROUP, :] = tail
    tokg_ref[rp : rp + GROUP, :] = tail

    for k in range(depth):
        zz = z ^ k
        d_copy_x(zz, 1 - y, 1 - x).wait_recv()
        s_copy(zz, c).start()
    for k in range(depth):
        s_copy(z ^ k, 1 - c).wait_recv()
    for copy in g_copies[:3]:
        copy.start()

    cols_t = wa_ref[:, 2 * width : 2 * width + 128].astype(jnp.float32).T
    norms_ref[...] = cols_t[0:8, :]

    @pl.loop(0, slots // ROWS)
    def _(i):
        rows = pl.ds(i * ROWS, ROWS)
        normal, _ = layer_stats(x_ref[rows, :].astype(jnp.float32))
        normed = (normal * norms_ref[0:1, :] + norms_ref[2:3, :]).astype(jnp.bfloat16)
        for part_i, start in enumerate((0, width, HALF)):
            cols = slice(part_i * width, (part_i + 1) * width)
            qkv_ref[rows, cols] = mul(normed, wa_ref[:, start : start + width]).astype(jnp.bfloat16)

    lane = iota((slots, 128), 1)
    key_bias = jnp.where(iota((slots, 128), 0) < length, 0.0, NEGATIVE).astype(jnp.bfloat16)
    causal = iota((ROWS, ROWS), 1) <= iota((ROWS, ROWS), 0)
    lane_b = iota((ROWS, 128), 1)
    pairs = heads // 2
    slots_for = [[] for _ in range(pairs)]
    for i, tick in enumerate(ticks[:pairs]):
        slots_for[i].append(tick)

    @pl.loop(0, pairs)
    def _(p):
        cols = pl.ds(p * 128, 128)
        q = qkv_ref[:, cols].astype(jnp.float32) * (HEAD_DIM ** -0.5 * LOG2E)
        q_hi = q.astype(jnp.bfloat16)
        q_lo = (q - q_hi.astype(jnp.float32)).astype(jnp.bfloat16)
        k = qkv_ref[:, pl.ds(width + p * 128, 128)]
        v = qkv_ref[:, pl.ds(2 * width + p * 128, 128)]
        zero = jnp.zeros_like(q_hi)
        one = jnp.ones_like(q_hi)
        for half in range(2):
            own = own_lanes(lane, half)
            extra = extra_lane(half)
            qa_ref[half, :, 0:128] = jnp.where(own, q_hi, zero)
            qa_ref[half, :, 128:256] = jnp.where(own, q_lo, jnp.where(lane == extra, one, zero))
            ka_ref[half, :, 0:128] = k
            ka_ref[half, :, 128:256] = jnp.where(own, k, jnp.where(lane == extra, key_bias, zero))
            va_ref[half, :, :] = jnp.where(own, v, one)
        for i in range(slots // ROWS):
            rows = slice(i * ROWS, (i + 1) * ROWS)
            keys = (i + 1) * ROWS
            outs = []
            for half in range(2):
                s = mul(qa_ref[half, rows, :], ka_ref[half, 0:keys, :], NT)
                diag = jnp.where(causal, s[:, i * ROWS :], NEGATIVE)
                s = diag if i == 0 else jnp.concatenate([s[:, : i * ROWS], diag], axis=1)
                top = jnp.max(s, axis=1, keepdims=True)
                probs = jnp.exp2(s - top).astype(jnp.bfloat16)
                out = mul(probs, va_ref[half, 0:keys, :])
                total = pltpu.roll(out, HEAD_DIM, 1)
                outs.append(out / total)
                minus = -(top + jnp.log2(out))
                a, b, d = three_parts(minus)
                extra = extra_lane(half)
                seen = qa_ref[half, rows, 128:256]
                seen = jnp.where(lane_b == extra + 1, a, seen)
                seen = jnp.where(lane_b == extra + 2, b, seen)
                seen = jnp.where(lane_b == extra + 3, d, seen)
                aug_ref[2 * p + half, rows, :] = seen
            mixed_ref[rows, cols] = jnp.where(lane_b < HEAD_DIM, outs[0], outs[1]).astype(jnp.bfloat16)
        for i in range(pairs):
            @pl.when(p == i)
            def _():
                for tick in slots_for[i]:
                    tick()

    @pl.loop(0, slots // ROWS)
    def _(i):
        rows = pl.ds(i * ROWS, ROWS)
        hidden = x_ref[rows, :].astype(jnp.float32) + mul(mixed_ref[rows, :], wa_ref[:, HALF + width : HALF + 2 * width])
        hidden_ref[rows, :] = hidden
        normal, _ = layer_stats(hidden)
        normed_ref[rows, :] = (normal * norms_ref[1:2, :] + norms_ref[3:4, :]).astype(jnp.bfloat16)

    @pl.loop(0, 4)
    def _(i):
        rows = pl.ds(i * step, step)
        tokx_ref[rows, :] = mul(perm_ref[rows, :], normed_ref[...]).astype(jnp.bfloat16)

    for copy in x_copies[:3]:
        copy.start()
    g_copies[2].wait_recv()
    g_copies[3].start()
    for tick in ticks[pairs:]:
        tick()
    x_copies[2].wait_recv()
    x_copies[3].start()
    weights_end()
    for own, near, far, onward in (x_copies, g_copies):
        own.wait()
        near.wait()
        far.wait_send()
        onward.wait()
    first.wait_send()
    for k in range(1, depth):
        z_copy(k, z).wait_send()
    for zz in range(depth):
        y_copy(zz, y).wait_send()
        x_copy(zz, x).wait_send()
        d_copy_x(zz, y, x).wait_send()
        s_copy(zz, c).wait_send()


def front(length, x, ids, table, g, local, w_in, w_out):
    slots, width = x.shape
    rp = padded_rows(slots)
    part = w_out.shape[0]
    bf = jnp.bfloat16
    f32 = jnp.float32
    whole = pl.BlockSpec(memory_space=pltpu.VMEM)
    far = pl.BlockSpec(memory_space=pl.ANY)
    dma = pltpu.SemaphoreType.DMA
    return pl.pallas_call(
        front_kernel,
        out_shape=(
            jax.ShapeDtypeStruct((slots, 3 * width), bf),
            jax.ShapeDtypeStruct((slots, width), bf),
            jax.ShapeDtypeStruct((HEADS, slots, 128), bf),
            jax.ShapeDtypeStruct((slots, width), f32),
            jax.ShapeDtypeStruct((4, rp + GROUP, width), bf),
            jax.ShapeDtypeStruct((4, rp + GROUP, width), bf),
            jax.ShapeDtypeStruct((2, EXPERTS, 2, part, width), bf),
            jax.ShapeDtypeStruct((width, WIDE), bf),
            jax.ShapeDtypeStruct((8, width), f32),
            jax.ShapeDtypeStruct((slots, 128), f32),
            jax.ShapeDtypeStruct((8, 128), jnp.int32),
        ),
        in_specs=[pl.BlockSpec(memory_space=pltpu.SMEM)] + [whole] * 5 + [far] * 2,
        out_specs=(whole, whole, whole, whole, far, far, far, whole, whole, whole, whole),
        scratch_shapes=[
            pltpu.VMEM((rp, slots), bf),
            pltpu.VMEM((slots, width), bf),
            pltpu.VMEM((2, slots, 256), bf),
            pltpu.VMEM((2, slots, 256), bf),
            pltpu.VMEM((2, slots, 128), bf),
            pltpu.VMEM((rp + GROUP, width), bf),
            pltpu.VMEM((rp + GROUP, width), bf),
            pltpu.VMEM((32, WIDE), bf),
            dma((2,)), dma((3,)), dma((4,)), dma((4,)), dma((4,)), dma((4,)), dma((4,)), dma((4,)), dma((4,)),
            dma((4,)), dma((4,)),
            dma((2,)), dma((2, 3)), dma((2, 3)),
            dma((3,)), dma((3, 2)), dma((3, 2)), dma((2, 4)), dma((2, 4)), dma((2, 4)), dma((2, 4)), dma((2, 4)),
        ],
        compiler_params=pltpu.CompilerParams(vmem_limit_bytes=56 * MIB, collective_id=0, has_side_effects=True),
        name="front",
    )(length, x, ids, table, g, local, w_in, w_out)


CHUNK = 32


def experts_kernel(
    n_ref, x_ref, g_ref, w_ref,
    o_ref, dx_ref, gw1_ref, gw2_ref,
    xb, gb, ob, db, acc1, acc2, blank, sem_in, sem_out, sem_zero,
):
    sources, groups, _, width = x_ref.shape
    groups = groups - 1
    rows = CHUNK * GROUP

    blank[...] = jnp.zeros_like(blank)
    xb[...] = jnp.zeros_like(xb)
    gw1_ref[...] = jnp.zeros_like(gw1_ref)
    gw2_ref[...] = jnp.zeros_like(gw2_ref)

    totals = []
    for e in range(EXPERTS):
        totals.append(lax.fori_loop(0, sources, lambda s, t, e=e: t + n_ref[s * EXPERTS + e], 0))
    first = [0]
    for e in range(EXPERTS):
        first.append(first[-1] + (totals[e] + (CHUNK - 1)) // CHUNK)
    chunks = first[EXPERTS]

    def pick(values, e):
        out = values[0]
        for i in range(1, EXPERTS):
            out = jnp.where(e == i, values[i], out)
        return out

    def locate(c):
        e = jnp.int32(0)
        for i in range(1, EXPERTS):
            e = e + jnp.where(c >= first[i], 1, 0)
        begin = (c - pick(first, e)) * CHUNK
        return e, begin, jnp.minimum(begin + CHUNK, pick(totals, e))

    def pieces(c, act):
        e, begin, end = locate(c)

        def visit(s, base):
            n = n_ref[s * EXPERTS + e]
            low = jnp.maximum(base, begin)
            size = jnp.minimum(base + n, end) - low
            skip = jnp.int32(0)
            for i in range(EXPERTS - 1):
                skip = skip + jnp.where(e > i, n_ref[s * EXPERTS + i], 0)

            @pl.when(size > 0)
            def _():
                act(s, skip + low - base, low - begin, size)

            return base + n

        lax.fori_loop(0, sources, visit, jnp.int32(0))

    def load(c, slot):
        def act(s, at, to, size):
            for k, (src, dst) in enumerate(((x_ref, xb), (g_ref, gb))):
                pltpu.make_async_copy(
                    src.at[s, pl.ds(at, size)], dst.at[slot, pl.ds(to, size)], sem_in.at[k, slot]
                ).start()

        pieces(c, act)

    def store(c, slot):
        def act(s, at, to, size):
            for k, (src, dst) in enumerate(((ob, o_ref), (db, dx_ref))):
                pltpu.make_async_copy(
                    src.at[slot, pl.ds(to, size)], dst.at[s, pl.ds(at, size)], sem_out.at[k, slot]
                ).start()

        pieces(c, act)

    def settle(c, slot, bufs, sems):
        _, begin, end = locate(c)
        for k, buf in enumerate(bufs):
            part = buf.at[slot, pl.ds(0, end - begin)]
            pltpu.make_async_copy(part, part, sems.at[k, slot]).wait()

    def used_groups(s):
        t = n_ref[s * EXPERTS]
        for e in range(1, EXPERTS):
            t = t + n_ref[s * EXPERTS + e]
        return t

    def rest(s, act):
        t = used_groups(s)

        @pl.when(groups - t > 0)
        def _():
            for k, dst in enumerate((o_ref, dx_ref)):
                act(
                    pltpu.make_async_copy(
                        blank.at[pl.ds(0, groups - t)], dst.at[s, pl.ds(t, groups - t)], sem_zero.at[k, s]
                    )
                )

    @pl.loop(0, sources)
    def _(s):
        rest(s, lambda copy: copy.start())

    @pl.when(chunks > 0)
    def _():
        load(0, 0)

    @pl.loop(0, chunks)
    def _(c):
        slot = c % 2
        e, begin, end = locate(c)

        @pl.when(c + 1 < chunks)
        def _():
            load(c + 1, 1 - slot)

        settle(c, slot, (xb, gb), sem_in)

        @pl.when(c >= 2)
        def _():
            settle(c - 2, slot, (ob, db), sem_out)

        x = xb[slot].reshape(rows, width)
        g = gb[slot].reshape(rows, width)
        g = jnp.where(iota((rows, width), 0) < (end - begin) * GROUP, g, jnp.zeros_like(g))
        w1 = w_ref[0, e]
        w2 = w_ref[1, e]
        pre = mul(x, w1)
        square = pre * pre
        t = jnp.tanh(ROOT * pre * (1.0 + CUBIC * square))
        act = (0.5 * pre * (1.0 + t)).astype(jnp.bfloat16)
        slope = 0.5 * (1.0 + t) + 0.5 * pre * (1.0 - t * t) * (ROOT * (1.0 + 3.0 * CUBIC * square))
        grad_pre = (slope * mul(g, w2, NT)).astype(jnp.bfloat16)
        ob[slot] = mul(act, w2).astype(jnp.bfloat16).reshape(CHUNK, GROUP, width)
        db[slot] = mul(grad_pre, w1, NT).astype(jnp.bfloat16).reshape(CHUNK, GROUP, width)
        store(c, slot)
        add1 = mul(x.T, grad_pre)
        add2 = mul(act.T, g)

        @pl.when(begin == 0)
        def _():
            acc1[...] = add1
            acc2[...] = add2

        @pl.when(begin > 0)
        def _():
            acc1[...] += add1
            acc2[...] += add2

        @pl.when(end == pick(totals, e))
        def _():
            gw1_ref[e] = acc1[...].astype(gw1_ref.dtype)
            gw2_ref[e] = acc2[...].astype(gw2_ref.dtype)

    @pl.when(chunks >= 2)
    def _():
        settle(chunks - 2, chunks % 2, (ob, db), sem_out)

    @pl.when(chunks >= 1)
    def _():
        settle(chunks - 1, (chunks - 1) % 2, (ob, db), sem_out)

    @pl.loop(0, sources)
    def _(s):
        rest(s, lambda copy: copy.wait())


def experts(n16, xs, gs, w):
    sources, groups, _, width = xs.shape
    hidden = w.shape[2]
    bf = jnp.bfloat16
    whole = pl.BlockSpec(memory_space=pltpu.VMEM)
    far = pl.BlockSpec(memory_space=pl.ANY)
    out_rows = jax.ShapeDtypeStruct((sources, groups - 1, GROUP, width), bf)
    return pl.pallas_call(
        experts_kernel,
        out_shape=(
            out_rows, out_rows,
            jax.ShapeDtypeStruct((EXPERTS, width, hidden), bf),
            jax.ShapeDtypeStruct((EXPERTS, hidden, width), bf),
        ),
        in_specs=[pl.BlockSpec(memory_space=pltpu.SMEM), far, far, whole],
        out_specs=(far, far, whole, whole),
        scratch_shapes=[pltpu.VMEM((2, CHUNK, GROUP, width), bf)] * 4
        + [pltpu.VMEM((width, hidden), jnp.float32), pltpu.VMEM((hidden, width), jnp.float32)]
        + [pltpu.VMEM((groups - 1, GROUP, width), bf)]
        + [pltpu.SemaphoreType.DMA((2, 2)), pltpu.SemaphoreType.DMA((2, 2)), pltpu.SemaphoreType.DMA((2, sources))],
        compiler_params=pltpu.CompilerParams(vmem_limit_bytes=56 * MIB),
        name="experts",
    )(n16, xs, gs, w)


GROUPS = 4
UNIT = 384


def back_kernel(
    len_ref, norms_ref, counts_ref, x_far, g_far, hidden_far, qkv_far, mixed_far, aug_far, pos_far, wa_far,
    o_far, dx_far, gw1_far, gw2_far,
    out_far, gx_far, gwq_ref, gwo_ref, gn_out, cnt_out, gwin_ref, gwout_ref,
    y_land, up_land, down_land, o_near, o_beside,
    x_ref, g_ref, gx_ref, qkv_ref, mixed_ref, aug_ref, pos_ref, wa_ref,
    branch_ref, gmix_ref, first_t, mixed_t,
    qa_ref, ka_ref, va_ref, oa_ref, dv_ref, dk_ref, dq_ref,
    dx_own, dx_near, dx_beside, os_ref, in_ref, sum_ref, lane_out, lane_in, hid_ref, outb_ref,
    half_land, d_land, y_small, x_small, z_small, last_out, last_in,
    gn_ref, gn_send, gn_land, gn_t,
    load_sem, aug_sem, dxs_send, dxs_recv, dxx_send, dxx_recv,
    yw_send, yw_recv, up_send, up_recv, dn_send, dn_recv, on_send, on_recv, ob_send, ob_recv, in_sem,
    ln_send, ln_recv, h_send, h_recv, d_send, d_recv, sy_send, sy_recv, sx_send, sx_recv, sz_send, sz_recv,
    l_send, l_recv, gs_send, gs_recv, hid_sem, out_sem, gx_sem,
):
    slots, width = x_ref.shape
    heads = width // HEAD_DIM
    pairs = heads // 2
    rp = dx_own.shape[1]
    piece = rp // 4
    part = gw1_far.shape[2]
    owned = gwq_ref.shape[0]
    depth = 4
    length = len_ref[0]
    scale = HEAD_DIM ** -0.5
    f32 = jnp.float32
    bf = jnp.bfloat16
    me = Place()
    z, y, x, c = me.z, me.y, me.x, me.c
    sibling, beside, across = me.at(c=1 - c), me.at(x=1 - x), me.at(y=1 - y)
    above, below = me.at(z=jnp.minimum(z + 1, depth - 1)), me.at(z=jnp.maximum(z - 1, 0))
    me.greet([sibling, beside, across, me.at(x=1 - x, c=1 - c)] + [me.at(z=z ^ k) for k in range(1, depth)])

    loads = {
        "dx": [pltpu.make_async_copy(dx_far.at[2 * xx + c], dx_own.at[xx], load_sem.at[xx]) for xx in range(2)],
    }
    plain = (
        ("x", x_far, x_ref), ("mixed", mixed_far, mixed_ref), ("hidden", hidden_far, gx_ref), ("g", g_far, g_ref),
        ("pos", pos_far, pos_ref), ("wa", wa_far, wa_ref), ("qkv", qkv_far, qkv_ref),
    )
    for i, (name, src, dst) in enumerate(plain):
        loads[name] = [pltpu.make_async_copy(src, dst, load_sem.at[2 + i])]

    def loaded(*names):
        for name in names:
            for copy in loads[name]:
                copy.wait()

    def dx_sib(xx):
        return push(dx_far.at[2 * xx + 1 - c], dx_near.at[xx], dxs_send.at[xx], dxs_recv.at[xx], sibling)

    def rows_of(i):
        return pl.ds(i * piece, piece)

    def dx_over(i):
        return push(dx_own.at[1 - x, rows_of(i)], dx_beside.at[rows_of(i)], dxx_send.at[i], dxx_recv.at[i], beside)

    gws = (gw1_far, gw2_far)

    def y_push(k, e):
        return push(gws[k].at[e, 1 - y], y_land.at[k, e], yw_send.at[k, e], yw_recv.at[k, e], across)

    def up_push(k, e, slot):
        return push(sum_ref.at[slot], up_land.at[k, e], up_send.at[k, e], up_recv.at[k, e], above)

    def down_push(k, e, slot):
        return push(sum_ref.at[slot], down_land.at[k, e], dn_send.at[k, e], dn_recv.at[k, e], below)

    def o_sib(xx):
        return push(o_far.at[2 * xx + 1 - c], o_near.at[xx], on_send.at[xx], on_recv.at[xx], sibling)

    def o_over(i, slot):
        return push(sum_ref.at[slot, pl.ds(0, piece)], o_beside.at[rows_of(i)], ob_send.at[i], ob_recv.at[i], beside)

    lanes = [(1 - x, c), (x, 1 - c), (1 - x, 1 - c)]
    lane_rows = part // 4
    mine = 2 * x + c

    def lane_push(i, arrive):
        xx, cc = lanes[i]
        src = lane_out.at[pl.ds(pl.multiple_of(lane_rows * (2 * xx + cc), 16), lane_rows)]
        dst = lane_in.at[2 * xx + cc] if arrive else lane_in.at[mine]
        return push(src, dst, ln_send.at[i], ln_recv.at[i], me.at(x=xx, c=cc))

    weights = [(k, i) for i in range(depth) for k in (0, 1)]

    class WeightItem:
        def __init__(self, k, i):
            self.k, self.m = k, 3 - i
            self.rows = part

        def e(self):
            return z ^ self.m

        def flags(self):
            e = self.e()
            if self.m == 0:
                return z > 0, z < depth - 1
            return (e > z) & (z > 0), (e < z) & (z < depth - 1)

        def ready(self):
            k, e = self.k, self.e()
            y_push(k, e).wait_recv()
            for flag, copy in zip(self.flags(), (up_push, down_push)):
                @pl.when(flag)
                def _():
                    copy(k, e, 0).wait_recv()

        def sources(self):
            k, e = self.k, self.e()
            a, b = self.flags()
            return [
                (gws[k].at[e, y], None), (y_land.at[k, e], None), (up_land.at[k, e], a), (down_land.at[k, e], b)
            ]

        def finish(self, total, slot):
            k, e = self.k, self.e()
            if self.m:
                def put(rows, value):
                    sum_ref[slot, rows, :] = value.astype(bf)

                total(put)

                @pl.when(e > z)
                def _():
                    up_push(k, e, slot).start()

                @pl.when(e < z)
                def _():
                    down_push(k, e, slot).start()
            elif k == 1:
                def put(rows, value):
                    gwout_ref[rows, :] = value

                total(put)
            else:
                def put(rows, value):
                    lane_out[rows, :] = value.astype(bf)

                total(put)
                for i in range(3):
                    lane_push(i, False).start()
                lane_in[mine] = lane_out[pl.ds(pl.multiple_of(lane_rows * mine, 16), lane_rows), :]

        def sent(self, slot):
            k, e = self.k, self.e()
            if self.m:
                @pl.when(e > z)
                def _():
                    up_push(k, e, slot).wait_send()

                @pl.when(e < z)
                def _():
                    down_push(k, e, slot).wait_send()

    class OutItem:
        def __init__(self, stage, i):
            self.stage, self.i = stage, i
            self.rows = piece

        def ready(self):
            if self.i == 0:
                o_sib(1 - x if self.stage == 0 else x).wait_recv()
            if self.stage:
                o_over(self.i, 0).wait_recv()

        def sources(self):
            xx = 1 - x if self.stage == 0 else x
            rows = rows_of(self.i)
            found = [(o_far.at[2 * xx + c, rows], None), (o_near.at[xx, rows], None)]
            if self.stage:
                found.append((o_beside.at[rows], None))
            return found

        def finish(self, total, slot):
            if self.stage == 0:
                def put(rows, value):
                    sum_ref[slot, rows, :] = value.astype(bf)

                total(put)
                o_over(self.i, slot).start()
            else:
                base = self.i * piece

                def put(rows, value):
                    os_ref[pl.ds(base + rows.start, rows.size), :] = value.astype(bf)

                total(put)

        def sent(self, slot):
            if self.stage == 0:
                o_over(self.i, slot).wait_send()

    w_items = [WeightItem(k, i) for k, i in [(kk, ii) for ii in range(depth) for kk in (0, 1)]]
    o_items = [OutItem(s, i) for s in range(2) for i in range(4)]
    order = [
        w_items[0], w_items[1], o_items[0], o_items[1], w_items[2], o_items[2], o_items[3], w_items[3],
        o_items[4], o_items[5], w_items[4], o_items[6], o_items[7], w_items[5], w_items[6], w_items[7],
    ]
    senders = [item for item in order if (isinstance(item, WeightItem) and item.m) or getattr(item, "stage", 1) == 0]
    sum_slot = {id(item): n % 3 for n, item in enumerate(senders)}
    state = {"next": 0, "y": 0}

    def y_next():
        if state["y"] < len(w_items):
            item = w_items[state["y"]]
            y_push(item.k, item.e()).start()
            state["y"] += 1

    def fetch(item, slot):
        for n, (src, flag) in enumerate(item.sources()):
            copy = pltpu.make_async_copy(src, in_ref.at[slot, n, pl.ds(0, item.rows)], in_sem.at[slot, n])
            if flag is None:
                copy.start()
            else:
                pl.when(flag)(copy.start)

    def finish(item, slot):
        sources = item.sources()
        for n, (src, flag) in enumerate(sources):
            copy = pltpu.make_async_copy(src, in_ref.at[slot, n, pl.ds(0, item.rows)], in_sem.at[slot, n])
            if flag is None:
                copy.wait()
            else:
                pl.when(flag)(copy.wait)
        place = sum_slot.get(id(item), 0)
        if id(item) in sum_slot:
            n = senders.index(item)
            if n >= 3:
                senders[n - 3].sent(place)

        tile = 16

        def total(put):
            @pl.loop(0, item.rows // tile)
            def _(i):
                rows = pl.ds(pl.multiple_of(i * tile, tile), tile)
                value = None
                for n, (src, flag) in enumerate(sources):
                    term = in_ref[slot, n, rows, :].astype(f32)
                    if flag is not None:
                        term = jnp.where(flag, term, 0.0)
                    value = term if value is None else value + term
                put(rows, value)

        item.finish(total, place)

    def tick():
        n = state["next"]
        if n > len(order):
            return
        if n < len(order):
            order[n].ready()
            fetch(order[n], n % 2)
            if isinstance(order[n], WeightItem):
                y_next()
        if n > 0:
            finish(order[n - 1], (n - 1) % 2)
        state["next"] += 1

    def home(g, side):
        store = dx_own if g < 2 else dx_near
        return store, side, pl.ds((g % 2) * UNIT, UNIT)

    def put_unit(g, u, value):
        store, side, _ = home(g, u // 3)
        lo = (g % 2) * UNIT + (u % 3) * 128
        store[side, 0:width, lo : lo + 128] = value.astype(bf)

    def block_rows(zz, yy, xx):
        return pl.ds(pl.multiple_of(2 * owned * (4 * zz + 2 * yy + xx), 16), 2 * owned)

    def block(g, zz, yy, xx):
        store, _, cols = home(g, 0)
        return store.at[c, block_rows(zz, yy, xx), cols]

    def half_push(g):
        store, _, cols = home(g, 0)
        return push(store.at[1 - c, pl.ds(0, width), cols], half_land.at[g], h_send.at[g], h_recv.at[g], sibling)

    def d_push(g, zz, peer):
        return push(block(g, zz, 1 - y, 1 - x), d_land.at[g, zz], d_send.at[g, zz], d_recv.at[g, zz], peer)

    def ys_push(g, zz):
        return push(block(g, zz, 1 - y, x), y_small.at[g, zz], sy_send.at[g, zz], sy_recv.at[g, zz], across)

    def xs_push(g, zz):
        return push(block(g, zz, y, 1 - x), x_small.at[g, zz], sx_send.at[g, zz], sx_recv.at[g, zz], beside)

    def zs_push(g, k, source):
        zz = z ^ k
        return push(block(g, zz, y, x), z_small.at[g, source], sz_send.at[g, k - 1], sz_recv.at[g, source], me.at(z=zz))

    def last_push(g):
        return push(last_out.at[g], last_in.at[g], l_send.at[g], l_recv.at[g], sibling)

    def small_a(g):
        half_push(g).wait_recv()
        store, _, cols = home(g, 0)

        @pl.loop(0, width // 64)
        def _(i):
            rows = pl.ds(pl.multiple_of(i * 64, 64), 64)
            store[c, rows, cols] = (store[c, rows, cols].astype(f32) + half_land[g, rows, :].astype(f32)).astype(bf)

        for zz in range(depth):
            d_push(g, zz, beside if zz % 2 == 0 else across).start()

    def small_b(g):
        store, _, cols = home(g, 0)
        for zz in range(depth):
            d_push(g, zz, beside).wait_recv()
            rows = block_rows(zz, 1 - y, x) if zz % 2 == 0 else block_rows(zz, y, 1 - x)
            store[c, rows, cols] = (store[c, rows, cols].astype(f32) + d_land[g, zz].astype(f32)).astype(bf)
            ys_push(g, zz).start()
            xs_push(g, zz).start()

    def small_c(g):
        store, _, cols = home(g, 0)
        for k in (3, 2, 1, 0):
            zz = z ^ k
            ys_push(g, zz).wait_recv()
            xs_push(g, zz).wait_recv()
            rows = block_rows(zz, y, x)
            value = store[c, rows, cols].astype(f32) + y_small[g, zz].astype(f32) + x_small[g, zz].astype(f32)
            store[c, rows, cols] = value.astype(bf)
            if k:
                zs_push(g, k, z).start()

    def columns(g, side):
        if g == 0:
            return [(gwo_ref, side * UNIT + 128 * i) for i in range(3)]
        found = []
        for i in range(3):
            u = 3 * side + i
            found.append((gwq_ref, (u // 2) * width + 256 * (g - 1) + (u % 2) * 128))
        return found

    def place_columns(g, side, value):
        for i, (ref, lo) in enumerate(columns(g, side)):
            ref[:, lo : lo + 128] = value[:, 128 * i : 128 * i + 128]

    def small_d(g):
        store, _, cols = home(g, 0)
        for k in range(1, depth):
            zs_push(g, k, z ^ k).wait_recv()
        value = store[c, block_rows(z, y, x), cols].astype(f32)
        for k in range(1, depth):
            value = value + z_small[g, z ^ k].astype(f32)
        own_part = jnp.where(c == 0, value[0:owned], value[owned:])
        last_out[g] = jnp.where(c == 0, value[owned:], value[0:owned])
        last_push(g).start()
        for side in range(2):
            @pl.when(c == side)
            def _():
                place_columns(g, side, own_part)

    def small_e(g):
        last_push(g).wait_recv()
        for side in range(2):
            @pl.when(c != side)
            def _():
                place_columns(g, side, last_in[g])

    def small_end(g):
        half_push(g).wait_send()
        for zz in range(depth):
            d_push(g, zz, beside).wait_send()
            ys_push(g, zz).wait_send()
            xs_push(g, zz).wait_send()
        for k in range(1, depth):
            zs_push(g, k, z).wait_send()
        last_push(g).wait_send()

    for xx in range(2):
        dx_sib(xx).start()
    for name in ("dx", "x", "mixed", "hidden", "g", "pos", "wa", "qkv"):
        for copy in loads[name]:
            copy.start()
    gn_ref[...] = jnp.zeros_like(gn_ref)
    in_ref[...] = jnp.zeros_like(in_ref)
    dx_sib(1 - x).wait_recv()
    loaded("dx")
    for i in range(4):
        rows = rows_of(i)
        dx_own[1 - x, rows, :] = (dx_own[1 - x, rows, :].astype(f32) + dx_near[1 - x, rows, :].astype(f32)).astype(bf)
        dx_over(i).start()
    for _ in range(3):
        y_next()
    for xx in range(2):
        o_sib(xx).start()

    loaded("x", "mixed")

    @pl.loop(0, slots // ROWS)
    def _(i):
        rows = pl.ds(i * ROWS, ROWS)
        normal, _ = layer_stats(x_ref[rows, :].astype(f32))
        branch_ref[rows, :] = (normal * norms_ref[0:1, :] + norms_ref[2:3, :]).astype(bf)

    first_t[...] = branch_ref[...].T
    mixed_t[...] = mixed_ref[...].T
    loaded("hidden", "g", "pos", "wa", "qkv")
    dx_sib(x).wait_recv()
    for i in range(4):
        rows = rows_of(i)
        dx_over(i).wait_recv()
        dx_own[x, rows, :] = (
            dx_own[x, rows, :].astype(f32) + dx_near[x, rows, :].astype(f32) + dx_beside[rows, :].astype(f32)
        ).astype(bf)

    @pl.loop(0, slots // ROWS)
    def _(i):
        rows = pl.ds(i * ROWS, ROWS)
        place = pos_ref[rows, 0:1].astype(jnp.int32)
        pick = (iota((ROWS, rp), 1) == place).astype(bf)
        grad = mul(pick, dx_own[x])
        normal, scaled = layer_stats(gx_ref[rows, :])
        gn_ref[1:2, :] += jnp.sum(grad * normal, axis=0, keepdims=True)
        gn_ref[3:4, :] += jnp.sum(grad, axis=0, keepdims=True)
        grad_hidden = g_ref[rows, :].astype(f32) + norm_backward(grad, normal, scaled, norms_ref[1:2, :])
        gx_ref[rows, :] = grad_hidden
        branch = grad_hidden.astype(bf)
        branch_ref[rows, :] = branch
        gmix_ref[rows, :] = mul(branch, wa_ref[:, HALF + width : HALF + 2 * width], NT).astype(bf)

    for i in range(4):
        dx_over(i).wait_send()
    tile = width // 3

    @pl.loop(0, 3)
    def _(i):
        rows = pl.ds(i * tile, tile)
        value = mul(mixed_t[rows, :], branch_ref[...]).astype(bf)
        for side in range(2):
            dx_own[side, rows, 0:UNIT] = value[:, side * UNIT : (side + 1) * UNIT]

    half_push(0).start()
    tick()
    tick()

    def group_product(g):
        j = g - 1
        store_units = []
        for t in range(3):
            lo = t * width + 256 * j
            for i in range(3):
                rows = slice(i * tile, (i + 1) * tile)
                value = mul(first_t[rows, :], qkv_ref[:, lo : lo + 256]).astype(bf)
                for n in range(2):
                    u = 2 * t + n
                    store, side, _ = home(g, u // 3)
                    at = (g % 2) * UNIT + (u % 3) * 128
                    store[side, rows, at : at + 128] = value[:, n * 128 : (n + 1) * 128]
        half_push(g).start()

    plan = [
        [tick, lambda: small_a(0), tick],
        [tick, lambda: small_b(0), tick, lambda: group_product(1)],
        [tick, lambda: small_c(0), lambda: small_a(1), tick],
        [tick, lambda: small_d(0), lambda: small_b(1), tick, lambda: group_product(2)],
        [tick, lambda: small_e(0), lambda: small_c(1), lambda: small_a(2), tick],
        [tick, lambda: small_d(1), lambda: small_b(2), tick, lambda: group_product(3)],
    ]

    lane = iota((slots, 128), 1)
    key_bias = jnp.where(iota((slots, 128), 0) < length, 0.0, NEGATIVE).astype(bf)
    causal = iota((ROWS, ROWS), 0) <= iota((ROWS, ROWS), 1)

    def aug_load(p, slot):
        return pltpu.make_async_copy(aug_far.at[pl.ds(2 * p, 2)], aug_ref.at[slot], aug_sem.at[slot])

    aug_load(0, 0).start()

    @pl.loop(0, pairs)
    def _(p):
        slot = p % 2

        @pl.when(p + 1 < pairs)
        def _():
            aug_load(p + 1, 1 - slot).start()

        aug_load(p, slot).wait()
        cols = pl.ds(p * 128, 128)
        k_cols = pl.ds(width + p * 128, 128)
        v_cols = pl.ds(2 * width + p * 128, 128)
        q = qkv_ref[:, cols]
        q_hi = (q.astype(f32) * (scale * LOG2E)).astype(bf)
        k = qkv_ref[:, k_cols]
        v = qkv_ref[:, v_cols]
        do = gmix_ref[:, cols]
        prod = do.astype(f32) * mixed_ref[:, cols].astype(f32)
        k_t = k.T
        zero = jnp.zeros_like(q)
        one = jnp.ones_like(q)
        for half in range(2):
            own = own_lanes(lane, half)
            extra = extra_lane(half)
            parts = (lane > extra) & (lane <= extra + 3)
            qa_ref[half, :, 0:128] = jnp.where(own, q_hi, zero)
            qa_ref[half, :, 128:256] = aug_ref[slot, half]
            ka_ref[half, :, 0:128] = k
            ka_ref[half, :, 128:256] = jnp.where(
                own, k, jnp.where(lane == extra, key_bias, jnp.where(parts, one, zero))
            )
            va_ref[half, :, :] = jnp.where(own, v, jnp.where(parts, one, zero))
            minus = -jnp.sum(jnp.where(own, prod, 0.0), axis=1, keepdims=True)
            a, b, d = three_parts(jnp.broadcast_to(minus, (slots, 128)))
            oa_ref[half, :, :] = jnp.where(
                own, do,
                jnp.where(lane == extra + 1, a, jnp.where(lane == extra + 2, b, jnp.where(lane == extra + 3, d, zero))),
            )
        for half in range(2):
            k_own = k_t[half * HEAD_DIM : (half + 1) * HEAD_DIM, :]
            heads_rows = slice(half * HEAD_DIM, (half + 1) * HEAD_DIM)
            for j in range(slots // ROWS):
                keys = slice(j * ROWS, (j + 1) * ROWS)
                late = slice(j * ROWS, slots)
                s = mul(ka_ref[half, keys, :], qa_ref[half, late, :], NT)
                diag = jnp.where(causal, s[:, :ROWS], NEGATIVE)
                s = diag if j == slots // ROWS - 1 else jnp.concatenate([diag, s[:, ROWS:]], axis=1)
                probs = jnp.exp2(s)
                dp = mul(va_ref[half, keys, :], oa_ref[half, late, :], NT)
                ds = (probs * dp).astype(bf)
                probs = probs.astype(bf)
                dv_ref[half, keys, :] = mul(probs, gmix_ref[late, cols])
                dk_ref[half, keys, :] = mul(ds, qkv_ref[late, cols])
                dq = mul(k_own[:, keys], ds)
                if j == 0:
                    dq_ref[heads_rows, late] = dq
                else:
                    dq_ref[heads_rows, late] += dq
        first = lane < HEAD_DIM
        qkv_ref[:, cols] = (dq_ref[...].T * scale).astype(bf)
        qkv_ref[:, k_cols] = (jnp.where(first, dk_ref[0], dk_ref[1]) * scale).astype(bf)
        qkv_ref[:, v_cols] = jnp.where(first, dv_ref[0], dv_ref[1]).astype(bf)
        for i in range(pairs):
            @pl.when(p == i)
            def _():
                for step in plan[i]:
                    step()

    @pl.loop(0, slots // ROWS)
    def _(i):
        rows = pl.ds(i * ROWS, ROWS)
        normal, scaled = layer_stats(x_ref[rows, :].astype(f32))
        grad = mul(qkv_ref[rows, : 2 * width], wa_ref[:, : 2 * width], NT) + mul(
            qkv_ref[rows, 2 * width :], wa_ref[:, HALF : HALF + width], NT
        )
        gn_ref[0:1, :] += jnp.sum(grad * normal, axis=0, keepdims=True)
        gn_ref[2:3, :] += jnp.sum(grad, axis=0, keepdims=True)
        gx_ref[rows, :] += norm_backward(grad, normal, scaled, norms_ref[0:1, :])

    gx_out = pltpu.make_async_copy(gx_ref, gx_far, gx_sem)
    gx_out.start()
    counts = jnp.where(iota((8, 128), 0) == iota((8, 128), 1), counts_ref[...], 0).astype(f32)
    gn_ref[4:5, 0:128] = jnp.sum(counts, axis=0, keepdims=True)
    gn_peers = [sibling, beside, across, me.at(z=z ^ 1), me.at(z=z ^ 2)]

    def gn_push(i):
        return push(gn_send.at[i], gn_land.at[i], gs_send.at[i], gs_recv.at[i], gn_peers[i])

    def gn_start(i):
        gn_send[i] = gn_ref[...]
        gn_push(i).start()

    def gn_end(i):
        gn_push(i).wait_recv()
        gn_ref[...] += gn_land[i]

    gn_start(0)
    small_a(3)
    small_c(2)
    small_e(1)
    gn_end(0)
    gn_start(1)
    small_b(3)
    small_d(2)
    gn_end(1)
    gn_start(2)
    while state["next"] <= len(order):
        tick()
    gn_end(2)
    gn_start(3)
    small_c(3)
    small_e(2)
    gn_end(3)
    gn_start(4)

    def hidden_load(i):
        return pltpu.make_async_copy(hidden_far.at[pl.ds(i * ROWS, ROWS)], hid_ref.at[i % 2], hid_sem.at[i % 2])

    def out_store(i):
        return pltpu.make_async_copy(outb_ref.at[i % 2], out_far.at[pl.ds(i * ROWS, ROWS)], out_sem.at[i % 2])

    blocks = slots // ROWS
    hidden_load(0).start()
    for i in range(blocks):
        if i + 1 < blocks:
            hidden_load(i + 1).start()
        place = pos_ref[i * ROWS : (i + 1) * ROWS, 0:1].astype(jnp.int32)
        pick = (iota((ROWS, rp), 1) == place).astype(bf)
        value = mul(pick, os_ref[...])
        hidden_load(i).wait()
        if i >= 2:
            out_store(i - 2).wait()
        outb_ref[i % 2] = (hid_ref[i % 2] + value).astype(bf)
        out_store(i).start()

    gn_end(4)
    gn_t[...] = jnp.concatenate([gn_ref[...], jnp.zeros((120, width), f32)], axis=0).T
    gn_out[...] = gn_t[pl.ds(pl.multiple_of(owned * (8 * z + 4 * y + 2 * x + c), 8), owned), :]
    cnt_out[...] = gn_ref[:, 0:128]
    small_d(3)
    for i in range(3):
        lane_push(i, True).wait_recv()
    for s in range(4):
        for b in range(2):
            lo = (4 * b + s) * part
            gwin_ref[:, lo : lo + part] = lane_in[s, :, b * part : (b + 1) * part].astype(f32)
    small_e(3)

    for i in range(blocks - 2, blocks):
        out_store(i).wait()
    gx_out.wait()
    for item in senders[-3:]:
        item.sent(sum_slot[id(item)])
    for xx in range(2):
        dx_sib(xx).wait_send()
        o_sib(xx).wait_send()
    for item in w_items:
        y_push(item.k, item.e()).wait_send()
    for i in range(3):
        lane_push(i, False).wait_send()
    for i in range(5):
        gn_push(i).wait_send()
    for g in range(GROUPS):
        small_end(g)


def back(length, norms, counts, x, g, hidden, qkv, mixed, aug, pos, wa, o_part, dx_part, gw1, gw2, owned):
    slots, width = x.shape
    rp = dx_part.shape[1]
    part = gw1.shape[2]
    bf = jnp.bfloat16
    f32 = jnp.float32
    whole = pl.BlockSpec(memory_space=pltpu.VMEM)
    far = pl.BlockSpec(memory_space=pl.ANY)
    dma = pltpu.SemaphoreType.DMA
    v = pltpu.VMEM
    out = jax.ShapeDtypeStruct
    return pl.pallas_call(
        back_kernel,
        out_shape=(
            out((slots, width), bf),
            out((slots, width), f32),
            out((owned, 3 * width), f32),
            out((owned, width), f32),
            out((owned, 128), f32),
            out((8, 128), f32),
            out((part // 4, 8 * part), f32),
            out((part, width), f32),
            out((2, EXPERTS, part, width), bf),
            out((2, EXPERTS, part, width), bf),
            out((2, EXPERTS, part, width), bf),
            out((2, rp, width), bf),
            out((rp, width), bf),
        ),
        in_specs=[pl.BlockSpec(memory_space=pltpu.SMEM), whole, whole] + [far] * 12,
        out_specs=(far, far, whole, whole, whole, whole, whole, whole, far, far, far, far, far),
        scratch_shapes=[
            v((slots, width), bf), v((slots, width), bf), v((slots, width), f32), v((slots, 3 * width), bf),
            v((slots, width), bf), v((2, 2, slots, 128), bf), v((slots, 128), f32), v((width, WIDE), bf),
            v((slots, width), bf), v((slots, width), bf), v((width, slots), bf), v((width, slots), bf),
            v((2, slots, 256), bf), v((2, slots, 256), bf), v((2, slots, 128), bf), v((2, slots, 128), bf),
            v((2, slots, 128), f32), v((2, slots, 128), f32), v((128, slots), f32),
            v((2, rp, width), bf), v((2, rp, width), bf), v((rp, width), bf), v((rp, width), bf),
            v((2, 4, part, width), bf), v((3, part, width), bf), v((part, width), bf), v((4, part // 4, width), bf),
            v((2, ROWS, width), f32), v((2, ROWS, width), bf),
            v((GROUPS, width, UNIT), bf),
            v((GROUPS, 4, 2 * owned, UNIT), bf), v((GROUPS, 4, 2 * owned, UNIT), bf),
            v((GROUPS, 4, 2 * owned, UNIT), bf), v((GROUPS, 4, 2 * owned, UNIT), bf),
            v((GROUPS, owned, UNIT), f32), v((GROUPS, owned, UNIT), f32),
            v((8, width), f32), v((5, 8, width), f32), v((5, 8, width), f32), v((width, 128), f32),
            dma((9,)), dma((2,)), dma((2,)), dma((2,)), dma((4,)), dma((4,)),
            dma((2, 4)), dma((2, 4)), dma((2, 4)), dma((2, 4)), dma((2, 4)), dma((2, 4)),
            dma((2,)), dma((2,)), dma((4,)), dma((4,)), dma((2, 4)),
            dma((3,)), dma((3,)), dma((4,)), dma((4,)), dma((4, 4)), dma((4, 4)), dma((4, 4)), dma((4, 4)),
            dma((4, 4)), dma((4, 4)), dma((4, 3)), dma((4, 4)),
            dma((4,)), dma((4,)), dma((5,)), dma((5,)), dma((2,)), dma((2,)), dma(()),
        ],
        compiler_params=pltpu.CompilerParams(vmem_limit_bytes=62 * MIB, collective_id=1, has_side_effects=True),
        name="back",
    )(length, norms, counts, x, g, hidden, qkv, mixed, aug, pos, wa, o_part, dx_part, gw1, gw2)


def plane_body(
    tokens, token_ids, lengths, hash_table, w_qkv, w_attn_out, norm_gains, norm_biases, w_in, w_out, cotangent
):
    slots, width = tokens.shape
    bf = jnp.bfloat16
    rp = padded_rows(slots)
    part = w_out.shape[0]
    owned = w_qkv.shape[0]

    norm_cols = jnp.concatenate([norm_gains, norm_biases], axis=1)
    local = jnp.concatenate(
        [w_qkv[:, : 2 * width], jnp.pad(norm_cols, ((0, 0), (0, 124))), w_qkv[:, 2 * width :], w_attn_out], axis=1
    )
    local = jnp.pad(local, ((0, 32 - local.shape[0]), (0, WIDE - local.shape[1])))
    table = jnp.pad(hash_table, (0, (-hash_table.shape[0]) % 8192)).reshape(64, 128).T.astype(bf)
    qkv, mixed, aug, hidden, xs, gs, w, wa, norms, pos, counts = front(
        lengths, tokens, token_ids.reshape(1, slots), table, cotangent, local, w_in, w_out
    )
    xs = xs.reshape(4, rp // GROUP + 1, GROUP, width)
    gs = gs.reshape(4, rp // GROUP + 1, GROUP, width)
    n16 = xs[:, rp // GROUP, :EXPERTS, 0].astype(jnp.int32).reshape(-1)
    o_part, dx_part, gw1, gw2 = experts(n16, xs, gs, w.reshape(2, EXPERTS, 2 * part, width))
    out, gx, gwq, gwo, gn, cnt, gwin, gwout = back(
        lengths, norms, counts, tokens, cotangent, hidden, qkv, mixed, aug, pos, wa,
        o_part.reshape(4, rp, width), dx_part.reshape(4, rp, width),
        gw1.reshape(EXPERTS, 2, part, width), gw2.reshape(EXPERTS, 2, part, width), owned,
    )[:8]
    return (out, gx, gwq, gwo, gn[:, 0:2], gn[:, 2:4], gwin, gwout, cnt[4, :EXPERTS].astype(jnp.int32))


def solution(mesh):
    placed = (
        P(("dp", "fsdp"), None),
        P(("dp", "fsdp")),
        P(("dp", "fsdp")),
        P(),
        P(("dp", "fsdp"), None),
        P(("dp", "fsdp"), None),
        P(("dp", "fsdp"), None),
        P(("dp", "fsdp"), None),
        P(("dp", "fsdp"), None),
        P(("dp", "fsdp"), None),
        P(("dp", "fsdp"), None),
    )
    by_plane = mesh.shape["dp"] == EXPERTS and mesh.shape["fsdp"] == 8
    return jax.shard_map(
        plane_body if by_plane else body,
        mesh=mesh,
        in_specs=placed,
        out_specs=(
            P(("dp", "fsdp"), None),
            P(("dp", "fsdp"), None),
            P(("dp", "fsdp"), None),
            P(("dp", "fsdp"), None),
            P(("dp", "fsdp"), None),
            P(("dp", "fsdp"), None),
            P(("dp", "fsdp"), None),
            P(("dp", "fsdp"), None),
            P(),
        ),
        check_vma=False,
    )
```

```python
import functools

import jax
import jax.numpy as jnp
from jax import lax
from jax.experimental import pallas as pl
from jax.experimental.pallas import tpu as pltpu
from jax.sharding import PartitionSpec as P

D = 768
HEADS = 12
HEAD_DIM = 64
EXPERTS = 4
BLOCK = 128


EPSILON = 1e-05
NEGATIVE = -1e30


def layer_stats(values):
    average = jnp.mean(values, axis=-1, keepdims=True)
    centred = values - average
    scaled = lax.rsqrt(jnp.mean(centred * centred, axis=-1, keepdims=True) + EPSILON)
    return (centred * scaled, scaled)


def norm_backward(grad_normed, normal, scaled, gain_col):
    grad_scaled = grad_normed * gain_col
    first_mean = jnp.mean(grad_scaled, axis=-1, keepdims=True)
    second_mean = jnp.mean(grad_scaled * normal, axis=-1, keepdims=True)
    return scaled * (grad_scaled - first_mean - normal * second_mean)


def head_groups(heads):
    group_width = 4
    return [(start, start + group_width) for start in range(0, heads, group_width)]


def allowed_keys(length, seq_len):
    places = jnp.arange(seq_len, dtype=jnp.int32)
    return (places[None, :] <= places[:, None]) & (places[None, :] < length)


def masked_scores(query_part, key_part, allowed):
    scale = query_part.shape[-1] ** (-0.5)
    raw = (
        jnp.einsum("qhd,khd->hqk", query_part, key_part, preferred_element_type=jnp.float32) * scale
    )
    return jnp.where(allowed[None], raw, NEGATIVE)


def attention_forward(entry):
    queries, keys, values, length = entry
    allowed = allowed_keys(length, queries.shape[0])
    mixed_parts = []
    total_parts = []
    for start, finish in head_groups(queries.shape[1]):
        scores = masked_scores(queries[:, start:finish], keys[:, start:finish], allowed)
        highest = jnp.max(scores, axis=-1, keepdims=True)
        totals = highest + jnp.log(jnp.sum(jnp.exp(scores - highest), axis=-1, keepdims=True))
        weights = jnp.exp(scores - totals).astype(jnp.bfloat16)
        mixed_parts.append(
            jnp.einsum(
                "hqk,khd->qhd", weights, values[:, start:finish], preferred_element_type=jnp.float32
            ).astype(jnp.bfloat16)
        )
        total_parts.append(totals[..., 0])
    return (jnp.concatenate(mixed_parts, axis=1), jnp.concatenate(total_parts, axis=0))


def attention_backward(entry):
    queries, keys, values, totals, grad_mixed, length = entry
    allowed = allowed_keys(length, queries.shape[0])
    scale = queries.shape[-1] ** (-0.5)
    query_parts, key_parts, value_parts = ([], [], [])
    for start, finish in head_groups(queries.shape[1]):
        scores = masked_scores(queries[:, start:finish], keys[:, start:finish], allowed)
        weights = jnp.exp(scores - totals[start:finish][..., None])
        grad_weights = jnp.einsum(
            "qhd,khd->hqk",
            grad_mixed[:, start:finish],
            values[:, start:finish],
            preferred_element_type=jnp.float32,
        )
        inner_sum = jnp.sum(grad_weights * weights, axis=-1, keepdims=True)
        grad_scores = (weights * (grad_weights - inner_sum)).astype(jnp.bfloat16)
        value_parts.append(
            jnp.einsum(
                "hqk,qhd->khd",
                weights.astype(jnp.bfloat16),
                grad_mixed[:, start:finish],
                preferred_element_type=jnp.float32,
            )
        )
        query_parts.append(
            jnp.einsum(
                "hqk,khd->qhd",
                grad_scores,
                keys[:, start:finish],
                preferred_element_type=jnp.float32,
            )
            * scale
        )
        key_parts.append(
            jnp.einsum(
                "hqk,qhd->khd",
                grad_scores,
                queries[:, start:finish],
                preferred_element_type=jnp.float32,
            )
            * scale
        )
    return (
        jnp.concatenate(query_parts, axis=1),
        jnp.concatenate(key_parts, axis=1),
        jnp.concatenate(value_parts, axis=1),
    )


def segment_table(group_ends, total_rows, block_rows):
    block_count = total_rows // block_rows
    block_starts = jnp.arange(block_count, dtype=jnp.int32) * block_rows
    points = jnp.sort(jnp.concatenate([block_starts, group_ends]))
    finishes = jnp.concatenate([points[1:], jnp.full((1,), total_rows, jnp.int32)])
    blocks = jnp.minimum(points // block_rows, block_count - 1)
    owners = jnp.sum((group_ends[None, :] <= points[:, None]).astype(jnp.int32), axis=1)
    active = (finishes > points) & (owners < group_ends.shape[0])
    owners = jnp.minimum(owners, group_ends.shape[0] - 1)
    return (points, finishes, blocks, owners, active)


def expert_forward(sorted_rows, inner_all, outer_all, table, block_rows):
    model_width = sorted_rows.shape[1]
    hidden_width = inner_all.shape[1]

    def visit(state, entry):
        start, finish, block_id, owner, live = entry

        def compute(inner_state):
            pre_all, result_all = inner_state
            base = block_id * block_rows
            rows_here = lax.dynamic_slice_in_dim(sorted_rows, base, block_rows, 0)
            inner = lax.dynamic_slice_in_dim(inner_all, owner * model_width, model_width, 0)
            outer = lax.dynamic_slice_in_dim(outer_all, owner * hidden_width, hidden_width, 0)
            places = base + jnp.arange(block_rows, dtype=jnp.int32)
            inside = ((places >= start) & (places < finish))[:, None]
            pre = jnp.dot(rows_here, inner, preferred_element_type=jnp.float32)
            result = jnp.dot(
                jax.nn.gelu(pre).astype(jnp.bfloat16), outer, preferred_element_type=jnp.float32
            )
            old_pre = lax.dynamic_slice_in_dim(pre_all, base, block_rows, 0)
            old_result = lax.dynamic_slice_in_dim(result_all, base, block_rows, 0)
            pre_all = lax.dynamic_update_slice_in_dim(
                pre_all, jnp.where(inside, pre, old_pre), base, 0
            )
            result_all = lax.dynamic_update_slice_in_dim(
                result_all, jnp.where(inside, result, old_result), base, 0
            )
            return (pre_all, result_all)

        return (lax.cond(live, compute, lambda same: same, state), None)

    start_state = (
        jnp.zeros((sorted_rows.shape[0], hidden_width), jnp.float32),
        jnp.zeros((sorted_rows.shape[0], model_width), jnp.float32),
    )
    final_state, _ = lax.scan(visit, start_state, table)
    return final_state


def expert_backward(sorted_rows, pre_all, grad_sorted, inner_all, outer_all, table, block_rows):
    model_width = sorted_rows.shape[1]
    hidden_width = inner_all.shape[1]

    def visit(state, entry):
        start, finish, block_id, owner, live = entry

        def compute(inner_state):
            grad_rows, grad_inner, grad_outer = inner_state
            base = block_id * block_rows
            rows_here = lax.dynamic_slice_in_dim(sorted_rows, base, block_rows, 0)
            pre = lax.dynamic_slice_in_dim(pre_all, base, block_rows, 0)
            inner = lax.dynamic_slice_in_dim(inner_all, owner * model_width, model_width, 0)
            outer = lax.dynamic_slice_in_dim(outer_all, owner * hidden_width, hidden_width, 0)
            places = base + jnp.arange(block_rows, dtype=jnp.int32)
            inside = ((places >= start) & (places < finish))[:, None]
            grad_block = jnp.where(
                inside,
                lax.dynamic_slice_in_dim(grad_sorted, base, block_rows, 0),
                jnp.zeros((), jnp.bfloat16),
            )
            activated, gelu_pull = jax.vjp(jax.nn.gelu, pre)
            outer_piece = jnp.einsum(
                "tf,td->fd",
                activated.astype(jnp.bfloat16),
                grad_block,
                preferred_element_type=jnp.float32,
            )
            grad_act = jnp.einsum(
                "td,fd->tf", grad_block, outer, preferred_element_type=jnp.float32
            )
            grad_pre = gelu_pull(grad_act)[0].astype(jnp.bfloat16)
            inner_piece = jnp.einsum(
                "td,tf->df", rows_here, grad_pre, preferred_element_type=jnp.float32
            )
            rows_piece = jnp.einsum(
                "tf,df->td", grad_pre, inner, preferred_element_type=jnp.float32
            )
            old_rows = lax.dynamic_slice_in_dim(grad_rows, base, block_rows, 0)
            grad_rows = lax.dynamic_update_slice_in_dim(grad_rows, old_rows + rows_piece, base, 0)
            old_inner = lax.dynamic_slice_in_dim(grad_inner, owner * model_width, model_width, 0)
            grad_inner = lax.dynamic_update_slice_in_dim(
                grad_inner, old_inner + inner_piece, owner * model_width, 0
            )
            old_outer = lax.dynamic_slice_in_dim(grad_outer, owner * hidden_width, hidden_width, 0)
            grad_outer = lax.dynamic_update_slice_in_dim(
                grad_outer, old_outer + outer_piece, owner * hidden_width, 0
            )
            return (grad_rows, grad_inner, grad_outer)

        return (lax.cond(live, compute, lambda same: same, state), None)

    start_state = (
        jnp.zeros(sorted_rows.shape, jnp.float32),
        jnp.zeros(inner_all.shape, jnp.float32),
        jnp.zeros(outer_all.shape, jnp.float32),
    )
    final_state, _ = lax.scan(visit, start_state, table)
    return final_state


def body(
    tokens,
    token_ids,
    lengths,
    hash_table,
    w_qkv,
    w_attn_out,
    norm_gains,
    norm_biases,
    w_in,
    w_out,
    cotangent,
):
    rows_count = tokens.shape[0]
    seq_count = lengths.shape[0]
    seq_len = rows_count // seq_count
    model_width = D
    expert_total = EXPERTS
    qkv_full, proj_full, gains_full, biases_full = (
        lax.all_gather(w_qkv, ("dp", "fsdp"), axis=0, tiled=True),
        lax.all_gather(w_attn_out, ("dp", "fsdp"), axis=0, tiled=True),
        lax.all_gather(norm_gains, ("dp", "fsdp"), axis=0, tiled=True),
        lax.all_gather(norm_biases, ("dp", "fsdp"), axis=0, tiled=True),
    )
    gains_f = gains_full.astype(jnp.float32)
    biases_f = biases_full.astype(jnp.float32)
    inputs = tokens.astype(jnp.float32)
    normal_one, scaled_one = layer_stats(inputs)
    first_in = (normal_one * gains_f[:, 0] + biases_f[:, 0]).astype(jnp.bfloat16)
    qkv_low = jnp.dot(first_in, qkv_full, preferred_element_type=jnp.float32).astype(jnp.bfloat16)
    packed = qkv_low.reshape(seq_count, seq_len, 3, HEADS, HEAD_DIM)
    queries = packed[:, :, 0]
    keys = packed[:, :, 1]
    values = packed[:, :, 2]
    mixed, totals = lax.map(attention_forward, (queries, keys, values, lengths))
    mixed_flat = mixed.reshape(rows_count, model_width)
    hidden = inputs + jnp.dot(mixed_flat, proj_full, preferred_element_type=jnp.float32)
    normal_two, scaled_two = layer_stats(hidden)
    second_in = (normal_two * gains_f[:, 1] + biases_f[:, 1]).astype(jnp.bfloat16)
    places = jnp.arange(rows_count, dtype=jnp.int32) % seq_len
    used = places < jnp.repeat(lengths, seq_len, total_repeat_length=rows_count)
    expert_ids = jnp.where(used, hash_table[token_ids], expert_total)
    matches = (expert_ids[:, None] == jnp.arange(expert_total, dtype=jnp.int32)[None, :]).astype(
        jnp.int32
    )
    local_counts = jnp.sum(matches, axis=0)
    expert_counts = lax.psum(local_counts, ("dp", "fsdp"))
    ordering = jnp.argsort(expert_ids, stable=True)
    inverse = (
        jnp.zeros((rows_count,), jnp.int32)
        .at[ordering]
        .set(jnp.arange(rows_count, dtype=jnp.int32))
    )
    group_ends = jnp.cumsum(local_counts)
    table = segment_table(group_ends, rows_count, BLOCK)
    inner_all, outer_all = (
        lax.all_gather(w_in, ("dp", "fsdp"), axis=0, tiled=True),
        lax.all_gather(w_out, ("dp", "fsdp"), axis=0, tiled=True),
    )
    sorted_rows = second_in[ordering]
    pre_all, result_sorted = expert_forward(sorted_rows, inner_all, outer_all, table, BLOCK)
    layer_out = (hidden + result_sorted[inverse]).astype(jnp.bfloat16)
    grad_out = cotangent.astype(jnp.float32)
    grad_sorted = cotangent[ordering]
    inner_back, outer_back = (
        lax.all_gather(w_in, ("dp", "fsdp"), axis=0, tiled=True),
        lax.all_gather(w_out, ("dp", "fsdp"), axis=0, tiled=True),
    )
    grad_rows_sorted, grad_inner, grad_outer = expert_backward(
        sorted_rows, pre_all, grad_sorted, inner_back, outer_back, table, BLOCK
    )
    grad_w_in, grad_w_out = (
        lax.psum_scatter(grad_inner, ("dp", "fsdp"), scatter_dimension=0, tiled=True),
        lax.psum_scatter(grad_outer, ("dp", "fsdp"), scatter_dimension=0, tiled=True),
    )
    grad_second = grad_rows_sorted[inverse]
    gain_two = jnp.sum(grad_second * normal_two, axis=0)
    bias_two = jnp.sum(grad_second, axis=0)
    grad_hidden = grad_out + norm_backward(grad_second, normal_two, scaled_two, gains_f[:, 1])
    grad_branch = grad_hidden.astype(jnp.bfloat16)
    qkv_back, proj_back = (
        lax.all_gather(w_qkv, ("dp", "fsdp"), axis=0, tiled=True),
        lax.all_gather(w_attn_out, ("dp", "fsdp"), axis=0, tiled=True),
    )
    grad_proj = jnp.einsum("td,te->de", mixed_flat, grad_branch, preferred_element_type=jnp.float32)
    grad_mixed = jnp.einsum(
        "te,de->td", grad_branch, proj_back, preferred_element_type=jnp.float32
    ).astype(jnp.bfloat16)
    grad_mixed = grad_mixed.reshape(seq_count, seq_len, HEADS, HEAD_DIM)
    grad_queries, grad_keys, grad_values = lax.map(
        attention_backward, (queries, keys, values, totals, grad_mixed, lengths)
    )
    grad_qkv = (
        jnp.stack([grad_queries, grad_keys, grad_values], axis=2)
        .reshape(rows_count, 3 * model_width)
        .astype(jnp.bfloat16)
    )
    grad_qkv_w = jnp.einsum("td,te->de", first_in, grad_qkv, preferred_element_type=jnp.float32)
    grad_first = jnp.einsum("te,de->td", grad_qkv, qkv_back, preferred_element_type=jnp.float32)
    gain_one = jnp.sum(grad_first * normal_one, axis=0)
    bias_one = jnp.sum(grad_first, axis=0)
    grad_tokens = grad_hidden + norm_backward(grad_first, normal_one, scaled_one, gains_f[:, 0])
    grad_gains = jnp.stack([gain_one, gain_two], axis=1)
    grad_biases = jnp.stack([bias_one, bias_two], axis=1)
    grad_w_qkv, grad_w_attn_out, grad_norm_gains, grad_norm_biases = (
        lax.psum_scatter(grad_qkv_w, ("dp", "fsdp"), scatter_dimension=0, tiled=True),
        lax.psum_scatter(grad_proj, ("dp", "fsdp"), scatter_dimension=0, tiled=True),
        lax.psum_scatter(grad_gains, ("dp", "fsdp"), scatter_dimension=0, tiled=True),
        lax.psum_scatter(grad_biases, ("dp", "fsdp"), scatter_dimension=0, tiled=True),
    )
    return (
        layer_out,
        grad_tokens,
        grad_w_qkv,
        grad_w_attn_out,
        grad_norm_gains,
        grad_norm_biases,
        grad_w_in,
        grad_w_out,
        expert_counts,
    )


LOG2E = 1.4426950408889634
ROWS = 256
GROUP = 16
MIB = 1024 * 1024
NT = (((1,), (1,)), ((), ()))
NN = (((1,), (0,)), ((), ()))
ROOT = 0.7978845608028654
CUBIC = 0.044715


def mul(a, b, dims=NN):
    return lax.dot_general(a, b, dims, preferred_element_type=jnp.float32)


def iota(shape, dim):
    return lax.broadcasted_iota(jnp.int32, shape, dim)


def padded_rows(slots):
    return slots + EXPERTS * GROUP


def three_parts(v):
    first = v.astype(jnp.bfloat16)
    rest = v - first.astype(jnp.float32)
    second = rest.astype(jnp.bfloat16)
    third = (rest - second.astype(jnp.float32)).astype(jnp.bfloat16)
    return first, second, third


def own_lanes(lane, half):
    return (lane < HEAD_DIM) if half == 0 else (lane >= HEAD_DIM)


def extra_lane(half):
    return HEAD_DIM if half == 0 else 0


def routing(ids, table, length, perm_ref):
    slots = ids.shape[1]
    chosen = (iota((table.shape[1], slots), 0) == (ids >> 7)).astype(jnp.bfloat16)
    rows = mul(table, chosen)
    expert = jnp.sum(
        jnp.where(iota(rows.shape, 0) == (ids & 127), rows, 0.0), axis=0, keepdims=True
    ).astype(jnp.int32)
    used = iota((1, slots), 1) < length
    member = (iota((8, slots), 0) == expert) & used
    member_f = jnp.where(member, 1.0, 0.0)
    perm_ref[0:slots, :] = (iota((slots, slots), 0) <= iota((slots, slots), 1)).astype(jnp.bfloat16)
    rank = mul(member_f.astype(jnp.bfloat16), perm_ref[0:slots, :])
    counts = rank[:, slots - 1 : slots]
    groups = jnp.floor((counts + (GROUP - 1)) * (1.0 / GROUP))
    row8 = iota((8, 1), 0)
    start = jnp.zeros((8, 1), jnp.float32)
    for e in range(EXPERTS - 1):
        start = start + jnp.where(row8 > e, groups[e : e + 1, :], 0.0)
    place = jnp.sum(member_f * (rank - 1.0 + start * GROUP), axis=0, keepdims=True)
    place = jnp.where(used, place, -1.0)
    return place, counts, groups


MESH = pl.DeviceIdType.MESH
HALF = 1664
WIDE = 2 * HALF


class Place:
    def __init__(self):
        self.z = lax.axis_index("dp")
        f = lax.axis_index("fsdp")
        self.y = f // 4
        self.x = (f // 2) % 2
        self.c = f % 2

    def at(self, z=None, y=None, x=None, c=None):
        z = self.z if z is None else z
        y = self.y if y is None else y
        x = self.x if x is None else x
        c = self.c if c is None else c
        return (z, 4 * y + 2 * x + c)

    def greet(self, peers):
        barrier = pltpu.get_barrier_semaphore()
        for peer in peers:
            pl.semaphore_signal(barrier, inc=1, device_id=peer, device_id_type=MESH)
        pl.semaphore_wait(barrier, len(peers))


def push(src, dst, send, recv, peer):
    return pltpu.make_async_remote_copy(
        src_ref=src, dst_ref=dst, send_sem=send, recv_sem=recv, device_id=peer, device_id_type=MESH
    )


def front_kernel(
    len_ref, x_ref, ids_ref, table_ref, g_ref, local_ref, win_ref, wout_ref,
    qkv_ref, mixed_ref, aug_ref, hidden_ref, xs_ref, gs_ref, w_ref, wa_ref, norms_ref, pos_ref, counts_ref,
    perm_ref, normed_ref, qa_ref, ka_ref, va_ref, tokx_ref, tokg_ref, sib_ref,
    sem0, sz, rz, sy, ry, sx, rx, sd, rd, ss, rs,
    tok_local, tok_send, tok_recv,
    lane_local, lane_send, lane_recv, up_send, down_send, line_recv, y_send, y_recv,
):
    slots, width = x_ref.shape
    heads = width // HEAD_DIM
    rp = padded_rows(slots)
    length = len_ref[0]
    me = Place()
    z, y, x, c = me.z, me.y, me.x, me.c
    depth = 4
    sibling, beside, across = me.at(c=1 - c), me.at(x=1 - x), me.at(y=1 - y)
    me.greet([sibling, beside, across, me.at(x=1 - x, c=1 - c)] + [me.at(z=z ^ k) for k in range(1, depth)])

    first = push(local_ref, sib_ref, sem0.at[0], sem0.at[1], sibling)
    first.start()

    def block(zz, yy, xx):
        rows = pl.ds(pl.multiple_of(48 * (4 * zz + 2 * yy + xx), 48), 48)
        return wa_ref.at[rows, pl.ds(pl.multiple_of(c * HALF, 128), HALF)]

    def share(zz, yy, xx, send, recv, peer):
        ref = block(zz, yy, xx)
        return push(ref, ref, send, recv, peer)

    def z_up(source):
        return share(source, y, x, sz.at[0, source], rz.at[source], me.at(z=jnp.minimum(z + 1, depth - 1)))

    def z_down(source):
        return share(source, y, x, sz.at[1, source], rz.at[source], me.at(z=jnp.maximum(z - 1, 0)))

    def y_copy(zz, source_y):
        return share(zz, source_y, x, sy.at[zz], ry.at[zz], across)

    def x_copy(zz, source_x):
        return share(zz, y, source_x, sx.at[zz], rx.at[zz], beside)

    def d_copy_x(zz, yy, xx):
        return share(zz, yy, xx, sd.at[zz], rd.at[zz], beside)

    def d_copy_y(zz, yy, xx):
        return share(zz, yy, xx, sd.at[zz], rd.at[zz], across)

    def s_copy(zz, side):
        ref = wa_ref.at[pl.ds(pl.multiple_of(192 * zz, 192), 192), pl.ds(pl.multiple_of(side * HALF, 128), HALF)]
        return push(ref, ref, ss.at[zz], rs.at[zz], sibling)

    part = wout_ref.shape[0]
    rows_in = win_ref.shape[0]
    lanes = [(1 - x, c), (x, 1 - c), (1 - x, 1 - c)]

    def lane_cols(b, xx, cc):
        return win_ref.at[:, pl.ds(pl.multiple_of(part * (4 * b + 2 * xx + cc), 128), part)]

    def lane_home(b, xx, cc):
        return w_ref.at[0, z, y, pl.ds(pl.multiple_of(rows_in * (2 * xx + cc), rows_in), rows_in), pl.ds(b * part, part)]

    def lane_copy(i, b, arrive):
        xx, cc = lanes[i]
        home = lane_home(b, xx, cc) if arrive else lane_home(b, x, c)
        return push(lane_cols(b, xx, cc), home, lane_send.at[i, b], lane_recv.at[i, b], me.at(x=xx, c=cc))

    def lane_own(b):
        return pltpu.make_async_copy(lane_cols(b, x, c), lane_home(b, x, c), lane_local.at[b])

    own_out = pltpu.make_async_copy(wout_ref, w_ref.at[1, z, y], lane_local.at[2])

    def shard(k, zz, yy):
        return w_ref.at[k, zz, yy]

    def up_copy(k, zz):
        return push(shard(k, zz, y), shard(k, zz, y), up_send.at[k, zz], line_recv.at[k, zz], me.at(z=jnp.minimum(z + 1, depth - 1)))

    def down_copy(k, zz):
        return push(shard(k, zz, y), shard(k, zz, y), down_send.at[k, zz], line_recv.at[k, zz], me.at(z=jnp.maximum(z - 1, 0)))

    def over_copy(k, zz, yy):
        return push(shard(k, zz, yy), shard(k, zz, yy), y_send.at[k, zz], y_recv.at[k, zz], across)

    def spread(k):
        @pl.when(z < depth - 1)
        def _():
            up_copy(k, z).start()

        @pl.when(z > 0)
        def _():
            down_copy(k, z).start()

    def relay(k, s):
        @pl.when(z >= s)
        def _():
            up_copy(k, z - s).wait_recv()

            @pl.when(z < depth - 1)
            def _():
                up_copy(k, z - s).start()

            over_copy(k, z - s, y).start()

        @pl.when(z + s < depth)
        def _():
            down_copy(k, z + s).wait_recv()

            @pl.when(z > 0)
            def _():
                down_copy(k, z + s).start()

            over_copy(k, z + s, y).start()

    def weights_start():
        for i in range(3):
            for b in range(2):
                lane_copy(i, b, False).start()

    def weights_lane():
        for i in range(3):
            for b in range(2):
                lane_copy(i, b, True).wait_recv()
        for b in range(2):
            lane_own(b).wait()
        spread(0)

    def relay_of(k, s):
        return functools.partial(relay, k, s)

    def weights_end():
        for k in (1, 0):
            for zz in range(depth):
                @pl.when(zz != z)
                def _():
                    over_copy(k, zz, 1 - y).wait()

                for copy, stop in ((up_copy, depth - 1), (down_copy, 0)):
                    inside = (zz <= z) if stop else (zz >= z)

                    @pl.when(inside & (z != stop))
                    def _():
                        copy(k, zz).wait_send()

        for i in range(3):
            for b in range(2):
                lane_copy(i, b, False).wait_send()

    mine = 2 * x + c

    def tok_copies(k, scratch, far_ref):
        own = pltpu.make_async_copy(scratch, far_ref.at[mine], tok_local.at[k])
        near = push(scratch, far_ref.at[mine], tok_send.at[k, 0], tok_recv.at[k, 0], sibling)
        far = push(scratch, far_ref.at[mine], tok_send.at[k, 1], tok_recv.at[k, 1], beside)
        slot = far_ref.at[2 * (1 - x) + c]
        onward = push(slot, slot, tok_send.at[k, 2], tok_recv.at[k, 2], sibling)
        return own, near, far, onward

    x_copies = tok_copies(0, tokx_ref, xs_ref)
    g_copies = tok_copies(1, tokg_ref, gs_ref)

    first.wait_recv()
    zero_core = c == 0
    own_cols = pl.ds(pl.multiple_of(c * HALF, 128), HALF)
    local = local_ref[0:24, own_cols]
    other = sib_ref[0:24, own_cols]
    own_rows = pl.ds(pl.multiple_of(48 * (4 * z + 2 * y + x), 48), 48)
    wa_ref[own_rows, own_cols] = jnp.concatenate(
        [jnp.where(zero_core, local, other), jnp.where(zero_core, other, local)], axis=0
    )
    def planes(s, act):
        @pl.when(z >= s)
        def _():
            act(z - s, True)

        if s:
            @pl.when(z + s < depth)
            def _():
                act(z + s, False)

    def z_arrived(zz, upward):
        z_up(zz).wait_recv()
        if upward:
            pl.when(z < depth - 1)(z_up(zz).start)
        else:
            pl.when(z > 0)(z_down(zz).start)
        y_copy(zz, y).start()
        x_copy(zz, x).start()

    def near_arrived(zz, _):
        y_copy(zz, 1 - y).wait_recv()
        x_copy(zz, 1 - x).wait_recv()
        pl.when(zz % 2 == 0)(d_copy_x(zz, 1 - y, x).start)
        pl.when(zz % 2 == 1)(d_copy_y(zz, y, 1 - x).start)

    def corner_arrived(zz, _):
        d_copy_x(zz, 1 - y, 1 - x).wait_recv()
        s_copy(zz, c).start()

    pl.when(z < depth - 1)(z_up(z).start)
    pl.when(z > 0)(z_down(z).start)
    y_copy(z, y).start()
    x_copy(z, x).start()
    for b in range(2):
        lane_own(b).start()
    own_out.start()

    place, counts, groups = routing(ids_ref[...], table_ref[...], length, perm_ref)
    place_i = place.astype(jnp.int32)
    pos_ref[...] = jnp.broadcast_to(place, (128, slots)).T
    counts_ref[...] = jnp.broadcast_to(counts, (8, 128)).astype(jnp.int32)

    planes(1, z_arrived)
    planes(0, near_arrived)
    planes(2, z_arrived)
    planes(1, near_arrived)
    planes(3, z_arrived)
    own_out.wait()
    spread(1)
    planes(0, corner_arrived)
    step = rp // 4

    @pl.loop(0, 4)
    def _(i):
        base = i * step
        perm_ref[pl.ds(base, step), :] = (
            iota((step, slots), 0) + base == place_i
        ).astype(jnp.bfloat16)

    planes(2, near_arrived)
    planes(1, corner_arrived)
    planes(3, near_arrived)
    weights_start()

    @pl.loop(0, 4)
    def _(i):
        rows = pl.ds(i * step, step)
        tokg_ref[rows, :] = mul(perm_ref[rows, :], g_ref[...]).astype(jnp.bfloat16)

    tail = jnp.broadcast_to(jnp.concatenate([groups, groups], axis=0), (GROUP, width)).astype(jnp.bfloat16)
    tokx_ref[rp : rp + GROUP, :] = tail
    tokg_ref[rp : rp + GROUP, :] = tail

    planes(2, corner_arrived)
    planes(3, corner_arrived)
    for k in range(depth):
        s_copy(z ^ k, 1 - c).wait_recv()
    for copy in g_copies[:3]:
        copy.start()

    relay(1, 1)
    cols_t = wa_ref[:, 2 * width : 2 * width + 128].astype(jnp.float32).T
    norms_ref[...] = cols_t[0:8, :]

    @pl.loop(0, slots // ROWS)
    def _(i):
        rows = pl.ds(i * ROWS, ROWS)
        normal, _ = layer_stats(x_ref[rows, :].astype(jnp.float32))
        normed = (normal * norms_ref[0:1, :] + norms_ref[2:3, :]).astype(jnp.bfloat16)
        for part_i, start in enumerate((0, width, HALF)):
            cols = slice(part_i * width, (part_i + 1) * width)
            qkv_ref[rows, cols] = mul(normed, wa_ref[:, start : start + width]).astype(jnp.bfloat16)

    lane = iota((slots, 128), 1)
    key_bias = jnp.where(iota((slots, 128), 0) < length, 0.0, NEGATIVE).astype(jnp.bfloat16)
    causal = iota((ROWS, ROWS), 1) <= iota((ROWS, ROWS), 0)
    lane_b = iota((ROWS, 128), 1)
    pairs = heads // 2
    slots_for = [[], [weights_lane], [], [relay_of(1, 2)], [], [relay_of(0, 1)]]

    @pl.loop(0, pairs)
    def _(p):
        cols = pl.ds(p * 128, 128)
        q = qkv_ref[:, cols].astype(jnp.float32) * (HEAD_DIM ** -0.5 * LOG2E)
        q_hi = q.astype(jnp.bfloat16)
        q_lo = (q - q_hi.astype(jnp.float32)).astype(jnp.bfloat16)
        k = qkv_ref[:, pl.ds(width + p * 128, 128)]
        v = qkv_ref[:, pl.ds(2 * width + p * 128, 128)]
        zero = jnp.zeros_like(q_hi)
        one = jnp.ones_like(q_hi)
        for half in range(2):
            own = own_lanes(lane, half)
            extra = extra_lane(half)
            qa_ref[half, :, 0:128] = jnp.where(own, q_hi, zero)
            qa_ref[half, :, 128:256] = jnp.where(own, q_lo, jnp.where(lane == extra, one, zero))
            ka_ref[half, :, 0:128] = k
            ka_ref[half, :, 128:256] = jnp.where(own, k, jnp.where(lane == extra, key_bias, zero))
            va_ref[half, :, :] = jnp.where(own, v, one)
        for i in range(slots // ROWS):
            rows = slice(i * ROWS, (i + 1) * ROWS)
            keys = (i + 1) * ROWS
            outs = []
            for half in range(2):
                s = mul(qa_ref[half, rows, :], ka_ref[half, 0:keys, :], NT)
                diag = jnp.where(causal, s[:, i * ROWS :], NEGATIVE)
                s = diag if i == 0 else jnp.concatenate([s[:, : i * ROWS], diag], axis=1)
                top = jnp.max(s, axis=1, keepdims=True)
                probs = jnp.exp2(s - top).astype(jnp.bfloat16)
                out = mul(probs, va_ref[half, 0:keys, :])
                total = pltpu.roll(out, HEAD_DIM, 1)
                outs.append(out / total)
                minus = -(top + jnp.log2(out))
                a, b, d = three_parts(minus)
                extra = extra_lane(half)
                seen = qa_ref[half, rows, 128:256]
                seen = jnp.where(lane_b == extra + 1, a, seen)
                seen = jnp.where(lane_b == extra + 2, b, seen)
                seen = jnp.where(lane_b == extra + 3, d, seen)
                aug_ref[2 * p + half, rows, :] = seen
            mixed_ref[rows, cols] = jnp.where(lane_b < HEAD_DIM, outs[0], outs[1]).astype(jnp.bfloat16)
        for i in range(pairs):
            @pl.when(p == i)
            def _():
                for tick in slots_for[i]:
                    tick()

    @pl.loop(0, slots // ROWS)
    def _(i):
        rows = pl.ds(i * ROWS, ROWS)
        hidden = x_ref[rows, :].astype(jnp.float32) + mul(mixed_ref[rows, :], wa_ref[:, HALF + width : HALF + 2 * width])
        hidden_ref[rows, :] = hidden
        normal, _ = layer_stats(hidden)
        normed_ref[rows, :] = (normal * norms_ref[1:2, :] + norms_ref[3:4, :]).astype(jnp.bfloat16)

    @pl.loop(0, 4)
    def _(i):
        rows = pl.ds(i * step, step)
        tokx_ref[rows, :] = mul(perm_ref[rows, :], normed_ref[...]).astype(jnp.bfloat16)

    for copy in x_copies[:3]:
        copy.start()
    relay(1, 3)
    relay(0, 2)
    g_copies[2].wait_recv()
    g_copies[3].start()
    relay(0, 3)
    x_copies[2].wait_recv()
    x_copies[3].start()
    weights_end()
    for own, near, far, onward in (x_copies, g_copies):
        own.wait()
        near.wait()
        far.wait_send()
        onward.wait()
    first.wait_send()
    for zz in range(depth):
        pl.when((zz <= z) & (z < depth - 1))(z_up(zz).wait_send)
        pl.when((zz >= z) & (z > 0))(z_down(zz).wait_send)
        y_copy(zz, y).wait_send()
        x_copy(zz, x).wait_send()
        d_copy_x(zz, y, x).wait_send()
        s_copy(zz, c).wait_send()


def front(length, x, ids, table, g, local, w_in, w_out):
    slots, width = x.shape
    rp = padded_rows(slots)
    part = w_out.shape[0]
    bf = jnp.bfloat16
    f32 = jnp.float32
    whole = pl.BlockSpec(memory_space=pltpu.VMEM)
    far = pl.BlockSpec(memory_space=pl.ANY)
    dma = pltpu.SemaphoreType.DMA
    return pl.pallas_call(
        front_kernel,
        out_shape=(
            jax.ShapeDtypeStruct((slots, 3 * width), bf),
            jax.ShapeDtypeStruct((slots, width), bf),
            jax.ShapeDtypeStruct((HEADS, slots, 128), bf),
            jax.ShapeDtypeStruct((slots, width), f32),
            jax.ShapeDtypeStruct((4, rp + GROUP, width), bf),
            jax.ShapeDtypeStruct((4, rp + GROUP, width), bf),
            jax.ShapeDtypeStruct((2, EXPERTS, 2, part, width), bf),
            jax.ShapeDtypeStruct((width, WIDE), bf),
            jax.ShapeDtypeStruct((8, width), f32),
            jax.ShapeDtypeStruct((slots, 128), f32),
            jax.ShapeDtypeStruct((8, 128), jnp.int32),
        ),
        in_specs=[pl.BlockSpec(memory_space=pltpu.SMEM)] + [whole] * 5 + [far] * 2,
        out_specs=(whole, whole, whole, whole, far, far, far, whole, whole, whole, whole),
        scratch_shapes=[
            pltpu.VMEM((rp, slots), bf),
            pltpu.VMEM((slots, width), bf),
            pltpu.VMEM((2, slots, 256), bf),
            pltpu.VMEM((2, slots, 256), bf),
            pltpu.VMEM((2, slots, 128), bf),
            pltpu.VMEM((rp + GROUP, width), bf),
            pltpu.VMEM((rp + GROUP, width), bf),
            pltpu.VMEM((32, WIDE), bf),
            dma((2,)), dma((2, 4)), dma((4,)), dma((4,)), dma((4,)), dma((4,)), dma((4,)), dma((4,)), dma((4,)),
            dma((4,)), dma((4,)),
            dma((2,)), dma((2, 3)), dma((2, 3)),
            dma((3,)), dma((3, 2)), dma((3, 2)), dma((2, 4)), dma((2, 4)), dma((2, 4)), dma((2, 4)), dma((2, 4)),
        ],
        compiler_params=pltpu.CompilerParams(vmem_limit_bytes=56 * MIB, collective_id=0, has_side_effects=True),
        name="front",
    )(length, x, ids, table, g, local, w_in, w_out)


CHUNK = 32
TURN = 2


def experts_kernel(
    fresh, n_ref, who_ref, x_ref, g_ref, w_far, *refs,
):
    if fresh:
        late_far = None
    else:
        late_far, refs = refs[0], refs[3:]
    (
        o_ref, dx_ref, gw1_far, gw2_far,
        w_ref, xb, gb, ob, db, acc1, acc2, stage, blank, sem_in, sem_out, sem_zero, sem_w, sem_gw,
    ) = refs
    sources, groups, _, width = x_ref.shape
    groups = groups - 1
    rows = CHUNK * GROUP
    y = who_ref[TURN]

    copies = []
    for i in range(TURN):
        for k in range(2):
            if not fresh and i == TURN - 1:
                pairs = [(w_far.at[k, who_ref[i], y], y), (late_far.at[k], 1 - y)]
            else:
                pairs = [(w_far.at[k, who_ref[i], h], h) for h in range(2)]
            for n, (src, h) in enumerate(pairs):
                copies.append(pltpu.make_async_copy(src, w_ref.at[i, k, h], sem_w.at[i, 2 * k + n]))
    for copy in copies:
        copy.start()

    totals = []
    for i in range(TURN):
        totals.append(lax.fori_loop(0, sources, lambda s, t, i=i: t + n_ref[s * EXPERTS + who_ref[i]], 0))
    first = [0]
    for i in range(TURN):
        first.append(first[-1] + (totals[i] + (CHUNK - 1)) // CHUNK)
    chunks = first[TURN]

    def locate(c):
        i = jnp.where(c >= first[1], 1, 0)
        begin = (c - jnp.where(i == 1, first[1], 0)) * CHUNK
        return i, begin, jnp.minimum(begin + CHUNK, jnp.where(i == 1, totals[1], totals[0]))

    def pieces(c, act):
        i, begin, end = locate(c)
        e = who_ref[i]

        def visit(s, base):
            n = n_ref[s * EXPERTS + e]
            low = jnp.maximum(base, begin)
            size = jnp.minimum(base + n, end) - low
            skip = jnp.int32(0)
            for j in range(EXPERTS - 1):
                skip = skip + jnp.where(e > j, n_ref[s * EXPERTS + j], 0)

            @pl.when(size > 0)
            def _():
                act(s, skip + low - base, low - begin, size)

            return base + n

        lax.fori_loop(0, sources, visit, jnp.int32(0))

    def load(c, slot):
        def act(s, at, to, size):
            for k, (src, dst) in enumerate(((x_ref, xb), (g_ref, gb))):
                pltpu.make_async_copy(
                    src.at[s, pl.ds(at, size)], dst.at[slot, pl.ds(to, size)], sem_in.at[k, slot]
                ).start()

        pieces(c, act)

    def store(c, slot):
        def act(s, at, to, size):
            for k, (src, dst) in enumerate(((ob, o_ref), (db, dx_ref))):
                pltpu.make_async_copy(
                    src.at[slot, pl.ds(to, size)], dst.at[s, pl.ds(at, size)], sem_out.at[k, slot]
                ).start()

        pieces(c, act)

    def settle(c, slot, bufs, sems):
        _, begin, end = locate(c)
        for k, buf in enumerate(bufs):
            part = buf.at[slot, pl.ds(0, end - begin)]
            pltpu.make_async_copy(part, part, sems.at[k, slot]).wait()

    @pl.when(chunks > 0)
    def _():
        load(0, 0)

    def rest(s, act):
        t = n_ref[s * EXPERTS]
        for e in range(1, EXPERTS):
            t = t + n_ref[s * EXPERTS + e]

        @pl.when(groups - t > 0)
        def _():
            for k, dst in enumerate((o_ref, dx_ref)):
                act(
                    pltpu.make_async_copy(
                        blank.at[pl.ds(0, groups - t)], dst.at[s, pl.ds(t, groups - t)], sem_zero.at[k, s]
                    )
                )

    if fresh:
        blank[...] = jnp.zeros_like(blank)

        @pl.loop(0, sources)
        def _(s):
            rest(s, lambda copy: copy.start())

    def results(i):
        return [
            pltpu.make_async_copy(stage.at[k], far.at[i], sem_gw.at[k])
            for k, far in enumerate((gw1_far, gw2_far))
        ]

    @pl.loop(0, chunks)
    def _(c):
        slot = c % 2
        i, begin, end = locate(c)

        @pl.when(c + 1 < chunks)
        def _():
            load(c + 1, 1 - slot)

        settle(c, slot, (xb, gb), sem_in)

        @pl.when(c >= 2)
        def _():
            settle(c - 2, slot, (ob, db), sem_out)

        for n in range(TURN):
            @pl.when((begin == 0) & (i == n))
            def _():
                for copy in copies[4 * n : 4 * n + 4]:
                    copy.wait()

        @pl.when(end - begin < CHUNK)
        def _():
            @pl.loop(end - begin, CHUNK)
            def _(r):
                xb[slot, r] = jnp.zeros_like(xb[slot, r])
                gb[slot, r] = jnp.zeros_like(gb[slot, r])

        x = xb[slot].reshape(rows, width)
        g = gb[slot].reshape(rows, width)
        w1 = w_ref[i, 0].reshape(width, width)
        w2 = w_ref[i, 1].reshape(width, width)
        pre = mul(x, w1)
        square = pre * pre
        t = jnp.tanh(ROOT * pre * (1.0 + CUBIC * square))
        act = (0.5 * pre * (1.0 + t)).astype(jnp.bfloat16)
        slope = 0.5 * (1.0 + t) + 0.5 * pre * (1.0 - t * t) * (ROOT * (1.0 + 3.0 * CUBIC * square))
        grad_pre = (slope * mul(g, w2, NT)).astype(jnp.bfloat16)
        ob[slot] = mul(act, w2).astype(jnp.bfloat16).reshape(CHUNK, GROUP, width)
        db[slot] = mul(grad_pre, w1, NT).astype(jnp.bfloat16).reshape(CHUNK, GROUP, width)
        store(c, slot)
        add1 = mul(x.T, grad_pre)
        add2 = mul(act.T, g)

        @pl.when(begin == 0)
        def _():
            acc1[...] = add1
            acc2[...] = add2

        @pl.when(begin > 0)
        def _():
            acc1[...] += add1
            acc2[...] += add2

        for n in range(TURN):
            @pl.when((i == n) & (end == totals[n]))
            def _():
                if n:
                    @pl.when(totals[0] > 0)
                    def _():
                        for copy in results(0):
                            copy.wait()

                stage[0] = acc1[...].astype(stage.dtype)
                stage[1] = acc2[...].astype(stage.dtype)
                for copy in results(n):
                    copy.start()

    for n in range(TURN):
        wait_now = (totals[n] > 0) if n == TURN - 1 else (totals[n] > 0) & (totals[n + 1] == 0)

        @pl.when(wait_now)
        def _():
            for copy in results(n):
                copy.wait()

    for n in range(TURN):
        @pl.when(totals[n] == 0)
        def _():
            for copy in copies[4 * n : 4 * n + 4]:
                copy.wait()
            stage[...] = jnp.zeros_like(stage)
            for copy in results(n):
                copy.start()
            for copy in results(n):
                copy.wait()

    @pl.when(chunks >= 2)
    def _():
        settle(chunks - 2, chunks % 2, (ob, db), sem_out)

    @pl.when(chunks >= 1)
    def _():
        settle(chunks - 1, (chunks - 1) % 2, (ob, db), sem_out)

    if fresh:
        @pl.loop(0, sources)
        def _(s):
            rest(s, lambda copy: copy.wait())


def experts(n16, who, xs, gs, w, late=None, rows_out=None):
    sources, groups, _, width = xs.shape
    bf = jnp.bfloat16
    f32 = jnp.float32
    fresh = late is None
    far = pl.BlockSpec(memory_space=pl.ANY)
    smem = pl.BlockSpec(memory_space=pltpu.SMEM)
    out_rows = jax.ShapeDtypeStruct((sources, groups - 1, GROUP, width), bf)
    more = () if fresh else (late,) + rows_out
    dma = pltpu.SemaphoreType.DMA
    slots = CHUNK * GROUP * width
    typical = sources * (groups - 1) * GROUP * 5 // 16
    return pl.pallas_call(
        functools.partial(experts_kernel, fresh),
        out_shape=(
            out_rows, out_rows,
            jax.ShapeDtypeStruct((TURN, width, width), bf),
            jax.ShapeDtypeStruct((TURN, width, width), bf),
        ),
        in_specs=[smem, smem] + [far] * (3 + len(more)),
        out_specs=(far, far, far, far),
        scratch_shapes=[pltpu.VMEM((TURN, 2, 2, width // 2, width), bf)]
        + [pltpu.VMEM((2, CHUNK, GROUP, width), bf)] * 4
        + [pltpu.VMEM((width, width), f32)] * 2
        + [pltpu.VMEM((2, width, width), bf), pltpu.VMEM((groups - 1, GROUP, width), bf)]
        + [dma((2, 2)), dma((2, 2)), dma((2, sources)), dma((TURN, 4)), dma((2,))],
        input_output_aliases={} if fresh else {6: 0, 7: 1},
        cost_estimate=pl.CostEstimate(
            flops=12 * typical * width * width, bytes_accessed=8 * typical * width, transcendentals=typical * width
        ),
        compiler_params=pltpu.CompilerParams(vmem_limit_bytes=56 * MIB),
        name="experts",
    )(n16, who, xs, gs, w, *more)


GROUPS = 4
UNIT = 384


def back_kernel(
    len_ref, norms_ref, counts_ref, x_far, g_far, hidden_far, qkv_far, mixed_far, aug_far, pos_far, wa_far,
    o_far, dx_far, gw1a_far, gw2a_far, gw1b_far, gw2b_far, y_first,
    out_far, gx_far, gwq_ref, gwo_ref, gn_out, cnt_out, gwin_ref, gwout_ref,
    y_land, up_land, down_land, o_near, o_beside,
    x_ref, g_ref, gx_ref, qkv_ref, mixed_ref, aug_ref, pos_ref, wa_ref,
    branch_ref, gmix_ref, first_t, mixed_t,
    qa_ref, ka_ref, va_ref, oa_ref, dv_ref, dk_ref, dq_ref,
    dx_own, dx_near, dx_beside, os_ref, in_ref, sum_ref, lane_out, lane_in, hid_ref, outb_ref,
    half_land, d_land, y_small, x_small, z_small, last_out, last_in,
    gn_ref, gn_send, gn_land, gn_t,
    load_sem, aug_sem, dxs_send, dxs_recv, dxx_send, dxx_recv,
    yw_send, yw_recv, up_send, up_recv, dn_send, dn_recv, on_send, on_recv, ob_send, ob_recv, in_sem,
    ln_send, ln_recv, h_send, h_recv, d_send, d_recv, sy_send, sy_recv, sx_send, sx_recv, sz_send, sz_recv,
    l_send, l_recv, gs_send, gs_recv, hid_sem, out_sem, gx_sem,
):
    slots, width = x_ref.shape
    heads = width // HEAD_DIM
    pairs = heads // 2
    rp = dx_own.shape[1]
    piece = rp // 4
    part = gw1a_far.shape[2]
    owned = gwq_ref.shape[0]
    depth = 4
    length = len_ref[0]
    scale = HEAD_DIM ** -0.5
    f32 = jnp.float32
    bf = jnp.bfloat16
    me = Place()
    z, y, x, c = me.z, me.y, me.x, me.c
    sibling, beside, across = me.at(c=1 - c), me.at(x=1 - x), me.at(y=1 - y)
    above, below = me.at(z=jnp.minimum(z + 1, depth - 1)), me.at(z=jnp.maximum(z - 1, 0))
    me.greet([sibling, beside, across, me.at(x=1 - x, c=1 - c)] + [me.at(z=z ^ k) for k in range(1, depth)])

    loads = {
        "dx": [pltpu.make_async_copy(dx_far.at[2 * xx + c], dx_own.at[xx], load_sem.at[xx]) for xx in range(2)],
    }
    plain = (
        ("x", x_far, x_ref), ("mixed", mixed_far, mixed_ref), ("hidden", hidden_far, gx_ref), ("g", g_far, g_ref),
        ("pos", pos_far, pos_ref), ("wa", wa_far, wa_ref), ("qkv", qkv_far, qkv_ref),
    )
    for i, (name, src, dst) in enumerate(plain):
        loads[name] = [pltpu.make_async_copy(src, dst, load_sem.at[2 + i])]

    def loaded(*names):
        for name in names:
            for copy in loads[name]:
                copy.wait()

    def dx_sib(xx):
        return push(dx_far.at[2 * xx + 1 - c], dx_near.at[xx], dxs_send.at[xx], dxs_recv.at[xx], sibling)

    def rows_of(i):
        return pl.ds(i * piece, piece)

    def dx_over(i):
        return push(dx_own.at[1 - x, rows_of(i)], dx_beside.at[rows_of(i)], dxx_send.at[i], dxx_recv.at[i], beside)

    gws = ((gw1a_far, gw1b_far), (gw2a_far, gw2b_far))

    def product(k, i):
        return gws[k][i // 2].at[i % 2]

    def y_push(k, i):
        return push(product(k, i).at[1 - y], y_land.at[k, i], yw_send.at[k, i], yw_recv.at[k, i], across)

    def up_push(k, e, slot):
        return push(sum_ref.at[slot], up_land.at[k, e], up_send.at[k, e], up_recv.at[k, e], above)

    def down_push(k, e, slot):
        return push(sum_ref.at[slot], down_land.at[k, e], dn_send.at[k, e], dn_recv.at[k, e], below)

    def o_sib(xx):
        return push(o_far.at[2 * xx + 1 - c], o_near.at[xx], on_send.at[xx], on_recv.at[xx], sibling)

    def o_over(i, slot):
        return push(sum_ref.at[slot, pl.ds(0, piece)], o_beside.at[rows_of(i)], ob_send.at[i], ob_recv.at[i], beside)

    lanes = [(1 - x, c), (x, 1 - c), (1 - x, 1 - c)]
    lane_rows = part // 4
    mine = 2 * x + c

    def lane_push(i, arrive):
        xx, cc = lanes[i]
        src = lane_out.at[pl.ds(pl.multiple_of(lane_rows * (2 * xx + cc), 16), lane_rows)]
        dst = lane_in.at[2 * xx + cc] if arrive else lane_in.at[mine]
        return push(src, dst, ln_send.at[i], ln_recv.at[i], me.at(x=xx, c=cc))

    weights = [(k, i) for i in range(depth) for k in (0, 1)]

    class WeightItem:
        def __init__(self, k, i):
            self.k, self.i, self.m = k, i, 3 - i
            self.rows = part

        def e(self):
            return (3 * (1 - z // 2), (3 * z + 2) % 5, 1 + z % 2, z)[self.i]

        def flags(self):
            e = self.e()
            if self.m == 0:
                return z > 0, z < depth - 1
            return (e > z) & (z > 0), (e < z) & (z < depth - 1)

        def ready(self):
            k, e = self.k, self.e()
            if self.i:
                y_push(k, self.i).wait_recv()
            for flag, copy in zip(self.flags(), (up_push, down_push)):
                @pl.when(flag)
                def _():
                    copy(k, e, 0).wait_recv()

        def sources(self):
            k, e = self.k, self.e()
            a, b = self.flags()
            return [
                (product(k, self.i).at[y], None), ((y_land.at[k, self.i] if self.i else y_first.at[k]), None),
                (up_land.at[k, e], a), (down_land.at[k, e], b)
            ]

        def finish(self, total, slot):
            k, e = self.k, self.e()
            if self.m:
                def put(rows, value):
                    sum_ref[slot, rows, :] = value.astype(bf)

                total(put)

                @pl.when(e > z)
                def _():
                    up_push(k, e, slot).start()

                @pl.when(e < z)
                def _():
                    down_push(k, e, slot).start()
            elif k == 1:
                def put(rows, value):
                    gwout_ref[rows, :] = value

                total(put)
            else:
                def put(rows, value):
                    lane_out[rows, :] = value.astype(bf)

                total(put)
                for i in range(3):
                    lane_push(i, False).start()
                lane_in[mine] = lane_out[pl.ds(pl.multiple_of(lane_rows * mine, 16), lane_rows), :]

        def sent(self, slot):
            k, e = self.k, self.e()
            if self.m:
                @pl.when(e > z)
                def _():
                    up_push(k, e, slot).wait_send()

                @pl.when(e < z)
                def _():
                    down_push(k, e, slot).wait_send()

    class OutItem:
        def __init__(self, stage, i):
            self.stage, self.i = stage, i
            self.rows = piece

        def ready(self):
            if self.i == 0:
                o_sib(1 - x if self.stage == 0 else x).wait_recv()
            if self.stage:
                o_over(self.i, 0).wait_recv()

        def sources(self):
            xx = 1 - x if self.stage == 0 else x
            rows = rows_of(self.i)
            found = [(o_far.at[2 * xx + c, rows], None), (o_near.at[xx, rows], None)]
            if self.stage:
                found.append((o_beside.at[rows], None))
            return found

        def finish(self, total, slot):
            if self.stage == 0:
                def put(rows, value):
                    sum_ref[slot, rows, :] = value.astype(bf)

                total(put)
                o_over(self.i, slot).start()
            else:
                base = self.i * piece

                def put(rows, value):
                    os_ref[pl.ds(base + rows.start, rows.size), :] = value.astype(bf)

                total(put)

        def sent(self, slot):
            if self.stage == 0:
                o_over(self.i, slot).wait_send()

    w_items = [WeightItem(k, i) for k, i in [(kk, ii) for ii in range(depth) for kk in (0, 1)]]
    o_items = [OutItem(s, i) for s in range(2) for i in range(4)]
    order = (
        w_items[0:3] + o_items[0:4] + [w_items[3], w_items[4], o_items[4], o_items[5], o_items[6], w_items[5], o_items[7]]
        + w_items[6:8]
    )
    senders = [item for item in order if (isinstance(item, WeightItem) and item.m) or getattr(item, "stage", 1) == 0]
    sum_slot = {id(item): n % 3 for n, item in enumerate(senders)}
    state = {"next": 0, "y": 2, "open": None}

    def y_next():
        if state["y"] < len(w_items):
            item = w_items[state["y"]]
            y_push(item.k, item.i).start()
            state["y"] += 1

    def fetch(item, slot):
        for n, (src, flag) in enumerate(item.sources()):
            copy = pltpu.make_async_copy(src, in_ref.at[slot, n, pl.ds(0, item.rows)], in_sem.at[slot, n])
            if flag is None:
                copy.start()
            else:
                pl.when(flag)(copy.start)

    def finish(item, slot):
        sources = item.sources()
        for n, (src, flag) in enumerate(sources):
            copy = pltpu.make_async_copy(src, in_ref.at[slot, n, pl.ds(0, item.rows)], in_sem.at[slot, n])
            if flag is None:
                copy.wait()
            else:
                pl.when(flag)(copy.wait)
        place = sum_slot.get(id(item), 0)
        if id(item) in sum_slot:
            n = senders.index(item)
            if n >= 3:
                senders[n - 3].sent(place)

        tile = 16

        def total(put):
            @pl.loop(0, item.rows // tile)
            def _(i):
                rows = pl.ds(pl.multiple_of(i * tile, tile), tile)
                value = None
                for n, (src, flag) in enumerate(sources):
                    term = in_ref[slot, n, rows, :].astype(f32)
                    if flag is not None:
                        term = jnp.where(flag, term, 0.0)
                    value = term if value is None else value + term
                put(rows, value)

        item.finish(total, place)

    def settle_last():
        if state["open"] is not None:
            n = state["open"]
            finish(order[n], n % 2)
            state["open"] = None

    def tick():
        settle_last()
        n = state["next"]
        if n < len(order):
            order[n].ready()
            if isinstance(order[n], WeightItem):
                y_next()
            fetch(order[n], n % 2)
            state["open"] = n
            state["next"] += 1

    def home(g, side):
        store = dx_own if g < 2 else dx_near
        return store, side, pl.ds((g % 2) * UNIT, UNIT)

    def put_unit(g, u, value):
        store, side, _ = home(g, u // 3)
        lo = (g % 2) * UNIT + (u % 3) * 128
        store[side, 0:width, lo : lo + 128] = value.astype(bf)

    def block_rows(zz, yy, xx):
        return pl.ds(pl.multiple_of(2 * owned * (4 * zz + 2 * yy + xx), 16), 2 * owned)

    def block(g, zz, yy, xx):
        store, _, cols = home(g, 0)
        return store.at[c, block_rows(zz, yy, xx), cols]

    def half_push(g):
        store, _, cols = home(g, 0)
        return push(store.at[1 - c, pl.ds(0, width), cols], half_land.at[g], h_send.at[g], h_recv.at[g], sibling)

    def d_push(g, zz, peer):
        return push(block(g, zz, 1 - y, 1 - x), d_land.at[g, zz], d_send.at[g, zz], d_recv.at[g, zz], peer)

    def ys_push(g, zz):
        return push(block(g, zz, 1 - y, x), y_small.at[g, zz], sy_send.at[g, zz], sy_recv.at[g, zz], across)

    def xs_push(g, zz):
        return push(block(g, zz, y, 1 - x), x_small.at[g, zz], sx_send.at[g, zz], sx_recv.at[g, zz], beside)

    def zs_push(g, k, source):
        zz = z ^ k
        return push(block(g, zz, y, x), z_small.at[g, source], sz_send.at[g, k - 1], sz_recv.at[g, source], me.at(z=zz))

    def last_push(g):
        return push(last_out.at[g], last_in.at[g], l_send.at[g], l_recv.at[g], sibling)

    def small_a(g):
        half_push(g).wait_recv()
        store, _, cols = home(g, 0)

        @pl.loop(0, width // 64)
        def _(i):
            rows = pl.ds(pl.multiple_of(i * 64, 64), 64)
            store[c, rows, cols] = (store[c, rows, cols].astype(f32) + half_land[g, rows, :].astype(f32)).astype(bf)

        for zz in range(depth):
            d_push(g, zz, beside if zz % 2 == 0 else across).start()

    def small_b(g):
        store, _, cols = home(g, 0)
        for zz in range(depth):
            d_push(g, zz, beside).wait_recv()
            rows = block_rows(zz, 1 - y, x) if zz % 2 == 0 else block_rows(zz, y, 1 - x)
            store[c, rows, cols] = (store[c, rows, cols].astype(f32) + d_land[g, zz].astype(f32)).astype(bf)
            ys_push(g, zz).start()
            xs_push(g, zz).start()

    def small_c(g):
        store, _, cols = home(g, 0)
        for k in (3, 2, 1, 0):
            zz = z ^ k
            ys_push(g, zz).wait_recv()
            xs_push(g, zz).wait_recv()
            rows = block_rows(zz, y, x)
            value = store[c, rows, cols].astype(f32) + y_small[g, zz].astype(f32) + x_small[g, zz].astype(f32)
            store[c, rows, cols] = value.astype(bf)
            if k:
                zs_push(g, k, z).start()

    def columns(g, side):
        if g == 0:
            return [(gwo_ref, side * UNIT + 128 * i) for i in range(3)]
        found = []
        for i in range(3):
            u = 3 * side + i
            found.append((gwq_ref, (u // 2) * width + 256 * (g - 1) + (u % 2) * 128))
        return found

    def place_columns(g, side, value):
        for i, (ref, lo) in enumerate(columns(g, side)):
            ref[:, lo : lo + 128] = value[:, 128 * i : 128 * i + 128]

    def small_d(g):
        store, _, cols = home(g, 0)
        for k in range(1, depth):
            zs_push(g, k, z ^ k).wait_recv()
        value = store[c, block_rows(z, y, x), cols].astype(f32)
        for k in range(1, depth):
            value = value + z_small[g, z ^ k].astype(f32)
        own_part = jnp.where(c == 0, value[0:owned], value[owned:])
        last_out[g] = jnp.where(c == 0, value[owned:], value[0:owned])
        last_push(g).start()
        for side in range(2):
            @pl.when(c == side)
            def _():
                place_columns(g, side, own_part)

    def small_e(g):
        last_push(g).wait_recv()
        for side in range(2):
            @pl.when(c != side)
            def _():
                place_columns(g, side, last_in[g])

    def small_end(g):
        half_push(g).wait_send()
        for zz in range(depth):
            d_push(g, zz, beside).wait_send()
            ys_push(g, zz).wait_send()
            xs_push(g, zz).wait_send()
        for k in range(1, depth):
            zs_push(g, k, z).wait_send()
        last_push(g).wait_send()

    for xx in range(2):
        dx_sib(xx).start()
    for name in ("dx", "x", "mixed", "hidden", "g", "pos", "wa", "qkv"):
        for copy in loads[name]:
            copy.start()
    gn_ref[...] = jnp.zeros_like(gn_ref)
    in_ref[...] = jnp.zeros_like(in_ref)
    dx_sib(1 - x).wait_recv()
    loaded("dx")
    for i in range(4):
        rows = rows_of(i)
        dx_own[1 - x, rows, :] = (dx_own[1 - x, rows, :].astype(f32) + dx_near[1 - x, rows, :].astype(f32)).astype(bf)
        dx_over(i).start()
    for _ in range(2):
        y_next()
    for xx in range(2):
        o_sib(xx).start()

    loaded("x", "mixed")

    @pl.loop(0, slots // ROWS)
    def _(i):
        rows = pl.ds(i * ROWS, ROWS)
        normal, _ = layer_stats(x_ref[rows, :].astype(f32))
        branch_ref[rows, :] = (normal * norms_ref[0:1, :] + norms_ref[2:3, :]).astype(bf)

    first_t[...] = branch_ref[...].T
    mixed_t[...] = mixed_ref[...].T
    loaded("hidden", "g", "pos", "wa", "qkv")
    tick()
    tick()
    tick()
    settle_last()
    dx_sib(x).wait_recv()
    for i in range(4):
        rows = rows_of(i)
        dx_over(i).wait_recv()
        dx_own[x, rows, :] = (
            dx_own[x, rows, :].astype(f32) + dx_near[x, rows, :].astype(f32) + dx_beside[rows, :].astype(f32)
        ).astype(bf)

    for _ in range(4):
        tick()
    settle_last()

    @pl.loop(0, slots // ROWS)
    def _(i):
        rows = pl.ds(i * ROWS, ROWS)
        place = pos_ref[rows, 0:1].astype(jnp.int32)
        pick = (iota((ROWS, rp), 1) == place).astype(bf)
        grad = mul(pick, dx_own[x])
        normal, scaled = layer_stats(gx_ref[rows, :])
        gn_ref[1:2, :] += jnp.sum(grad * normal, axis=0, keepdims=True)
        gn_ref[3:4, :] += jnp.sum(grad, axis=0, keepdims=True)
        grad_hidden = g_ref[rows, :].astype(f32) + norm_backward(grad, normal, scaled, norms_ref[1:2, :])
        gx_ref[rows, :] = grad_hidden
        branch = grad_hidden.astype(bf)
        branch_ref[rows, :] = branch
        gmix_ref[rows, :] = mul(branch, wa_ref[:, HALF + width : HALF + 2 * width], NT).astype(bf)

    for i in range(4):
        dx_over(i).wait_send()
    tile = width // 3

    @pl.loop(0, 3)
    def _(i):
        rows = pl.ds(i * tile, tile)
        value = mul(mixed_t[rows, :], branch_ref[...]).astype(bf)
        for side in range(2):
            dx_own[side, rows, 0:UNIT] = value[:, side * UNIT : (side + 1) * UNIT]

    half_push(0).start()
    tick()

    def group_product(g):
        j = g - 1
        store_units = []
        for t in range(3):
            lo = t * width + 256 * j
            for i in range(3):
                rows = slice(i * tile, (i + 1) * tile)
                value = mul(first_t[rows, :], qkv_ref[:, lo : lo + 256]).astype(bf)
                for n in range(2):
                    u = 2 * t + n
                    store, side, _ = home(g, u // 3)
                    at = (g % 2) * UNIT + (u % 3) * 128
                    store[side, rows, at : at + 128] = value[:, n * 128 : (n + 1) * 128]
        half_push(g).start()

    plan = [
        [settle_last],
        [tick, lambda: small_a(0), lambda: group_product(1)],
        [tick, tick],
        [tick, lambda: small_b(0), lambda: small_a(1), lambda: group_product(2)],
        [tick],
        [tick, lambda: small_c(0), lambda: small_b(1), lambda: small_a(2), lambda: group_product(3)],
    ]

    lane = iota((slots, 128), 1)
    key_bias = jnp.where(iota((slots, 128), 0) < length, 0.0, NEGATIVE).astype(bf)
    causal = iota((ROWS, ROWS), 0) <= iota((ROWS, ROWS), 1)

    def aug_load(p, slot):
        return pltpu.make_async_copy(aug_far.at[pl.ds(2 * p, 2)], aug_ref.at[slot], aug_sem.at[slot])

    aug_load(0, 0).start()

    @pl.loop(0, pairs)
    def _(p):
        slot = p % 2

        @pl.when(p + 1 < pairs)
        def _():
            aug_load(p + 1, 1 - slot).start()

        aug_load(p, slot).wait()
        cols = pl.ds(p * 128, 128)
        k_cols = pl.ds(width + p * 128, 128)
        v_cols = pl.ds(2 * width + p * 128, 128)
        q = qkv_ref[:, cols]
        q_hi = (q.astype(f32) * (scale * LOG2E)).astype(bf)
        k = qkv_ref[:, k_cols]
        v = qkv_ref[:, v_cols]
        do = gmix_ref[:, cols]
        prod = do.astype(f32) * mixed_ref[:, cols].astype(f32)
        k_t = k.T
        zero = jnp.zeros_like(q)
        one = jnp.ones_like(q)
        for half in range(2):
            own = own_lanes(lane, half)
            extra = extra_lane(half)
            parts = (lane > extra) & (lane <= extra + 3)
            qa_ref[half, :, 0:128] = jnp.where(own, q_hi, zero)
            qa_ref[half, :, 128:256] = aug_ref[slot, half]
            ka_ref[half, :, 0:128] = k
            ka_ref[half, :, 128:256] = jnp.where(
                own, k, jnp.where(lane == extra, key_bias, jnp.where(parts, one, zero))
            )
            va_ref[half, :, :] = jnp.where(own, v, jnp.where(parts, one, zero))
            minus = -jnp.sum(jnp.where(own, prod, 0.0), axis=1, keepdims=True)
            a, b, d = three_parts(jnp.broadcast_to(minus, (slots, 128)))
            oa_ref[half, :, :] = jnp.where(
                own, do,
                jnp.where(lane == extra + 1, a, jnp.where(lane == extra + 2, b, jnp.where(lane == extra + 3, d, zero))),
            )
        for half in range(2):
            k_own = k_t[half * HEAD_DIM : (half + 1) * HEAD_DIM, :]
            heads_rows = slice(half * HEAD_DIM, (half + 1) * HEAD_DIM)
            for j in range(slots // ROWS):
                keys = slice(j * ROWS, (j + 1) * ROWS)
                late = slice(j * ROWS, slots)
                s = mul(ka_ref[half, keys, :], qa_ref[half, late, :], NT)
                diag = jnp.where(causal, s[:, :ROWS], NEGATIVE)
                s = diag if j == slots // ROWS - 1 else jnp.concatenate([diag, s[:, ROWS:]], axis=1)
                probs = jnp.exp2(s)
                dp = mul(va_ref[half, keys, :], oa_ref[half, late, :], NT)
                ds = (probs * dp).astype(bf)
                probs = probs.astype(bf)
                dv_ref[half, keys, :] = mul(probs, gmix_ref[late, cols])
                dk_ref[half, keys, :] = mul(ds, qkv_ref[late, cols])
                dq = mul(k_own[:, keys], ds)
                if j == 0:
                    dq_ref[heads_rows, late] = dq
                else:
                    dq_ref[heads_rows, late] += dq
        first = lane < HEAD_DIM
        qkv_ref[:, cols] = (dq_ref[...].T * scale).astype(bf)
        qkv_ref[:, k_cols] = (jnp.where(first, dk_ref[0], dk_ref[1]) * scale).astype(bf)
        qkv_ref[:, v_cols] = jnp.where(first, dv_ref[0], dv_ref[1]).astype(bf)
        for i in range(pairs):
            @pl.when(p == i)
            def _():
                for step in plan[i]:
                    step()

    @pl.loop(0, slots // ROWS)
    def _(i):
        rows = pl.ds(i * ROWS, ROWS)
        normal, scaled = layer_stats(x_ref[rows, :].astype(f32))
        grad = mul(qkv_ref[rows, : 2 * width], wa_ref[:, : 2 * width], NT) + mul(
            qkv_ref[rows, 2 * width :], wa_ref[:, HALF : HALF + width], NT
        )
        gn_ref[0:1, :] += jnp.sum(grad * normal, axis=0, keepdims=True)
        gn_ref[2:3, :] += jnp.sum(grad, axis=0, keepdims=True)
        gx_ref[rows, :] += norm_backward(grad, normal, scaled, norms_ref[0:1, :])

    gx_out = pltpu.make_async_copy(gx_ref, gx_far, gx_sem)
    gx_out.start()
    counts = jnp.where(iota((8, 128), 0) == iota((8, 128), 1), counts_ref[...], 0).astype(f32)
    gn_ref[4:5, 0:128] = jnp.sum(counts, axis=0, keepdims=True)
    gn_peers = [sibling, beside, across, me.at(z=z ^ 1), me.at(z=z ^ 2)]

    def gn_push(i):
        return push(gn_send.at[i], gn_land.at[i], gs_send.at[i], gs_recv.at[i], gn_peers[i])

    def gn_start(i):
        gn_send[i] = gn_ref[...]
        gn_push(i).start()

    def gn_end(i):
        gn_push(i).wait_recv()
        gn_ref[...] += gn_land[i]

    gn_start(0)
    settle_last()
    small_a(3)
    small_d(0)
    small_c(1)
    small_b(2)
    gn_end(0)
    gn_start(1)
    tick()
    settle_last()
    gn_end(1)
    gn_start(2)
    small_b(3)
    small_e(0)
    small_d(1)
    small_c(2)
    gn_end(2)
    gn_start(3)
    tick()
    settle_last()
    small_c(3)
    small_e(1)
    small_d(2)
    gn_end(3)
    gn_start(4)

    def hidden_load(i):
        return pltpu.make_async_copy(hidden_far.at[pl.ds(i * ROWS, ROWS)], hid_ref.at[i % 2], hid_sem.at[i % 2])

    def out_store(i):
        return pltpu.make_async_copy(outb_ref.at[i % 2], out_far.at[pl.ds(i * ROWS, ROWS)], out_sem.at[i % 2])

    blocks = slots // ROWS
    hidden_load(0).start()
    for i in range(blocks):
        if i + 1 < blocks:
            hidden_load(i + 1).start()
        place = pos_ref[i * ROWS : (i + 1) * ROWS, 0:1].astype(jnp.int32)
        pick = (iota((ROWS, rp), 1) == place).astype(bf)
        value = mul(pick, os_ref[...])
        hidden_load(i).wait()
        if i >= 2:
            out_store(i - 2).wait()
        outb_ref[i % 2] = (hid_ref[i % 2] + value).astype(bf)
        out_store(i).start()

    small_e(2)
    gn_end(4)
    gn_t[...] = jnp.concatenate([gn_ref[...], jnp.zeros((120, width), f32)], axis=0).T
    gn_out[...] = gn_t[pl.ds(pl.multiple_of(owned * (8 * z + 4 * y + 2 * x + c), 8), owned), :]
    cnt_out[...] = gn_ref[:, 0:128]
    small_d(3)
    for i in range(3):
        lane_push(i, True).wait_recv()
    for s in range(4):
        for b in range(2):
            lo = (4 * b + s) * part
            gwin_ref[:, lo : lo + part] = lane_in[s, :, b * part : (b + 1) * part].astype(f32)
    small_e(3)

    for i in range(blocks - 2, blocks):
        out_store(i).wait()
    gx_out.wait()
    for item in senders[-3:]:
        item.sent(sum_slot[id(item)])
    for xx in range(2):
        dx_sib(xx).wait_send()
        o_sib(xx).wait_send()
    for item in w_items[2:]:
        y_push(item.k, item.i).wait_send()
    for i in range(3):
        lane_push(i, False).wait_send()
    for i in range(5):
        gn_push(i).wait_send()
    for g in range(GROUPS):
        small_end(g)


def back(length, norms, counts, x, g, hidden, qkv, mixed, aug, pos, wa, o_part, dx_part, gws, y_first, owned):
    slots, width = x.shape
    rp = dx_part.shape[1]
    part = gws[0].shape[2]
    bf = jnp.bfloat16
    f32 = jnp.float32
    whole = pl.BlockSpec(memory_space=pltpu.VMEM)
    far = pl.BlockSpec(memory_space=pl.ANY)
    dma = pltpu.SemaphoreType.DMA
    v = pltpu.VMEM
    out = jax.ShapeDtypeStruct
    return pl.pallas_call(
        back_kernel,
        out_shape=(
            out((slots, width), bf),
            out((slots, width), f32),
            out((owned, 3 * width), f32),
            out((owned, width), f32),
            out((owned, 128), f32),
            out((8, 128), f32),
            out((part // 4, 8 * part), f32),
            out((part, width), f32),
            out((2, EXPERTS, part, width), bf),
            out((2, EXPERTS, part, width), bf),
            out((2, EXPERTS, part, width), bf),
            out((2, rp, width), bf),
            out((rp, width), bf),
        ),
        in_specs=[pl.BlockSpec(memory_space=pltpu.SMEM), whole, whole] + [far] * 15,
        out_specs=(far, far, whole, whole, whole, whole, whole, whole, far, far, far, far, far),
        scratch_shapes=[
            v((slots, width), bf), v((slots, width), bf), v((slots, width), f32), v((slots, 3 * width), bf),
            v((slots, width), bf), v((2, 2, slots, 128), bf), v((slots, 128), f32), v((width, WIDE), bf),
            v((slots, width), bf), v((slots, width), bf), v((width, slots), bf), v((width, slots), bf),
            v((2, slots, 256), bf), v((2, slots, 256), bf), v((2, slots, 128), bf), v((2, slots, 128), bf),
            v((2, slots, 128), f32), v((2, slots, 128), f32), v((128, slots), f32),
            v((2, rp, width), bf), v((2, rp, width), bf), v((rp, width), bf), v((rp, width), bf),
            v((2, 4, part, width), bf), v((3, part, width), bf), v((part, width), bf), v((4, part // 4, width), bf),
            v((2, ROWS, width), f32), v((2, ROWS, width), bf),
            v((GROUPS, width, UNIT), bf),
            v((GROUPS, 4, 2 * owned, UNIT), bf), v((GROUPS, 4, 2 * owned, UNIT), bf),
            v((GROUPS, 4, 2 * owned, UNIT), bf), v((GROUPS, 4, 2 * owned, UNIT), bf),
            v((GROUPS, owned, UNIT), f32), v((GROUPS, owned, UNIT), f32),
            v((8, width), f32), v((5, 8, width), f32), v((5, 8, width), f32), v((width, 128), f32),
            dma((9,)), dma((2,)), dma((2,)), dma((2,)), dma((4,)), dma((4,)),
            dma((2, 4)), dma((2, 4)), dma((2, 4)), dma((2, 4)), dma((2, 4)), dma((2, 4)),
            dma((2,)), dma((2,)), dma((4,)), dma((4,)), dma((2, 4)),
            dma((3,)), dma((3,)), dma((4,)), dma((4,)), dma((4, 4)), dma((4, 4)), dma((4, 4)), dma((4, 4)),
            dma((4, 4)), dma((4, 4)), dma((4, 3)), dma((4, 4)),
            dma((4,)), dma((4,)), dma((5,)), dma((5,)), dma((2,)), dma((2,)), dma(()),
        ],
        compiler_params=pltpu.CompilerParams(vmem_limit_bytes=62 * MIB, collective_id=1, has_side_effects=True),
        name="back",
    )(length, norms, counts, x, g, hidden, qkv, mixed, aug, pos, wa, o_part, dx_part, *gws, y_first)


def plane_body(
    tokens, token_ids, lengths, hash_table, w_qkv, w_attn_out, norm_gains, norm_biases, w_in, w_out, cotangent
):
    slots, width = tokens.shape
    bf = jnp.bfloat16
    rp = padded_rows(slots)
    part = w_out.shape[0]
    owned = w_qkv.shape[0]

    norm_cols = jnp.concatenate([norm_gains, norm_biases], axis=1)
    local = jnp.concatenate(
        [w_qkv[:, : 2 * width], jnp.pad(norm_cols, ((0, 0), (0, 124))), w_qkv[:, 2 * width :], w_attn_out], axis=1
    )
    local = jnp.pad(local, ((0, 32 - local.shape[0]), (0, WIDE - local.shape[1])))
    table = jnp.pad(hash_table, (0, (-hash_table.shape[0]) % 8192)).reshape(64, 128).T.astype(bf)
    qkv, mixed, aug, hidden, xs, gs, w, wa, norms, pos, counts = front(
        lengths, tokens, token_ids.reshape(1, slots), table, cotangent, local, w_in, w_out
    )
    xs = xs.reshape(4, rp // GROUP + 1, GROUP, width)
    gs = gs.reshape(4, rp // GROUP + 1, GROUP, width)
    n16 = xs[:, rp // GROUP, :EXPERTS, 0].astype(jnp.int32).reshape(-1)
    z = lax.axis_index("dp")
    y = lax.axis_index("fsdp") // 4
    over = [(i, i ^ 4) for i in range(lax.axis_size("fsdp"))]
    late = lax.ppermute(lax.dynamic_slice(w, (0, z, y, 0, 0), (2, 1, 1, part, width)).reshape(2, part, width), "fsdp", over)
    turn_a = jnp.stack([3 * (1 - z // 2), (3 * z + 2) % 5, y])
    turn_b = jnp.stack([1 + z % 2, z, y])
    o_part, dx_part, gw1a, gw2a = experts(n16, turn_a, xs, gs, w)
    halves = lambda v: v.reshape(TURN, 2, part, width)
    gw1a, gw2a = halves(gw1a), halves(gw2a)
    across = lambda v: lax.dynamic_slice(v, (0, 1 - y, 0, 0), (1, 1, part, width)).reshape(1, part, width)
    y_first = lax.ppermute(jnp.concatenate([across(gw1a), across(gw2a)], axis=0), "fsdp", over)
    o_part, dx_part, gw1b, gw2b = experts(n16, turn_b, xs, gs, w, late, (o_part, dx_part))
    out, gx, gwq, gwo, gn, cnt, gwin, gwout = back(
        lengths, norms, counts, tokens, cotangent, hidden, qkv, mixed, aug, pos, wa,
        o_part.reshape(4, rp, width), dx_part.reshape(4, rp, width),
        (gw1a, gw2a, halves(gw1b), halves(gw2b)), y_first, owned,
    )[:8]
    return (out, gx, gwq, gwo, gn[:, 0:2], gn[:, 2:4], gwin, gwout, cnt[4, :EXPERTS].astype(jnp.int32))


def solution(mesh):
    placed = (
        P(("dp", "fsdp"), None),
        P(("dp", "fsdp")),
        P(("dp", "fsdp")),
        P(),
        P(("dp", "fsdp"), None),
        P(("dp", "fsdp"), None),
        P(("dp", "fsdp"), None),
        P(("dp", "fsdp"), None),
        P(("dp", "fsdp"), None),
        P(("dp", "fsdp"), None),
        P(("dp", "fsdp"), None),
    )
    by_plane = mesh.shape["dp"] == EXPERTS and mesh.shape["fsdp"] == 8
    return jax.shard_map(
        plane_body if by_plane else body,
        mesh=mesh,
        in_specs=placed,
        out_specs=(
            P(("dp", "fsdp"), None),
            P(("dp", "fsdp"), None),
            P(("dp", "fsdp"), None),
            P(("dp", "fsdp"), None),
            P(("dp", "fsdp"), None),
            P(("dp", "fsdp"), None),
            P(("dp", "fsdp"), None),
            P(("dp", "fsdp"), None),
            P(),
        ),
        check_vma=False,
    )
```

```python
import functools

import jax
import jax.numpy as jnp
from jax import lax
from jax.experimental import pallas as pl
from jax.experimental.pallas import tpu as pltpu
from jax.sharding import PartitionSpec as P

D = 768
HEADS = 12
HEAD_DIM = 64
EXPERTS = 4
BLOCK = 128


EPSILON = 1e-05
NEGATIVE = -1e30


def layer_stats(values):
    average = jnp.mean(values, axis=-1, keepdims=True)
    centred = values - average
    scaled = lax.rsqrt(jnp.mean(centred * centred, axis=-1, keepdims=True) + EPSILON)
    return (centred * scaled, scaled)


def norm_backward(grad_normed, normal, scaled, gain_col):
    grad_scaled = grad_normed * gain_col
    first_mean = jnp.mean(grad_scaled, axis=-1, keepdims=True)
    second_mean = jnp.mean(grad_scaled * normal, axis=-1, keepdims=True)
    return scaled * (grad_scaled - first_mean - normal * second_mean)


def head_groups(heads):
    group_width = 4
    return [(start, start + group_width) for start in range(0, heads, group_width)]


def allowed_keys(length, seq_len):
    places = jnp.arange(seq_len, dtype=jnp.int32)
    return (places[None, :] <= places[:, None]) & (places[None, :] < length)


def masked_scores(query_part, key_part, allowed):
    scale = query_part.shape[-1] ** (-0.5)
    raw = (
        jnp.einsum("qhd,khd->hqk", query_part, key_part, preferred_element_type=jnp.float32) * scale
    )
    return jnp.where(allowed[None], raw, NEGATIVE)


def attention_forward(entry):
    queries, keys, values, length = entry
    allowed = allowed_keys(length, queries.shape[0])
    mixed_parts = []
    total_parts = []
    for start, finish in head_groups(queries.shape[1]):
        scores = masked_scores(queries[:, start:finish], keys[:, start:finish], allowed)
        highest = jnp.max(scores, axis=-1, keepdims=True)
        totals = highest + jnp.log(jnp.sum(jnp.exp(scores - highest), axis=-1, keepdims=True))
        weights = jnp.exp(scores - totals).astype(jnp.bfloat16)
        mixed_parts.append(
            jnp.einsum(
                "hqk,khd->qhd", weights, values[:, start:finish], preferred_element_type=jnp.float32
            ).astype(jnp.bfloat16)
        )
        total_parts.append(totals[..., 0])
    return (jnp.concatenate(mixed_parts, axis=1), jnp.concatenate(total_parts, axis=0))


def attention_backward(entry):
    queries, keys, values, totals, grad_mixed, length = entry
    allowed = allowed_keys(length, queries.shape[0])
    scale = queries.shape[-1] ** (-0.5)
    query_parts, key_parts, value_parts = ([], [], [])
    for start, finish in head_groups(queries.shape[1]):
        scores = masked_scores(queries[:, start:finish], keys[:, start:finish], allowed)
        weights = jnp.exp(scores - totals[start:finish][..., None])
        grad_weights = jnp.einsum(
            "qhd,khd->hqk",
            grad_mixed[:, start:finish],
            values[:, start:finish],
            preferred_element_type=jnp.float32,
        )
        inner_sum = jnp.sum(grad_weights * weights, axis=-1, keepdims=True)
        grad_scores = (weights * (grad_weights - inner_sum)).astype(jnp.bfloat16)
        value_parts.append(
            jnp.einsum(
                "hqk,qhd->khd",
                weights.astype(jnp.bfloat16),
                grad_mixed[:, start:finish],
                preferred_element_type=jnp.float32,
            )
        )
        query_parts.append(
            jnp.einsum(
                "hqk,khd->qhd",
                grad_scores,
                keys[:, start:finish],
                preferred_element_type=jnp.float32,
            )
            * scale
        )
        key_parts.append(
            jnp.einsum(
                "hqk,qhd->khd",
                grad_scores,
                queries[:, start:finish],
                preferred_element_type=jnp.float32,
            )
            * scale
        )
    return (
        jnp.concatenate(query_parts, axis=1),
        jnp.concatenate(key_parts, axis=1),
        jnp.concatenate(value_parts, axis=1),
    )


def segment_table(group_ends, total_rows, block_rows):
    block_count = total_rows // block_rows
    block_starts = jnp.arange(block_count, dtype=jnp.int32) * block_rows
    points = jnp.sort(jnp.concatenate([block_starts, group_ends]))
    finishes = jnp.concatenate([points[1:], jnp.full((1,), total_rows, jnp.int32)])
    blocks = jnp.minimum(points // block_rows, block_count - 1)
    owners = jnp.sum((group_ends[None, :] <= points[:, None]).astype(jnp.int32), axis=1)
    active = (finishes > points) & (owners < group_ends.shape[0])
    owners = jnp.minimum(owners, group_ends.shape[0] - 1)
    return (points, finishes, blocks, owners, active)


def expert_forward(sorted_rows, inner_all, outer_all, table, block_rows):
    model_width = sorted_rows.shape[1]
    hidden_width = inner_all.shape[1]

    def visit(state, entry):
        start, finish, block_id, owner, live = entry

        def compute(inner_state):
            pre_all, result_all = inner_state
            base = block_id * block_rows
            rows_here = lax.dynamic_slice_in_dim(sorted_rows, base, block_rows, 0)
            inner = lax.dynamic_slice_in_dim(inner_all, owner * model_width, model_width, 0)
            outer = lax.dynamic_slice_in_dim(outer_all, owner * hidden_width, hidden_width, 0)
            places = base + jnp.arange(block_rows, dtype=jnp.int32)
            inside = ((places >= start) & (places < finish))[:, None]
            pre = jnp.dot(rows_here, inner, preferred_element_type=jnp.float32)
            result = jnp.dot(
                jax.nn.gelu(pre).astype(jnp.bfloat16), outer, preferred_element_type=jnp.float32
            )
            old_pre = lax.dynamic_slice_in_dim(pre_all, base, block_rows, 0)
            old_result = lax.dynamic_slice_in_dim(result_all, base, block_rows, 0)
            pre_all = lax.dynamic_update_slice_in_dim(
                pre_all, jnp.where(inside, pre, old_pre), base, 0
            )
            result_all = lax.dynamic_update_slice_in_dim(
                result_all, jnp.where(inside, result, old_result), base, 0
            )
            return (pre_all, result_all)

        return (lax.cond(live, compute, lambda same: same, state), None)

    start_state = (
        jnp.zeros((sorted_rows.shape[0], hidden_width), jnp.float32),
        jnp.zeros((sorted_rows.shape[0], model_width), jnp.float32),
    )
    final_state, _ = lax.scan(visit, start_state, table)
    return final_state


def expert_backward(sorted_rows, pre_all, grad_sorted, inner_all, outer_all, table, block_rows):
    model_width = sorted_rows.shape[1]
    hidden_width = inner_all.shape[1]

    def visit(state, entry):
        start, finish, block_id, owner, live = entry

        def compute(inner_state):
            grad_rows, grad_inner, grad_outer = inner_state
            base = block_id * block_rows
            rows_here = lax.dynamic_slice_in_dim(sorted_rows, base, block_rows, 0)
            pre = lax.dynamic_slice_in_dim(pre_all, base, block_rows, 0)
            inner = lax.dynamic_slice_in_dim(inner_all, owner * model_width, model_width, 0)
            outer = lax.dynamic_slice_in_dim(outer_all, owner * hidden_width, hidden_width, 0)
            places = base + jnp.arange(block_rows, dtype=jnp.int32)
            inside = ((places >= start) & (places < finish))[:, None]
            grad_block = jnp.where(
                inside,
                lax.dynamic_slice_in_dim(grad_sorted, base, block_rows, 0),
                jnp.zeros((), jnp.bfloat16),
            )
            activated, gelu_pull = jax.vjp(jax.nn.gelu, pre)
            outer_piece = jnp.einsum(
                "tf,td->fd",
                activated.astype(jnp.bfloat16),
                grad_block,
                preferred_element_type=jnp.float32,
            )
            grad_act = jnp.einsum(
                "td,fd->tf", grad_block, outer, preferred_element_type=jnp.float32
            )
            grad_pre = gelu_pull(grad_act)[0].astype(jnp.bfloat16)
            inner_piece = jnp.einsum(
                "td,tf->df", rows_here, grad_pre, preferred_element_type=jnp.float32
            )
            rows_piece = jnp.einsum(
                "tf,df->td", grad_pre, inner, preferred_element_type=jnp.float32
            )
            old_rows = lax.dynamic_slice_in_dim(grad_rows, base, block_rows, 0)
            grad_rows = lax.dynamic_update_slice_in_dim(grad_rows, old_rows + rows_piece, base, 0)
            old_inner = lax.dynamic_slice_in_dim(grad_inner, owner * model_width, model_width, 0)
            grad_inner = lax.dynamic_update_slice_in_dim(
                grad_inner, old_inner + inner_piece, owner * model_width, 0
            )
            old_outer = lax.dynamic_slice_in_dim(grad_outer, owner * hidden_width, hidden_width, 0)
            grad_outer = lax.dynamic_update_slice_in_dim(
                grad_outer, old_outer + outer_piece, owner * hidden_width, 0
            )
            return (grad_rows, grad_inner, grad_outer)

        return (lax.cond(live, compute, lambda same: same, state), None)

    start_state = (
        jnp.zeros(sorted_rows.shape, jnp.float32),
        jnp.zeros(inner_all.shape, jnp.float32),
        jnp.zeros(outer_all.shape, jnp.float32),
    )
    final_state, _ = lax.scan(visit, start_state, table)
    return final_state


def body(
    tokens,
    token_ids,
    lengths,
    hash_table,
    w_qkv,
    w_attn_out,
    norm_gains,
    norm_biases,
    w_in,
    w_out,
    cotangent,
):
    rows_count = tokens.shape[0]
    seq_count = lengths.shape[0]
    seq_len = rows_count // seq_count
    model_width = D
    expert_total = EXPERTS
    qkv_full, proj_full, gains_full, biases_full = (
        lax.all_gather(w_qkv, ("dp", "fsdp"), axis=0, tiled=True),
        lax.all_gather(w_attn_out, ("dp", "fsdp"), axis=0, tiled=True),
        lax.all_gather(norm_gains, ("dp", "fsdp"), axis=0, tiled=True),
        lax.all_gather(norm_biases, ("dp", "fsdp"), axis=0, tiled=True),
    )
    gains_f = gains_full.astype(jnp.float32)
    biases_f = biases_full.astype(jnp.float32)
    inputs = tokens.astype(jnp.float32)
    normal_one, scaled_one = layer_stats(inputs)
    first_in = (normal_one * gains_f[:, 0] + biases_f[:, 0]).astype(jnp.bfloat16)
    qkv_low = jnp.dot(first_in, qkv_full, preferred_element_type=jnp.float32).astype(jnp.bfloat16)
    packed = qkv_low.reshape(seq_count, seq_len, 3, HEADS, HEAD_DIM)
    queries = packed[:, :, 0]
    keys = packed[:, :, 1]
    values = packed[:, :, 2]
    mixed, totals = lax.map(attention_forward, (queries, keys, values, lengths))
    mixed_flat = mixed.reshape(rows_count, model_width)
    hidden = inputs + jnp.dot(mixed_flat, proj_full, preferred_element_type=jnp.float32)
    normal_two, scaled_two = layer_stats(hidden)
    second_in = (normal_two * gains_f[:, 1] + biases_f[:, 1]).astype(jnp.bfloat16)
    places = jnp.arange(rows_count, dtype=jnp.int32) % seq_len
    used = places < jnp.repeat(lengths, seq_len, total_repeat_length=rows_count)
    expert_ids = jnp.where(used, hash_table[token_ids], expert_total)
    matches = (expert_ids[:, None] == jnp.arange(expert_total, dtype=jnp.int32)[None, :]).astype(
        jnp.int32
    )
    local_counts = jnp.sum(matches, axis=0)
    expert_counts = lax.psum(local_counts, ("dp", "fsdp"))
    ordering = jnp.argsort(expert_ids, stable=True)
    inverse = (
        jnp.zeros((rows_count,), jnp.int32)
        .at[ordering]
        .set(jnp.arange(rows_count, dtype=jnp.int32))
    )
    group_ends = jnp.cumsum(local_counts)
    table = segment_table(group_ends, rows_count, BLOCK)
    inner_all, outer_all = (
        lax.all_gather(w_in, ("dp", "fsdp"), axis=0, tiled=True),
        lax.all_gather(w_out, ("dp", "fsdp"), axis=0, tiled=True),
    )
    sorted_rows = second_in[ordering]
    pre_all, result_sorted = expert_forward(sorted_rows, inner_all, outer_all, table, BLOCK)
    layer_out = (hidden + result_sorted[inverse]).astype(jnp.bfloat16)
    grad_out = cotangent.astype(jnp.float32)
    grad_sorted = cotangent[ordering]
    inner_back, outer_back = (
        lax.all_gather(w_in, ("dp", "fsdp"), axis=0, tiled=True),
        lax.all_gather(w_out, ("dp", "fsdp"), axis=0, tiled=True),
    )
    grad_rows_sorted, grad_inner, grad_outer = expert_backward(
        sorted_rows, pre_all, grad_sorted, inner_back, outer_back, table, BLOCK
    )
    grad_w_in, grad_w_out = (
        lax.psum_scatter(grad_inner, ("dp", "fsdp"), scatter_dimension=0, tiled=True),
        lax.psum_scatter(grad_outer, ("dp", "fsdp"), scatter_dimension=0, tiled=True),
    )
    grad_second = grad_rows_sorted[inverse]
    gain_two = jnp.sum(grad_second * normal_two, axis=0)
    bias_two = jnp.sum(grad_second, axis=0)
    grad_hidden = grad_out + norm_backward(grad_second, normal_two, scaled_two, gains_f[:, 1])
    grad_branch = grad_hidden.astype(jnp.bfloat16)
    qkv_back, proj_back = (
        lax.all_gather(w_qkv, ("dp", "fsdp"), axis=0, tiled=True),
        lax.all_gather(w_attn_out, ("dp", "fsdp"), axis=0, tiled=True),
    )
    grad_proj = jnp.einsum("td,te->de", mixed_flat, grad_branch, preferred_element_type=jnp.float32)
    grad_mixed = jnp.einsum(
        "te,de->td", grad_branch, proj_back, preferred_element_type=jnp.float32
    ).astype(jnp.bfloat16)
    grad_mixed = grad_mixed.reshape(seq_count, seq_len, HEADS, HEAD_DIM)
    grad_queries, grad_keys, grad_values = lax.map(
        attention_backward, (queries, keys, values, totals, grad_mixed, lengths)
    )
    grad_qkv = (
        jnp.stack([grad_queries, grad_keys, grad_values], axis=2)
        .reshape(rows_count, 3 * model_width)
        .astype(jnp.bfloat16)
    )
    grad_qkv_w = jnp.einsum("td,te->de", first_in, grad_qkv, preferred_element_type=jnp.float32)
    grad_first = jnp.einsum("te,de->td", grad_qkv, qkv_back, preferred_element_type=jnp.float32)
    gain_one = jnp.sum(grad_first * normal_one, axis=0)
    bias_one = jnp.sum(grad_first, axis=0)
    grad_tokens = grad_hidden + norm_backward(grad_first, normal_one, scaled_one, gains_f[:, 0])
    grad_gains = jnp.stack([gain_one, gain_two], axis=1)
    grad_biases = jnp.stack([bias_one, bias_two], axis=1)
    grad_w_qkv, grad_w_attn_out, grad_norm_gains, grad_norm_biases = (
        lax.psum_scatter(grad_qkv_w, ("dp", "fsdp"), scatter_dimension=0, tiled=True),
        lax.psum_scatter(grad_proj, ("dp", "fsdp"), scatter_dimension=0, tiled=True),
        lax.psum_scatter(grad_gains, ("dp", "fsdp"), scatter_dimension=0, tiled=True),
        lax.psum_scatter(grad_biases, ("dp", "fsdp"), scatter_dimension=0, tiled=True),
    )
    return (
        layer_out,
        grad_tokens,
        grad_w_qkv,
        grad_w_attn_out,
        grad_norm_gains,
        grad_norm_biases,
        grad_w_in,
        grad_w_out,
        expert_counts,
    )


LOG2E = 1.4426950408889634
ROWS = 256
GROUP = 16
MIB = 1024 * 1024
NT = (((1,), (1,)), ((), ()))
NN = (((1,), (0,)), ((), ()))
ROOT = 0.7978845608028654
CUBIC = 0.044715


def mul(a, b, dims=NN):
    return lax.dot_general(a, b, dims, preferred_element_type=jnp.float32)


def iota(shape, dim):
    return lax.broadcasted_iota(jnp.int32, shape, dim)


def padded_rows(slots):
    return slots + EXPERTS * GROUP


def three_parts(v):
    first = v.astype(jnp.bfloat16)
    rest = v - first.astype(jnp.float32)
    second = rest.astype(jnp.bfloat16)
    third = (rest - second.astype(jnp.float32)).astype(jnp.bfloat16)
    return first, second, third


def own_lanes(lane, half):
    return (lane < HEAD_DIM) if half == 0 else (lane >= HEAD_DIM)


def extra_lane(half):
    return HEAD_DIM if half == 0 else 0


def routing(ids, table, length, perm_ref):
    slots = ids.shape[1]
    chosen = (iota((table.shape[1], slots), 0) == (ids >> 7)).astype(jnp.bfloat16)
    rows = mul(table, chosen)
    expert = jnp.sum(
        jnp.where(iota(rows.shape, 0) == (ids & 127), rows, 0.0), axis=0, keepdims=True
    ).astype(jnp.int32)
    used = iota((1, slots), 1) < length
    member = (iota((8, slots), 0) == expert) & used
    member_f = jnp.where(member, 1.0, 0.0)
    perm_ref[0:slots, :] = (iota((slots, slots), 0) <= iota((slots, slots), 1)).astype(jnp.bfloat16)
    rank = mul(member_f.astype(jnp.bfloat16), perm_ref[0:slots, :])
    counts = rank[:, slots - 1 : slots]
    groups = jnp.floor((counts + (GROUP - 1)) * (1.0 / GROUP))
    row8 = iota((8, 1), 0)
    start = jnp.zeros((8, 1), jnp.float32)
    for e in range(EXPERTS - 1):
        start = start + jnp.where(row8 > e, groups[e : e + 1, :], 0.0)
    place = jnp.sum(member_f * (rank - 1.0 + start * GROUP), axis=0, keepdims=True)
    place = jnp.where(used, place, -1.0)
    return place, counts, groups


MESH = pl.DeviceIdType.MESH
HALF = 1664
WIDE = 2 * HALF


class Place:
    def __init__(self):
        self.z = lax.axis_index("dp")
        f = lax.axis_index("fsdp")
        self.y = f // 4
        self.x = (f // 2) % 2
        self.c = f % 2

    def at(self, z=None, y=None, x=None, c=None):
        z = self.z if z is None else z
        y = self.y if y is None else y
        x = self.x if x is None else x
        c = self.c if c is None else c
        return (z, 4 * y + 2 * x + c)

    def greet(self, peers):
        barrier = pltpu.get_barrier_semaphore()
        for peer in peers:
            pl.semaphore_signal(barrier, inc=1, device_id=peer, device_id_type=MESH)
        pl.semaphore_wait(barrier, len(peers))


def push(src, dst, send, recv, peer):
    return pltpu.make_async_remote_copy(
        src_ref=src, dst_ref=dst, send_sem=send, recv_sem=recv, device_id=peer, device_id_type=MESH
    )


def front_kernel(
    len_ref, x_far, ids_ref, table_ref, g_far, wqkv_ref, wo_ref, gains_ref, biases_ref, win_ref, wout_ref,
    qkv_far, mixed_far, aug_far, hidden_far, xs_ref, gs_ref, w_ref, wa_far, norms_ref, pos_far, counts_ref, late_ref,
    x_ref, g_ref, qkv_ref, mixed_ref, aug_ref, hidden_ref, wa_ref, pos_ref, in_sem, out_sem, late_sem, local_ref,
    perm_ref, normed_ref, qa_ref, ka_ref, va_ref, tokx_ref, tokg_ref, sib_ref,
    sem0, sz, rz, sy, ry, sx, rx, sd, rd, ss, rs,
    tok_local, tok_send, tok_recv,
    lane_local, lane_send, lane_recv, up_send, down_send, line_recv, y_send, y_recv,
):
    slots, width = x_ref.shape
    heads = width // HEAD_DIM
    rp = padded_rows(slots)
    length = len_ref[0]
    me = Place()
    z, y, x, c = me.z, me.y, me.x, me.c
    depth = 4
    sibling, beside, across = me.at(c=1 - c), me.at(x=1 - x), me.at(y=1 - y)
    owned = wqkv_ref.shape[0]
    local_ref[0:owned, 0 : 2 * width] = wqkv_ref[:, 0 : 2 * width]
    local_ref[0:owned, HALF : HALF + width] = wqkv_ref[:, 2 * width :]
    local_ref[0:owned, HALF + width : HALF + 2 * width] = wo_ref[...]
    local_ref[0:owned, HALF + 2 * width :] = jnp.zeros((owned, HALF - 2 * width), jnp.bfloat16)
    lane_n = iota((owned, 128), 1)
    norm_cols = jnp.zeros((owned, 128), jnp.float32)
    for i, ref in enumerate((gains_ref, gains_ref, biases_ref, biases_ref)):
        norm_cols = jnp.where(lane_n == i, ref[:, i % 2 : i % 2 + 1].astype(jnp.float32), norm_cols)
    local_ref[0:owned, 2 * width : HALF] = norm_cols.astype(jnp.bfloat16)
    local_ref[owned:, :] = jnp.zeros((local_ref.shape[0] - owned, WIDE), jnp.bfloat16)
    me.greet([sibling, beside, across, me.at(x=1 - x, c=1 - c)] + [me.at(z=z ^ k) for k in range(1, depth)])

    first = push(local_ref, sib_ref, sem0.at[0], sem0.at[1], sibling)
    first.start()
    x_load = pltpu.make_async_copy(x_far, x_ref, in_sem.at[0])
    g_load = pltpu.make_async_copy(g_far, g_ref, in_sem.at[1])
    g_load.start()
    x_load.start()
    qkv_out, mixed_out, aug_out, hidden_out, wa_out, pos_out = [
        pltpu.make_async_copy(src, dst, out_sem.at[i])
        for i, (src, dst) in enumerate((
            (qkv_ref, qkv_far), (mixed_ref, mixed_far), (aug_ref, aug_far), (hidden_ref, hidden_far),
            (wa_ref, wa_far), (pos_ref, pos_far),
        ))
    ]

    def block(zz, yy, xx):
        rows = pl.ds(pl.multiple_of(48 * (4 * zz + 2 * yy + xx), 48), 48)
        return wa_ref.at[rows, pl.ds(pl.multiple_of(c * HALF, 128), HALF)]

    def share(zz, yy, xx, send, recv, peer):
        ref = block(zz, yy, xx)
        return push(ref, ref, send, recv, peer)

    def z_up(source):
        return share(source, y, x, sz.at[0, source], rz.at[source], me.at(z=jnp.minimum(z + 1, depth - 1)))

    def z_down(source):
        return share(source, y, x, sz.at[1, source], rz.at[source], me.at(z=jnp.maximum(z - 1, 0)))

    def y_copy(zz, source_y):
        return share(zz, source_y, x, sy.at[zz], ry.at[zz], across)

    def x_copy(zz, source_x):
        return share(zz, y, source_x, sx.at[zz], rx.at[zz], beside)

    def d_copy_x(zz, yy, xx):
        return share(zz, yy, xx, sd.at[zz], rd.at[zz], beside)

    def d_copy_y(zz, yy, xx):
        return share(zz, yy, xx, sd.at[zz], rd.at[zz], across)

    def s_copy(zz, side):
        ref = wa_ref.at[pl.ds(pl.multiple_of(192 * zz, 192), 192), pl.ds(pl.multiple_of(side * HALF, 128), HALF)]
        return push(ref, ref, ss.at[zz], rs.at[zz], sibling)

    part = wout_ref.shape[0]
    rows_in = win_ref.shape[0]
    lanes = [(1 - x, c), (x, 1 - c), (1 - x, 1 - c)]

    def lane_cols(b, xx, cc):
        return win_ref.at[:, pl.ds(pl.multiple_of(part * (4 * b + 2 * xx + cc), 128), part)]

    def lane_home(b, xx, cc):
        return w_ref.at[0, z, y, pl.ds(pl.multiple_of(rows_in * (2 * xx + cc), rows_in), rows_in), pl.ds(b * part, part)]

    def lane_copy(i, b, arrive):
        xx, cc = lanes[i]
        home = lane_home(b, xx, cc) if arrive else lane_home(b, x, c)
        return push(lane_cols(b, xx, cc), home, lane_send.at[i, b], lane_recv.at[i, b], me.at(x=xx, c=cc))

    def lane_own(b):
        return pltpu.make_async_copy(lane_cols(b, x, c), lane_home(b, x, c), lane_local.at[b])

    own_out = pltpu.make_async_copy(wout_ref, w_ref.at[1, z, y], lane_local.at[2])

    def shard(k, zz, yy):
        return w_ref.at[k, zz, yy]

    late_copies = [
        pltpu.make_async_copy(w_ref.at[0, z, y], late_ref.at[0], late_sem.at[0]),
        pltpu.make_async_copy(wout_ref, late_ref.at[1], late_sem.at[1]),
    ]

    def up_copy(k, zz):
        return push(shard(k, zz, y), shard(k, zz, y), up_send.at[k, zz], line_recv.at[k, zz], me.at(z=jnp.minimum(z + 1, depth - 1)))

    def down_copy(k, zz):
        return push(shard(k, zz, y), shard(k, zz, y), down_send.at[k, zz], line_recv.at[k, zz], me.at(z=jnp.maximum(z - 1, 0)))

    def over_copy(k, zz, yy):
        return push(shard(k, zz, yy), shard(k, zz, yy), y_send.at[k, zz], y_recv.at[k, zz], across)

    def spread(k):
        @pl.when(z < depth - 1)
        def _():
            up_copy(k, z).start()

        @pl.when(z > 0)
        def _():
            down_copy(k, z).start()

    def relay(k, s):
        @pl.when(z >= s)
        def _():
            up_copy(k, z - s).wait_recv()

            @pl.when(z < depth - 1)
            def _():
                up_copy(k, z - s).start()

            over_copy(k, z - s, y).start()

        @pl.when(z + s < depth)
        def _():
            down_copy(k, z + s).wait_recv()

            @pl.when(z > 0)
            def _():
                down_copy(k, z + s).start()

            over_copy(k, z + s, y).start()

    def weights_start():
        for i in range(3):
            for b in range(2):
                lane_copy(i, b, False).start()

    def weights_lane():
        for i in range(3):
            for b in range(2):
                lane_copy(i, b, True).wait_recv()
        for b in range(2):
            lane_own(b).wait()
        spread(0)
        late_copies[0].start()

    def relay_of(k, s):
        return functools.partial(relay, k, s)

    def weights_end():
        for k in (1, 0):
            for zz in range(depth):
                @pl.when(zz != z)
                def _():
                    over_copy(k, zz, 1 - y).wait()

                for copy, stop in ((up_copy, depth - 1), (down_copy, 0)):
                    inside = (zz <= z) if stop else (zz >= z)

                    @pl.when(inside & (z != stop))
                    def _():
                        copy(k, zz).wait_send()

        for i in range(3):
            for b in range(2):
                lane_copy(i, b, False).wait_send()

    mine = 2 * x + c

    def tok_copies(k, scratch, far_ref):
        own = pltpu.make_async_copy(scratch, far_ref.at[mine], tok_local.at[k])
        near = push(scratch, far_ref.at[mine], tok_send.at[k, 0], tok_recv.at[k, 0], sibling)
        far = push(scratch, far_ref.at[mine], tok_send.at[k, 1], tok_recv.at[k, 1], beside)
        slot = far_ref.at[2 * (1 - x) + c]
        onward = push(slot, slot, tok_send.at[k, 2], tok_recv.at[k, 2], sibling)
        return own, near, far, onward

    x_copies = tok_copies(0, tokx_ref, xs_ref)
    g_copies = tok_copies(1, tokg_ref, gs_ref)

    first.wait_recv()
    zero_core = c == 0
    own_cols = pl.ds(pl.multiple_of(c * HALF, 128), HALF)
    local = local_ref[0:24, own_cols]
    other = sib_ref[0:24, own_cols]
    own_rows = pl.ds(pl.multiple_of(48 * (4 * z + 2 * y + x), 48), 48)
    wa_ref[own_rows, own_cols] = jnp.concatenate(
        [jnp.where(zero_core, local, other), jnp.where(zero_core, other, local)], axis=0
    )
    def planes(s, act):
        @pl.when(z >= s)
        def _():
            act(z - s, True)

        if s:
            @pl.when(z + s < depth)
            def _():
                act(z + s, False)

    def z_arrived(zz, upward):
        z_up(zz).wait_recv()
        if upward:
            pl.when(z < depth - 1)(z_up(zz).start)
        else:
            pl.when(z > 0)(z_down(zz).start)
        y_copy(zz, y).start()
        x_copy(zz, x).start()

    def near_arrived(zz, _):
        y_copy(zz, 1 - y).wait_recv()
        x_copy(zz, 1 - x).wait_recv()
        pl.when(zz % 2 == 0)(d_copy_x(zz, 1 - y, x).start)
        pl.when(zz % 2 == 1)(d_copy_y(zz, y, 1 - x).start)

    def corner_arrived(zz, _):
        d_copy_x(zz, 1 - y, 1 - x).wait_recv()
        s_copy(zz, c).start()

    pl.when(z < depth - 1)(z_up(z).start)
    pl.when(z > 0)(z_down(z).start)
    y_copy(z, y).start()
    x_copy(z, x).start()
    for b in range(2):
        lane_own(b).start()
    own_out.start()
    late_copies[1].start()

    table = table_ref[...].astype(jnp.float32).T.astype(jnp.bfloat16)
    place, counts, groups = routing(ids_ref[...], table, length, perm_ref)
    place_i = place.astype(jnp.int32)
    pos_ref[...] = jnp.broadcast_to(place, (128, slots)).T
    pos_out.start()
    counts_ref[...] = jnp.broadcast_to(counts, (8, 128)).astype(jnp.int32)

    planes(1, z_arrived)
    planes(0, near_arrived)
    planes(2, z_arrived)
    planes(1, near_arrived)
    planes(3, z_arrived)
    own_out.wait()
    spread(1)
    planes(0, corner_arrived)
    step = rp // 4

    @pl.loop(0, 4)
    def _(i):
        base = i * step
        perm_ref[pl.ds(base, step), :] = (
            iota((step, slots), 0) + base == place_i
        ).astype(jnp.bfloat16)

    planes(2, near_arrived)
    planes(1, corner_arrived)
    planes(3, near_arrived)
    weights_start()

    g_load.wait()

    @pl.loop(0, 4)
    def _(i):
        rows = pl.ds(i * step, step)
        tokg_ref[rows, :] = mul(perm_ref[rows, :], g_ref[...]).astype(jnp.bfloat16)

    tail = jnp.broadcast_to(jnp.concatenate([groups, groups], axis=0), (GROUP, width)).astype(jnp.bfloat16)
    tokx_ref[rp : rp + GROUP, :] = tail
    tokg_ref[rp : rp + GROUP, :] = tail

    planes(2, corner_arrived)
    planes(3, corner_arrived)
    for k in range(depth):
        s_copy(z ^ k, 1 - c).wait_recv()
    for copy in g_copies[:3]:
        copy.start()
    wa_out.start()
    x_load.wait()

    cols_t = wa_ref[:, 2 * width : 2 * width + 128].astype(jnp.float32).T
    norms_ref[...] = cols_t[0:8, :]

    @pl.loop(0, slots // ROWS)
    def _(i):
        rows = pl.ds(i * ROWS, ROWS)
        normal, _ = layer_stats(x_ref[rows, :].astype(jnp.float32))
        normed = (normal * norms_ref[0:1, :] + norms_ref[2:3, :]).astype(jnp.bfloat16)
        for part_i, start in enumerate((0, width, HALF)):
            cols = slice(part_i * width, (part_i + 1) * width)
            qkv_ref[rows, cols] = mul(normed, wa_ref[:, start : start + width]).astype(jnp.bfloat16)

    qkv_out.start()
    lane = iota((slots, 128), 1)
    key_bias = jnp.where(iota((slots, 128), 0) < length, 0.0, NEGATIVE).astype(jnp.bfloat16)
    causal = iota((ROWS, ROWS), 1) <= iota((ROWS, ROWS), 0)
    lane_b = iota((ROWS, 128), 1)
    pairs = heads // 2
    slots_for = [[relay_of(1, 1)], [weights_lane], [], [relay_of(1, 2)], [], [relay_of(0, 1)]]

    @pl.loop(0, pairs)
    def _(p):
        cols = pl.ds(p * 128, 128)
        q = qkv_ref[:, cols].astype(jnp.float32) * (HEAD_DIM ** -0.5 * LOG2E)
        q_hi = q.astype(jnp.bfloat16)
        q_lo = (q - q_hi.astype(jnp.float32)).astype(jnp.bfloat16)
        k = qkv_ref[:, pl.ds(width + p * 128, 128)]
        v = qkv_ref[:, pl.ds(2 * width + p * 128, 128)]
        zero = jnp.zeros_like(q_hi)
        one = jnp.ones_like(q_hi)
        for half in range(2):
            own = own_lanes(lane, half)
            extra = extra_lane(half)
            qa_ref[half, :, 0:128] = jnp.where(own, q_hi, zero)
            qa_ref[half, :, 128:256] = jnp.where(own, q_lo, jnp.where(lane == extra, one, zero))
            ka_ref[half, :, 0:128] = k
            ka_ref[half, :, 128:256] = jnp.where(own, k, jnp.where(lane == extra, key_bias, zero))
            va_ref[half, :, :] = jnp.where(own, v, one)
        for i in range(slots // ROWS):
            rows = slice(i * ROWS, (i + 1) * ROWS)
            keys = (i + 1) * ROWS
            outs = []
            for half in range(2):
                s = mul(qa_ref[half, rows, :], ka_ref[half, 0:keys, :], NT)
                diag = jnp.where(causal, s[:, i * ROWS :], NEGATIVE)
                s = diag if i == 0 else jnp.concatenate([s[:, : i * ROWS], diag], axis=1)
                top = jnp.max(s, axis=1, keepdims=True)
                probs = jnp.exp2(s - top).astype(jnp.bfloat16)
                out = mul(probs, va_ref[half, 0:keys, :])
                total = pltpu.roll(out, HEAD_DIM, 1)
                outs.append(out / total)
                minus = -(top + jnp.log2(out))
                a, b, d = three_parts(minus)
                extra = extra_lane(half)
                seen = qa_ref[half, rows, 128:256]
                seen = jnp.where(lane_b == extra + 1, a, seen)
                seen = jnp.where(lane_b == extra + 2, b, seen)
                seen = jnp.where(lane_b == extra + 3, d, seen)
                aug_ref[2 * p + half, rows, :] = seen
            mixed_ref[rows, cols] = jnp.where(lane_b < HEAD_DIM, outs[0], outs[1]).astype(jnp.bfloat16)
        for i in range(pairs):
            @pl.when(p == i)
            def _():
                for tick in slots_for[i]:
                    tick()

    @pl.loop(0, slots // ROWS)
    def _(i):
        rows = pl.ds(i * ROWS, ROWS)
        hidden = x_ref[rows, :].astype(jnp.float32) + mul(mixed_ref[rows, :], wa_ref[:, HALF + width : HALF + 2 * width])
        hidden_ref[rows, :] = hidden
        normal, _ = layer_stats(hidden)
        normed_ref[rows, :] = (normal * norms_ref[1:2, :] + norms_ref[3:4, :]).astype(jnp.bfloat16)

    @pl.loop(0, 4)
    def _(i):
        rows = pl.ds(i * step, step)
        tokx_ref[rows, :] = mul(perm_ref[rows, :], normed_ref[...]).astype(jnp.bfloat16)

    for copy in x_copies[:3]:
        copy.start()
    for copy in (mixed_out, aug_out, hidden_out):
        copy.start()
    relay(1, 3)
    relay(0, 2)
    g_copies[2].wait_recv()
    g_copies[3].start()
    relay(0, 3)
    x_copies[2].wait_recv()
    x_copies[3].start()
    weights_end()
    for own, near, far, onward in (x_copies, g_copies):
        own.wait()
        near.wait()
        far.wait_send()
        onward.wait()
    for copy in [qkv_out, mixed_out, aug_out, hidden_out, wa_out, pos_out] + late_copies:
        copy.wait()
    first.wait_send()
    for zz in range(depth):
        pl.when((zz <= z) & (z < depth - 1))(z_up(zz).wait_send)
        pl.when((zz >= z) & (z > 0))(z_down(zz).wait_send)
        y_copy(zz, y).wait_send()
        x_copy(zz, x).wait_send()
        d_copy_x(zz, y, x).wait_send()
        s_copy(zz, c).wait_send()


def front(length, x, ids, table, g, w_qkv, w_o, gains, biases, w_in, w_out):
    slots, width = x.shape
    rp = padded_rows(slots)
    part = w_out.shape[0]
    bf = jnp.bfloat16
    f32 = jnp.float32
    whole = pl.BlockSpec(memory_space=pltpu.VMEM)
    far = pl.BlockSpec(memory_space=pl.ANY)
    dma = pltpu.SemaphoreType.DMA
    return pl.pallas_call(
        front_kernel,
        out_shape=(
            jax.ShapeDtypeStruct((slots, 3 * width), bf),
            jax.ShapeDtypeStruct((slots, width), bf),
            jax.ShapeDtypeStruct((HEADS, slots, 128), bf),
            jax.ShapeDtypeStruct((slots, width), f32),
            jax.ShapeDtypeStruct((4, rp + GROUP, width), bf),
            jax.ShapeDtypeStruct((4, rp + GROUP, width), bf),
            jax.ShapeDtypeStruct((2, EXPERTS, 2, part, width), bf),
            jax.ShapeDtypeStruct((width, WIDE), bf),
            jax.ShapeDtypeStruct((8, width), f32),
            jax.ShapeDtypeStruct((slots, 128), f32),
            jax.ShapeDtypeStruct((8, 128), jnp.int32),
            jax.ShapeDtypeStruct((2, part, width), bf),
        ),
        in_specs=[pl.BlockSpec(memory_space=pltpu.SMEM), far, whole, whole, far, whole, whole, whole, whole, far, far],
        out_specs=(far, far, far, far, far, far, far, far, whole, far, whole, far),
        scratch_shapes=[
            pltpu.VMEM((slots, width), bf),
            pltpu.VMEM((slots, width), bf),
            pltpu.VMEM((slots, 3 * width), bf),
            pltpu.VMEM((slots, width), bf),
            pltpu.VMEM((HEADS, slots, 128), bf),
            pltpu.VMEM((slots, width), f32),
            pltpu.VMEM((width, WIDE), bf),
            pltpu.VMEM((slots, 128), f32),
            dma((2,)), dma((6,)), dma((2,)),
            pltpu.VMEM((32, WIDE), bf),
            pltpu.VMEM((rp, slots), bf),
            pltpu.VMEM((slots, width), bf),
            pltpu.VMEM((2, slots, 256), bf),
            pltpu.VMEM((2, slots, 256), bf),
            pltpu.VMEM((2, slots, 128), bf),
            pltpu.VMEM((rp + GROUP, width), bf),
            pltpu.VMEM((rp + GROUP, width), bf),
            pltpu.VMEM((32, WIDE), bf),
            dma((2,)), dma((2, 4)), dma((4,)), dma((4,)), dma((4,)), dma((4,)), dma((4,)), dma((4,)), dma((4,)),
            dma((4,)), dma((4,)),
            dma((2,)), dma((2, 3)), dma((2, 3)),
            dma((3,)), dma((3, 2)), dma((3, 2)), dma((2, 4)), dma((2, 4)), dma((2, 4)), dma((2, 4)), dma((2, 4)),
        ],
        compiler_params=pltpu.CompilerParams(vmem_limit_bytes=56 * MIB, collective_id=0, has_side_effects=True),
        name="front",
    )(length, x, ids, table, g, w_qkv, w_o, gains, biases, w_in, w_out)


CHUNK = 32
TURN = 2


def experts_kernel(
    fresh, n_ref, x_ref, g_ref, w_far, *refs,
):
    if fresh:
        late_far = None
    else:
        late_far, refs = refs[0], refs[3:]
    (
        o_ref, dx_ref, gw1_far, gw2_far, cross_far,
        w_ref, xb, gb, ob, db, acc1, acc2, stage, blank, sem_in, sem_out, sem_zero, sem_w, sem_gw, sem_cross,
    ) = refs
    sources, groups, _, width = x_ref.shape
    groups = groups - 1
    z = lax.axis_index("dp")
    y = lax.axis_index("fsdp") // 4
    who = (3 * (1 - z // 2), (3 * z + 2) % 5) if fresh else (1 + z % 2, z)

    copies = []
    for i in range(TURN):
        for k in range(2):
            if not fresh and i == TURN - 1:
                pairs = [(w_far.at[k, who[i], y], y), (late_far.at[k], 1 - y)]
            else:
                pairs = [(w_far.at[k, who[i], h], h) for h in range(2)]
            for n, (src, h) in enumerate(pairs):
                copies.append(pltpu.make_async_copy(src, w_ref.at[i, k, h], sem_w.at[i, 2 * k + n]))
    for copy in copies:
        copy.start()

    totals = []
    for i in range(TURN):
        totals.append(lax.fori_loop(0, sources, lambda s, t, i=i: t + n_ref[s * EXPERTS + who[i]], 0))
    first = [0]
    for i in range(TURN):
        first.append(first[-1] + (totals[i] + (CHUNK - 1)) // CHUNK)
    chunks = first[TURN]

    def locate(c):
        i = jnp.where(c >= first[1], 1, 0)
        begin = (c - jnp.where(i == 1, first[1], 0)) * CHUNK
        return i, begin, jnp.minimum(begin + CHUNK, jnp.where(i == 1, totals[1], totals[0]))

    def pieces(c, act):
        i, begin, end = locate(c)
        e = jnp.where(i == 1, who[1], who[0])

        def visit(s, base):
            n = n_ref[s * EXPERTS + e]
            low = jnp.maximum(base, begin)
            size = jnp.minimum(base + n, end) - low
            skip = jnp.int32(0)
            for j in range(EXPERTS - 1):
                skip = skip + jnp.where(e > j, n_ref[s * EXPERTS + j], 0)

            @pl.when(size > 0)
            def _():
                act(s, skip + low - base, low - begin, size)

            return base + n

        lax.fori_loop(0, sources, visit, jnp.int32(0))

    def load(c, slot):
        def act(s, at, to, size):
            for k, (src, dst) in enumerate(((x_ref, xb), (g_ref, gb))):
                pltpu.make_async_copy(
                    src.at[s, pl.ds(at, size)], dst.at[slot, pl.ds(to, size)], sem_in.at[k, slot]
                ).start()

        pieces(c, act)

    def store(c, slot):
        def act(s, at, to, size):
            for k, (src, dst) in enumerate(((ob, o_ref), (db, dx_ref))):
                pltpu.make_async_copy(
                    src.at[slot, pl.ds(to, size)], dst.at[s, pl.ds(at, size)], sem_out.at[k, slot]
                ).start()

        pieces(c, act)

    def settle(c, slot, bufs, sems):
        _, begin, end = locate(c)
        for k, buf in enumerate(bufs):
            part = buf.at[slot, pl.ds(0, end - begin)]
            pltpu.make_async_copy(part, part, sems.at[k, slot]).wait()

    @pl.when(chunks > 0)
    def _():
        load(0, 0)

    def rest(s, act):
        t = n_ref[s * EXPERTS]
        for e in range(1, EXPERTS):
            t = t + n_ref[s * EXPERTS + e]

        @pl.when(groups - t > 0)
        def _():
            for k, dst in enumerate((o_ref, dx_ref)):
                act(
                    pltpu.make_async_copy(
                        blank.at[pl.ds(0, groups - t)], dst.at[s, pl.ds(t, groups - t)], sem_zero.at[k, s]
                    )
                )

    if fresh:
        blank[...] = jnp.zeros_like(blank)

        @pl.loop(0, sources)
        def _(s):
            rest(s, lambda copy: copy.start())

    def results(i):
        copies = [
            pltpu.make_async_copy(stage.at[k], far.at[i], sem_gw.at[k])
            for k, far in enumerate((gw1_far, gw2_far))
        ]
        if fresh and i == 0:
            half = pl.ds(pl.multiple_of((1 - y) * (width // 2), width // 2), width // 2)
            copies += [pltpu.make_async_copy(stage.at[k, half], cross_far.at[k], sem_cross.at[k]) for k in range(2)]
        return copies

    @pl.loop(0, chunks)
    def _(c):
        slot = c % 2
        i, begin, end = locate(c)

        @pl.when(c + 1 < chunks)
        def _():
            load(c + 1, 1 - slot)

        settle(c, slot, (xb, gb), sem_in)

        @pl.when(c >= 2)
        def _():
            settle(c - 2, slot, (ob, db), sem_out)

        for n in range(TURN):
            @pl.when((begin == 0) & (i == n))
            def _():
                for copy in copies[4 * n : 4 * n + 4]:
                    copy.wait()

        @pl.when(end - begin < CHUNK)
        def _():
            @pl.loop(end - begin, CHUNK)
            def _(r):
                xb[slot, r] = jnp.zeros_like(xb[slot, r])
                gb[slot, r] = jnp.zeros_like(gb[slot, r])

        def compute(groups_here):
            rows = groups_here * GROUP
            x = xb[slot, 0:groups_here].reshape(rows, width)
            g = gb[slot, 0:groups_here].reshape(rows, width)
            w1 = w_ref[i, 0].reshape(width, width)
            w2 = w_ref[i, 1].reshape(width, width)
            pre = mul(x, w1)
            square = pre * pre
            t = jnp.tanh(ROOT * pre * (1.0 + CUBIC * square))
            act = (0.5 * pre * (1.0 + t)).astype(jnp.bfloat16)
            slope = 0.5 * (1.0 + t) + 0.5 * pre * (1.0 - t * t) * (ROOT * (1.0 + 3.0 * CUBIC * square))
            grad_pre = (slope * mul(g, w2, NT)).astype(jnp.bfloat16)
            ob[slot, 0:groups_here] = mul(act, w2).astype(jnp.bfloat16).reshape(groups_here, GROUP, width)
            db[slot, 0:groups_here] = mul(grad_pre, w1, NT).astype(jnp.bfloat16).reshape(groups_here, GROUP, width)
            store(c, slot)
            add1 = mul(x.T, grad_pre)
            add2 = mul(act.T, g)

            @pl.when(begin == 0)
            def _():
                acc1[...] = add1
                acc2[...] = add2

            @pl.when(begin > 0)
            def _():
                acc1[...] += add1
                acc2[...] += add2

        pl.when(end - begin > CHUNK // 2)(functools.partial(compute, CHUNK))
        pl.when(end - begin <= CHUNK // 2)(functools.partial(compute, CHUNK // 2))

        for n in range(TURN):
            @pl.when((i == n) & (end == totals[n]))
            def _():
                if n:
                    @pl.when(totals[0] > 0)
                    def _():
                        for copy in results(0):
                            copy.wait()

                stage[0] = acc1[...].astype(stage.dtype)
                stage[1] = acc2[...].astype(stage.dtype)
                for copy in results(n):
                    copy.start()

    for n in range(TURN):
        wait_now = (totals[n] > 0) if n == TURN - 1 else (totals[n] > 0) & (totals[n + 1] == 0)

        @pl.when(wait_now)
        def _():
            for copy in results(n):
                copy.wait()

    for n in range(TURN):
        @pl.when(totals[n] == 0)
        def _():
            for copy in copies[4 * n : 4 * n + 4]:
                copy.wait()
            stage[...] = jnp.zeros_like(stage)
            for copy in results(n):
                copy.start()
            for copy in results(n):
                copy.wait()

    @pl.when(chunks >= 2)
    def _():
        settle(chunks - 2, chunks % 2, (ob, db), sem_out)

    @pl.when(chunks >= 1)
    def _():
        settle(chunks - 1, (chunks - 1) % 2, (ob, db), sem_out)

    if fresh:
        @pl.loop(0, sources)
        def _(s):
            rest(s, lambda copy: copy.wait())


def experts(n16, xs, gs, w, late=None, rows_out=None):
    sources, groups, _, width = xs.shape
    bf = jnp.bfloat16
    f32 = jnp.float32
    fresh = late is None
    far = pl.BlockSpec(memory_space=pl.ANY)
    smem = pl.BlockSpec(memory_space=pltpu.SMEM)
    out_rows = jax.ShapeDtypeStruct((sources, groups - 1, GROUP, width), bf)
    more = () if fresh else (late,) + rows_out
    dma = pltpu.SemaphoreType.DMA
    slots = CHUNK * GROUP * width
    typical = sources * (groups - 1) * GROUP * 5 // 16
    return pl.pallas_call(
        functools.partial(experts_kernel, fresh),
        out_shape=(
            out_rows, out_rows,
            jax.ShapeDtypeStruct((TURN, width, width), bf),
            jax.ShapeDtypeStruct((TURN, width, width), bf),
            jax.ShapeDtypeStruct((2, width // 2, width), bf),
        ),
        in_specs=[smem] + [far] * (3 + len(more)),
        out_specs=(far, far, far, far, far),
        scratch_shapes=[pltpu.VMEM((TURN, 2, 2, width // 2, width), bf)]
        + [pltpu.VMEM((2, CHUNK, GROUP, width), bf)] * 4
        + [pltpu.VMEM((width, width), f32)] * 2
        + [pltpu.VMEM((2, width, width), bf), pltpu.VMEM((groups - 1, GROUP, width), bf)]
        + [dma((2, 2)), dma((2, 2)), dma((2, sources)), dma((TURN, 4)), dma((2,)), dma((2,))],
        input_output_aliases={} if fresh else {5: 0, 6: 1},
        cost_estimate=pl.CostEstimate(
            flops=12 * typical * width * width, bytes_accessed=8 * typical * width, transcendentals=typical * width
        ),
        compiler_params=pltpu.CompilerParams(vmem_limit_bytes=56 * MIB),
        name="experts",
    )(n16, xs, gs, w, *more)


GROUPS = 4
UNIT = 384


def back_kernel(
    len_ref, norms_ref, counts_ref, x_far, g_far, hidden_far, qkv_far, mixed_far, aug_far, pos_far, wa_far,
    o_far, dx_far, gw1a_far, gw2a_far, gw1b_far, gw2b_far, y_first,
    out_far, gx_far, gwq_ref, gwo_ref, gn_out, cnt_out, gwin_ref, gwout_ref,
    y_land, up_land, down_land, o_near, o_beside,
    x_ref, g_ref, gx_ref, qkv_ref, mixed_ref, aug_ref, pos_ref, wa_ref,
    branch_ref, gmix_ref, first_t, mixed_t,
    qa_ref, ka_ref, va_ref, oa_ref, dv_ref, dk_ref, dq_ref,
    dx_own, dx_near, dx_beside, os_ref, in_ref, sum_ref, lane_out, lane_in, hid_ref, outb_ref,
    half_land, d_land, y_small, x_small, z_small, last_out, last_in,
    gn_ref, gn_send, gn_land, gn_t,
    load_sem, aug_sem, dxs_send, dxs_recv, dxx_send, dxx_recv,
    yw_send, yw_recv, up_send, up_recv, dn_send, dn_recv, on_send, on_recv, ob_send, ob_recv, in_sem,
    ln_send, ln_recv, h_send, h_recv, d_send, d_recv, sy_send, sy_recv, sx_send, sx_recv, sz_send, sz_recv,
    l_send, l_recv, gs_send, gs_recv, hid_sem, out_sem, gx_sem,
):
    slots, width = x_ref.shape
    heads = width // HEAD_DIM
    pairs = heads // 2
    rp = dx_own.shape[1]
    piece = rp // 256 * 64
    part = gw1a_far.shape[2]
    owned = gwq_ref.shape[0]
    depth = 4
    length = len_ref[0]
    scale = HEAD_DIM ** -0.5
    f32 = jnp.float32
    bf = jnp.bfloat16
    me = Place()
    z, y, x, c = me.z, me.y, me.x, me.c
    sibling, beside, across = me.at(c=1 - c), me.at(x=1 - x), me.at(y=1 - y)
    above, below = me.at(z=jnp.minimum(z + 1, depth - 1)), me.at(z=jnp.maximum(z - 1, 0))
    me.greet([sibling, beside, across, me.at(x=1 - x, c=1 - c)] + [me.at(z=z ^ k) for k in range(1, depth)])

    loads = {
        "dx": [pltpu.make_async_copy(dx_far.at[2 * xx + c], dx_own.at[xx], load_sem.at[xx]) for xx in range(2)],
    }
    plain = (
        ("x", x_far, x_ref), ("mixed", mixed_far, mixed_ref), ("hidden", hidden_far, gx_ref), ("g", g_far, g_ref),
        ("pos", pos_far, pos_ref), ("wa", wa_far, wa_ref), ("qkv", qkv_far, qkv_ref),
    )
    for i, (name, src, dst) in enumerate(plain):
        loads[name] = [pltpu.make_async_copy(src, dst, load_sem.at[2 + i])]

    def loaded(*names):
        for name in names:
            for copy in loads[name]:
                copy.wait()

    def dx_sib(xx):
        return push(dx_far.at[2 * xx + 1 - c], dx_near.at[xx], dxs_send.at[xx], dxs_recv.at[xx], sibling)

    def size_of(i):
        return rp - 3 * piece if i == 3 else piece

    def rows_of(i):
        return pl.ds(i * piece, size_of(i))

    def dx_over(i):
        return push(dx_own.at[1 - x, rows_of(i)], dx_beside.at[rows_of(i)], dxx_send.at[i], dxx_recv.at[i], beside)

    gws = ((gw1a_far, gw1b_far), (gw2a_far, gw2b_far))

    def product(k, i):
        return gws[k][i // 2].at[i % 2]

    def y_push(k, i):
        return push(product(k, i).at[1 - y], y_land.at[k, i], yw_send.at[k, i], yw_recv.at[k, i], across)

    def up_push(k, e, slot):
        return push(sum_ref.at[slot], up_land.at[k, e], up_send.at[k, e], up_recv.at[k, e], above)

    def down_push(k, e, slot):
        return push(sum_ref.at[slot], down_land.at[k, e], dn_send.at[k, e], dn_recv.at[k, e], below)

    def o_sib(xx):
        return push(o_far.at[2 * xx + 1 - c], o_near.at[xx], on_send.at[xx], on_recv.at[xx], sibling)

    def o_over():
        return push(os_ref, o_beside, ob_send.at[0], ob_recv.at[0], beside)

    lanes = [(1 - x, c), (x, 1 - c), (1 - x, 1 - c)]
    lane_rows = part // 4
    mine = 2 * x + c

    def lane_push(i, arrive):
        xx, cc = lanes[i]
        src = lane_out.at[pl.ds(pl.multiple_of(lane_rows * (2 * xx + cc), 16), lane_rows)]
        dst = lane_in.at[2 * xx + cc] if arrive else lane_in.at[mine]
        return push(src, dst, ln_send.at[i], ln_recv.at[i], me.at(x=xx, c=cc))

    weights = [(k, i) for i in range(depth) for k in (0, 1)]

    class WeightItem:
        def __init__(self, k, i):
            self.k, self.i, self.m = k, i, 3 - i
            self.rows = part

        def e(self):
            return (3 * (1 - z // 2), (3 * z + 2) % 5, 1 + z % 2, z)[self.i]

        def flags(self):
            e = self.e()
            if self.m == 0:
                return z > 0, z < depth - 1
            return (e > z) & (z > 0), (e < z) & (z < depth - 1)

        def ready(self):
            k, e = self.k, self.e()
            if self.i:
                y_push(k, self.i).wait_recv()
            for flag, copy in zip(self.flags(), (up_push, down_push)):
                @pl.when(flag)
                def _():
                    copy(k, e, 0).wait_recv()

        def sources(self):
            k, e = self.k, self.e()
            a, b = self.flags()
            return [
                (product(k, self.i).at[y], None), ((y_land.at[k, self.i] if self.i else y_first.at[k]), None),
                (up_land.at[k, e], a), (down_land.at[k, e], b)
            ]

        def finish(self, total, slot):
            k, e = self.k, self.e()
            if self.m:
                def put(rows, value):
                    sum_ref[slot, rows, :] = value.astype(bf)

                total(put)

                @pl.when(e > z)
                def _():
                    up_push(k, e, slot).start()

                @pl.when(e < z)
                def _():
                    down_push(k, e, slot).start()
            elif k == 1:
                def put(rows, value):
                    gwout_ref[rows, :] = value

                total(put)
            else:
                def put(rows, value):
                    lane_out[rows, :] = value.astype(bf)

                total(put)
                for i in range(3):
                    lane_push(i, False).start()
                lane_in[mine] = lane_out[pl.ds(pl.multiple_of(lane_rows * mine, 16), lane_rows), :]

        def sent(self, slot):
            k, e = self.k, self.e()
            if self.m:
                @pl.when(e > z)
                def _():
                    up_push(k, e, slot).wait_send()

                @pl.when(e < z)
                def _():
                    down_push(k, e, slot).wait_send()

    class OutItem:
        def __init__(self, stage, i):
            self.stage, self.i = stage, i
            self.rows = size_of(i)

        def ready(self):
            if self.i == 0:
                if self.stage == 0:
                    o_sib(1 - x).wait_recv()
                else:
                    o_sib(x).wait_recv()
                    o_over().wait()

        def sources(self):
            xx = 1 - x if self.stage == 0 else x
            rows = rows_of(self.i)
            found = [(o_far.at[2 * xx + c, rows], None), (o_near.at[xx, rows], None)]
            if self.stage:
                found.append((o_beside.at[rows], None))
            return found

        def finish(self, total, slot):
            base = self.i * piece

            def put(rows, value):
                os_ref[pl.ds(pl.multiple_of(base + rows.start, 64), rows.size), :] = value.astype(bf)

            total(put)

        def sent(self, slot):
            pass

    w_items = [WeightItem(k, i) for k, i in [(kk, ii) for ii in range(depth) for kk in (0, 1)]]
    o_items = [OutItem(s, i) for s in range(2) for i in range(4)]
    def w_pair(i):
        return w_items[2 * i : 2 * i + 2]

    def y_next(i):
        for k in range(2):
            y_push(k, i).start()

    def fetch(item, slot):
        for n, (src, flag) in enumerate(item.sources()):
            copy = pltpu.make_async_copy(src, in_ref.at[slot, n, pl.ds(0, item.rows)], in_sem.at[slot, n])
            if flag is None:
                copy.start()
            else:
                pl.when(flag)(copy.start)

    def finish(item, slot):
        sources = item.sources()
        for n, (src, flag) in enumerate(sources):
            copy = pltpu.make_async_copy(src, in_ref.at[slot, n, pl.ds(0, item.rows)], in_sem.at[slot, n])
            if flag is None:
                copy.wait()
            else:
                pl.when(flag)(copy.wait)
        place = 0
        if isinstance(item, WeightItem):
            place = item.k + 2 * (item.i % 2)
            if item.i == 2:
                w_items[item.k].sent(place)

        tile = 64

        def total(put):
            @pl.loop(0, item.rows // tile)
            def _(i):
                rows = pl.ds(pl.multiple_of(i * tile, tile), tile)
                value = None
                for n, (src, flag) in enumerate(sources):
                    term = in_ref[slot, n, rows, :].astype(f32)
                    if flag is not None:
                        term = jnp.where(flag, term, 0.0)
                    value = term if value is None else value + term
                put(rows, value)

        item.finish(total, place)

    def begin(items):
        for slot, item in enumerate(items):
            item.ready()
            fetch(item, slot)

    def close(items):
        for slot, item in enumerate(items):
            finish(item, slot)

    def group(items):
        begin(items)
        close(items)

    at_end = (z == 0) | (z == depth - 1)
    inside = (z > 0) & (z < depth - 1)

    def where(flag, act, items):
        pl.when(flag)(functools.partial(act, items))

    def home(g, side):
        store = dx_own if g < 2 else dx_near
        return store, side, pl.ds((g % 2) * UNIT, UNIT)

    def put_unit(g, u, value):
        store, side, _ = home(g, u // 3)
        lo = (g % 2) * UNIT + (u % 3) * 128
        store[side, 0:width, lo : lo + 128] = value.astype(bf)

    def block_rows(zz, yy, xx):
        return pl.ds(pl.multiple_of(2 * owned * (4 * zz + 2 * yy + xx), 16), 2 * owned)

    def block(g, zz, yy, xx):
        store, _, cols = home(g, 0)
        return store.at[c, block_rows(zz, yy, xx), cols]

    def half_push(g):
        store, _, cols = home(g, 0)
        return push(store.at[1 - c, pl.ds(0, width), cols], half_land.at[g], h_send.at[g], h_recv.at[g], sibling)

    def d_push(g, zz, peer):
        return push(block(g, zz, 1 - y, 1 - x), d_land.at[g, zz], d_send.at[g, zz], d_recv.at[g, zz], peer)

    def ys_push(g, zz):
        return push(block(g, zz, 1 - y, x), y_small.at[g, zz], sy_send.at[g, zz], sy_recv.at[g, zz], across)

    def xs_push(g, zz):
        return push(block(g, zz, y, 1 - x), x_small.at[g, zz], sx_send.at[g, zz], sx_recv.at[g, zz], beside)

    def zs_push(g, k, source):
        zz = z ^ k
        return push(block(g, zz, y, x), z_small.at[g, source], sz_send.at[g, k - 1], sz_recv.at[g, source], me.at(z=zz))

    def last_push(g):
        return push(last_out.at[g], last_in.at[g], l_send.at[g], l_recv.at[g], sibling)

    def small_a(g):
        half_push(g).wait_recv()
        store, _, cols = home(g, 0)

        @pl.loop(0, width // 64)
        def _(i):
            rows = pl.ds(pl.multiple_of(i * 64, 64), 64)
            store[c, rows, cols] = (store[c, rows, cols].astype(f32) + half_land[g, rows, :].astype(f32)).astype(bf)

        for zz in range(depth):
            d_push(g, zz, beside if zz % 2 == 0 else across).start()

    def small_b(g):
        store, _, cols = home(g, 0)
        for zz in range(depth):
            d_push(g, zz, beside).wait_recv()
            rows = block_rows(zz, 1 - y, x) if zz % 2 == 0 else block_rows(zz, y, 1 - x)
            store[c, rows, cols] = (store[c, rows, cols].astype(f32) + d_land[g, zz].astype(f32)).astype(bf)
            ys_push(g, zz).start()
            xs_push(g, zz).start()

    def small_c(g):
        store, _, cols = home(g, 0)
        for k in (3, 2, 1, 0):
            zz = z ^ k
            ys_push(g, zz).wait_recv()
            xs_push(g, zz).wait_recv()
            rows = block_rows(zz, y, x)
            value = store[c, rows, cols].astype(f32) + y_small[g, zz].astype(f32) + x_small[g, zz].astype(f32)
            store[c, rows, cols] = value.astype(bf)
            if k:
                zs_push(g, k, z).start()

    def columns(g, side):
        if g == 0:
            return [(gwo_ref, side * UNIT + 128 * i) for i in range(3)]
        found = []
        for i in range(3):
            u = 3 * side + i
            found.append((gwq_ref, (u // 2) * width + 256 * (g - 1) + (u % 2) * 128))
        return found

    def place_columns(g, side, value):
        for i, (ref, lo) in enumerate(columns(g, side)):
            ref[:, lo : lo + 128] = value[:, 128 * i : 128 * i + 128]

    def small_d(g):
        store, _, cols = home(g, 0)
        for k in range(1, depth):
            zs_push(g, k, z ^ k).wait_recv()
        value = store[c, block_rows(z, y, x), cols].astype(f32)
        for k in range(1, depth):
            value = value + z_small[g, z ^ k].astype(f32)
        own_part = jnp.where(c == 0, value[0:owned], value[owned:])
        last_out[g] = jnp.where(c == 0, value[owned:], value[0:owned])
        last_push(g).start()
        for side in range(2):
            @pl.when(c == side)
            def _():
                place_columns(g, side, own_part)

    def small_e(g):
        last_push(g).wait_recv()
        for side in range(2):
            @pl.when(c != side)
            def _():
                place_columns(g, side, last_in[g])

    def small_end(g):
        half_push(g).wait_send()
        for zz in range(depth):
            d_push(g, zz, beside).wait_send()
            ys_push(g, zz).wait_send()
            xs_push(g, zz).wait_send()
        for k in range(1, depth):
            zs_push(g, k, z).wait_send()
        last_push(g).wait_send()

    dx_sib(1 - x).start()
    dx_sib(x).start()
    for name in ("dx", "x", "mixed", "hidden", "g", "pos", "wa", "qkv"):
        for copy in loads[name]:
            copy.start()
    gn_ref[...] = jnp.zeros_like(gn_ref)
    in_ref[...] = jnp.zeros_like(in_ref)
    dx_sib(1 - x).wait_recv()
    loaded("dx")
    for i in range(4):
        rows = rows_of(i)
        dx_own[1 - x, rows, :] = (dx_own[1 - x, rows, :].astype(f32) + dx_near[1 - x, rows, :].astype(f32)).astype(bf)
        dx_over(i).start()
    y_next(1)
    o_sib(1 - x).start()
    o_sib(x).start()
    where(at_end, group, w_pair(0))

    loaded("x", "mixed")

    @pl.loop(0, slots // ROWS)
    def _(i):
        rows = pl.ds(i * ROWS, ROWS)
        normal, _ = layer_stats(x_ref[rows, :].astype(f32))
        branch_ref[rows, :] = (normal * norms_ref[0:1, :] + norms_ref[2:3, :]).astype(bf)

    first_t[...] = branch_ref[...].T
    mixed_t[...] = mixed_ref[...].T
    loaded("hidden", "g", "pos", "wa", "qkv")
    group(o_items[0:2])
    group(o_items[2:4])
    where(at_end, group, w_pair(1))
    where(inside, group, w_pair(0))
    y_next(2)
    dx_sib(x).wait_recv()
    for i in range(4):
        rows = rows_of(i)
        dx_over(i).wait_recv()
        dx_own[x, rows, :] = (
            dx_own[x, rows, :].astype(f32) + dx_near[x, rows, :].astype(f32) + dx_beside[rows, :].astype(f32)
        ).astype(bf)

    o_over().start()
    y_next(3)

    @pl.loop(0, slots // ROWS)
    def _(i):
        rows = pl.ds(i * ROWS, ROWS)
        place = pos_ref[rows, 0:1].astype(jnp.int32)
        pick = (iota((ROWS, rp), 1) == place).astype(bf)
        grad = mul(pick, dx_own[x])
        normal, scaled = layer_stats(gx_ref[rows, :])
        gn_ref[1:2, :] += jnp.sum(grad * normal, axis=0, keepdims=True)
        gn_ref[3:4, :] += jnp.sum(grad, axis=0, keepdims=True)
        grad_hidden = g_ref[rows, :].astype(f32) + norm_backward(grad, normal, scaled, norms_ref[1:2, :])
        gx_ref[rows, :] = grad_hidden
        branch = grad_hidden.astype(bf)
        branch_ref[rows, :] = branch
        gmix_ref[rows, :] = mul(branch, wa_ref[:, HALF + width : HALF + 2 * width], NT).astype(bf)

    for i in range(4):
        dx_over(i).wait_send()
    tile = width // 3

    @pl.loop(0, 3)
    def _(i):
        rows = pl.ds(i * tile, tile)
        value = mul(mixed_t[rows, :], branch_ref[...]).astype(bf)
        for side in range(2):
            dx_own[side, rows, 0:UNIT] = value[:, side * UNIT : (side + 1) * UNIT]

    half_push(0).start()

    def group_product(g):
        j = g - 1
        store_units = []
        for t in range(3):
            lo = t * width + 256 * j
            for i in range(3):
                rows = slice(i * tile, (i + 1) * tile)
                value = mul(first_t[rows, :], qkv_ref[:, lo : lo + 256]).astype(bf)
                for n in range(2):
                    u = 2 * t + n
                    store, side, _ = home(g, u // 3)
                    at = (g % 2) * UNIT + (u % 3) * 128
                    store[side, rows, at : at + 128] = value[:, n * 128 : (n + 1) * 128]
        half_push(g).start()

    plan = [
        [],
        [
            lambda: where(at_end, begin, w_pair(2)), lambda: where(inside, begin, w_pair(1)),
            lambda: small_a(0), lambda: group_product(1),
        ],
        [
            lambda: where(at_end, close, w_pair(2)), lambda: where(inside, close, w_pair(1)),
            lambda: where(inside, begin, w_pair(2)),
        ],
        [lambda: where(inside, close, w_pair(2)), lambda: small_a(1), lambda: group_product(2)],
        [],
        [lambda: small_a(2), lambda: group_product(3)],
    ]

    lane = iota((slots, 128), 1)
    key_bias = jnp.where(iota((slots, 128), 0) < length, 0.0, NEGATIVE).astype(bf)
    causal = iota((ROWS, ROWS), 0) <= iota((ROWS, ROWS), 1)

    def aug_load(p, slot):
        return pltpu.make_async_copy(aug_far.at[pl.ds(2 * p, 2)], aug_ref.at[slot], aug_sem.at[slot])

    aug_load(0, 0).start()

    @pl.loop(0, pairs)
    def _(p):
        slot = p % 2

        @pl.when(p + 1 < pairs)
        def _():
            aug_load(p + 1, 1 - slot).start()

        aug_load(p, slot).wait()
        cols = pl.ds(p * 128, 128)
        k_cols = pl.ds(width + p * 128, 128)
        v_cols = pl.ds(2 * width + p * 128, 128)
        q = qkv_ref[:, cols]
        q_hi = (q.astype(f32) * (scale * LOG2E)).astype(bf)
        k = qkv_ref[:, k_cols]
        v = qkv_ref[:, v_cols]
        do = gmix_ref[:, cols]
        prod = do.astype(f32) * mixed_ref[:, cols].astype(f32)
        k_t = k.T
        zero = jnp.zeros_like(q)
        one = jnp.ones_like(q)
        for half in range(2):
            own = own_lanes(lane, half)
            extra = extra_lane(half)
            parts = (lane > extra) & (lane <= extra + 3)
            qa_ref[half, :, 0:128] = jnp.where(own, q_hi, zero)
            qa_ref[half, :, 128:256] = aug_ref[slot, half]
            ka_ref[half, :, 0:128] = k
            ka_ref[half, :, 128:256] = jnp.where(
                own, k, jnp.where(lane == extra, key_bias, jnp.where(parts, one, zero))
            )
            va_ref[half, :, :] = jnp.where(own, v, jnp.where(parts, one, zero))
            minus = -jnp.sum(jnp.where(own, prod, 0.0), axis=1, keepdims=True)
            a, b, d = three_parts(jnp.broadcast_to(minus, (slots, 128)))
            oa_ref[half, :, :] = jnp.where(
                own, do,
                jnp.where(lane == extra + 1, a, jnp.where(lane == extra + 2, b, jnp.where(lane == extra + 3, d, zero))),
            )
        for half in range(2):
            k_own = k_t[half * HEAD_DIM : (half + 1) * HEAD_DIM, :]
            heads_rows = slice(half * HEAD_DIM, (half + 1) * HEAD_DIM)
            for j in range(slots // ROWS):
                keys = slice(j * ROWS, (j + 1) * ROWS)
                late = slice(j * ROWS, slots)
                s = mul(ka_ref[half, keys, :], qa_ref[half, late, :], NT)
                diag = jnp.where(causal, s[:, :ROWS], NEGATIVE)
                s = diag if j == slots // ROWS - 1 else jnp.concatenate([diag, s[:, ROWS:]], axis=1)
                probs = jnp.exp2(s)
                dp = mul(va_ref[half, keys, :], oa_ref[half, late, :], NT)
                ds = (probs * dp).astype(bf)
                probs = probs.astype(bf)
                dv_ref[half, keys, :] = mul(probs, gmix_ref[late, cols])
                dk_ref[half, keys, :] = mul(ds, qkv_ref[late, cols])
                dq = mul(k_own[:, keys], ds)
                if j == 0:
                    dq_ref[heads_rows, late] = dq
                else:
                    dq_ref[heads_rows, late] += dq
        first = lane < HEAD_DIM
        qkv_ref[:, cols] = (dq_ref[...].T * scale).astype(bf)
        qkv_ref[:, k_cols] = (jnp.where(first, dk_ref[0], dk_ref[1]) * scale).astype(bf)
        qkv_ref[:, v_cols] = jnp.where(first, dv_ref[0], dv_ref[1]).astype(bf)
        for i in range(pairs):
            @pl.when(p == i)
            def _():
                for step in plan[i]:
                    step()

    @pl.loop(0, slots // ROWS)
    def _(i):
        rows = pl.ds(i * ROWS, ROWS)
        normal, scaled = layer_stats(x_ref[rows, :].astype(f32))
        grad = mul(qkv_ref[rows, : 2 * width], wa_ref[:, : 2 * width], NT) + mul(
            qkv_ref[rows, 2 * width :], wa_ref[:, HALF : HALF + width], NT
        )
        gn_ref[0:1, :] += jnp.sum(grad * normal, axis=0, keepdims=True)
        gn_ref[2:3, :] += jnp.sum(grad, axis=0, keepdims=True)
        gx_ref[rows, :] += norm_backward(grad, normal, scaled, norms_ref[0:1, :])

    gx_out = pltpu.make_async_copy(gx_ref, gx_far, gx_sem)
    gx_out.start()
    counts = jnp.where(iota((8, 128), 0) == iota((8, 128), 1), counts_ref[...], 0).astype(f32)
    gn_ref[4:5, 0:128] = jnp.sum(counts, axis=0, keepdims=True)
    gn_peers = [sibling, beside, across, me.at(z=z ^ 1), me.at(z=z ^ 2)]

    def gn_push(i):
        return push(gn_send.at[i], gn_land.at[i], gs_send.at[i], gs_recv.at[i], gn_peers[i])

    def gn_start(i):
        gn_send[i] = gn_ref[...]
        gn_push(i).start()

    def gn_end(i):
        gn_push(i).wait_recv()
        gn_ref[...] += gn_land[i]

    gn_start(0)
    small_a(3)
    small_b(0)
    small_b(1)
    gn_end(0)
    gn_start(1)
    small_b(2)
    small_b(3)
    gn_end(1)
    gn_start(2)
    small_c(0)
    small_c(1)
    small_c(2)
    group(w_pair(3))
    gn_end(2)
    gn_start(3)
    small_c(3)
    group(o_items[4:6])
    gn_end(3)
    gn_start(4)
    group(o_items[6:8])
    small_d(0)
    small_d(1)
    small_d(2)
    small_d(3)
    small_e(0)
    small_e(1)

    def hidden_load(i):
        return pltpu.make_async_copy(hidden_far.at[pl.ds(i * ROWS, ROWS)], hid_ref.at[i % 2], hid_sem.at[i % 2])

    def out_store(i):
        return pltpu.make_async_copy(outb_ref.at[i % 2], out_far.at[pl.ds(i * ROWS, ROWS)], out_sem.at[i % 2])

    blocks = slots // ROWS
    hidden_load(0).start()
    for i in range(blocks):
        if i + 1 < blocks:
            hidden_load(i + 1).start()
        place = pos_ref[i * ROWS : (i + 1) * ROWS, 0:1].astype(jnp.int32)
        pick = (iota((ROWS, rp), 1) == place).astype(bf)
        value = mul(pick, os_ref[...])
        hidden_load(i).wait()
        if i >= 2:
            out_store(i - 2).wait()
        outb_ref[i % 2] = (hid_ref[i % 2] + value).astype(bf)
        out_store(i).start()

    small_e(2)
    gn_end(4)
    gn_t[...] = jnp.concatenate([gn_ref[...], jnp.zeros((120, width), f32)], axis=0).T
    gn_out[...] = gn_t[pl.ds(pl.multiple_of(owned * (8 * z + 4 * y + 2 * x + c), 8), owned), :]
    cnt_out[...] = gn_ref[:, 0:128]
    for i in range(3):
        lane_push(i, True).wait_recv()
    for s in range(4):
        for b in range(2):
            lo = (4 * b + s) * part
            gwin_ref[:, lo : lo + part] = lane_in[s, :, b * part : (b + 1) * part].astype(f32)
    small_e(3)

    for i in range(blocks - 2, blocks):
        out_store(i).wait()
    gx_out.wait()
    for item in w_items[2:6]:
        item.sent(item.k + 2 * (item.i % 2))
    for xx in range(2):
        dx_sib(xx).wait_send()
        o_sib(xx).wait_send()
    for item in w_items[2:]:
        y_push(item.k, item.i).wait_send()
    for i in range(3):
        lane_push(i, False).wait_send()
    for i in range(5):
        gn_push(i).wait_send()
    for g in range(GROUPS):
        small_end(g)


def back(length, norms, counts, x, g, hidden, qkv, mixed, aug, pos, wa, o_part, dx_part, gws, y_first, owned):
    slots, width = x.shape
    rp = dx_part.shape[1]
    part = gws[0].shape[2]
    bf = jnp.bfloat16
    f32 = jnp.float32
    whole = pl.BlockSpec(memory_space=pltpu.VMEM)
    far = pl.BlockSpec(memory_space=pl.ANY)
    dma = pltpu.SemaphoreType.DMA
    v = pltpu.VMEM
    out = jax.ShapeDtypeStruct
    return pl.pallas_call(
        back_kernel,
        out_shape=(
            out((slots, width), bf),
            out((slots, width), f32),
            out((owned, 3 * width), f32),
            out((owned, width), f32),
            out((owned, 128), f32),
            out((8, 128), f32),
            out((part // 4, 8 * part), f32),
            out((part, width), f32),
            out((2, EXPERTS, part, width), bf),
            out((2, EXPERTS, part, width), bf),
            out((2, EXPERTS, part, width), bf),
            out((2, rp, width), bf),
            out((rp, width), bf),
        ),
        in_specs=[pl.BlockSpec(memory_space=pltpu.SMEM), whole, whole] + [far] * 15,
        out_specs=(far, far, whole, whole, whole, whole, whole, whole, far, far, far, far, far),
        scratch_shapes=[
            v((slots, width), bf), v((slots, width), bf), v((slots, width), f32), v((slots, 3 * width), bf),
            v((slots, width), bf), v((2, 2, slots, 128), bf), v((slots, 128), f32), v((width, WIDE), bf),
            v((slots, width), bf), v((slots, width), bf), v((width, slots), bf), v((width, slots), bf),
            v((2, slots, 256), bf), v((2, slots, 256), bf), v((2, slots, 128), bf), v((2, slots, 128), bf),
            v((2, slots, 128), f32), v((2, slots, 128), f32), v((128, slots), f32),
            v((2, rp, width), bf), v((2, rp, width), bf), v((rp, width), bf), v((rp, width), bf),
            v((2, 4, part, width), bf), v((4, part, width), bf), v((part, width), bf), v((4, part // 4, width), bf),
            v((2, ROWS, width), f32), v((2, ROWS, width), bf),
            v((GROUPS, width, UNIT), bf),
            v((GROUPS, 4, 2 * owned, UNIT), bf), v((GROUPS, 4, 2 * owned, UNIT), bf),
            v((GROUPS, 4, 2 * owned, UNIT), bf), v((GROUPS, 4, 2 * owned, UNIT), bf),
            v((GROUPS, owned, UNIT), f32), v((GROUPS, owned, UNIT), f32),
            v((8, width), f32), v((5, 8, width), f32), v((5, 8, width), f32), v((width, 128), f32),
            dma((9,)), dma((2,)), dma((2,)), dma((2,)), dma((4,)), dma((4,)),
            dma((2, 4)), dma((2, 4)), dma((2, 4)), dma((2, 4)), dma((2, 4)), dma((2, 4)),
            dma((2,)), dma((2,)), dma((4,)), dma((4,)), dma((3, 4)),
            dma((3,)), dma((3,)), dma((4,)), dma((4,)), dma((4, 4)), dma((4, 4)), dma((4, 4)), dma((4, 4)),
            dma((4, 4)), dma((4, 4)), dma((4, 3)), dma((4, 4)),
            dma((4,)), dma((4,)), dma((5,)), dma((5,)), dma((2,)), dma((2,)), dma(()),
        ],
        compiler_params=pltpu.CompilerParams(vmem_limit_bytes=62 * MIB, collective_id=1, has_side_effects=True),
        name="back",
    )(length, norms, counts, x, g, hidden, qkv, mixed, aug, pos, wa, o_part, dx_part, *gws, y_first)


def plane_body(
    tokens, token_ids, lengths, hash_table, w_qkv, w_attn_out, norm_gains, norm_biases, w_in, w_out, cotangent
):
    slots, width = tokens.shape
    bf = jnp.bfloat16
    rp = padded_rows(slots)
    part = w_out.shape[0]
    owned = w_qkv.shape[0]

    table = jnp.pad(hash_table, (0, (-hash_table.shape[0]) % 8192)).reshape(64, 128)
    qkv, mixed, aug, hidden, xs, gs, w, wa, norms, pos, counts, late = front(
        lengths, tokens, token_ids.reshape(1, slots), table, cotangent,
        w_qkv, w_attn_out, norm_gains, norm_biases, w_in, w_out,
    )
    xs = xs.reshape(4, rp // GROUP + 1, GROUP, width)
    gs = gs.reshape(4, rp // GROUP + 1, GROUP, width)
    n16 = xs[:, rp // GROUP, :EXPERTS, 0].astype(jnp.int32).reshape(-1)
    over = [(i, i ^ 4) for i in range(lax.axis_size("fsdp"))]
    late = lax.ppermute(late, "fsdp", over)
    o_part, dx_part, gw1a, gw2a, cross = experts(n16, xs, gs, w)
    y_first = lax.ppermute(cross, "fsdp", over)
    o_part, dx_part, gw1b, gw2b, _ = experts(n16, xs, gs, w, late, (o_part, dx_part))
    halves = lambda v: v.reshape(TURN, 2, part, width)
    out, gx, gwq, gwo, gn, cnt, gwin, gwout = back(
        lengths, norms, counts, tokens, cotangent, hidden, qkv, mixed, aug, pos, wa,
        o_part.reshape(4, rp, width), dx_part.reshape(4, rp, width),
        (halves(gw1a), halves(gw2a), halves(gw1b), halves(gw2b)), y_first, owned,
    )[:8]
    return (out, gx, gwq, gwo, gn[:, 0:2], gn[:, 2:4], gwin, gwout, cnt[4, :EXPERTS].astype(jnp.int32))


def solution(mesh):
    placed = (
        P(("dp", "fsdp"), None),
        P(("dp", "fsdp")),
        P(("dp", "fsdp")),
        P(),
        P(("dp", "fsdp"), None),
        P(("dp", "fsdp"), None),
        P(("dp", "fsdp"), None),
        P(("dp", "fsdp"), None),
        P(("dp", "fsdp"), None),
        P(("dp", "fsdp"), None),
        P(("dp", "fsdp"), None),
    )
    by_plane = mesh.shape["dp"] == EXPERTS and mesh.shape["fsdp"] == 8
    return jax.shard_map(
        plane_body if by_plane else body,
        mesh=mesh,
        in_specs=placed,
        out_specs=(
            P(("dp", "fsdp"), None),
            P(("dp", "fsdp"), None),
            P(("dp", "fsdp"), None),
            P(("dp", "fsdp"), None),
            P(("dp", "fsdp"), None),
            P(("dp", "fsdp"), None),
            P(("dp", "fsdp"), None),
            P(("dp", "fsdp"), None),
            P(),
        ),
        check_vma=False,
    )
```
